32 devices in a mesh: dp: 8 (over y, x, core), head: 4 (over z).
Axes of the slice: x: 2, y: 2, z: 4, core: 2. Of those that a mesh axis runs over, the one named last changes fastest.
Arguments:
- tokens_in: bfloat16 [16384, 768], P(('dp', 'head')), may hold values from -6 to 6
- segment: int32 [16, 1024], P('dp'), may hold values from 0 to 7, never falling along the last dimension, each value on 1 to 384 neighbouring positions
- w_qkv: bfloat16 [2, 768, 3, 12, 64], P(None, None, None, 'head'), may hold values from -0.21875 to 0.21875
- qv_bias: bfloat16 [2, 2, 12, 64], P(None, None, 'head'), may hold values from -3 to 3
- w_out: bfloat16 [2, 768, 768], replicated, may hold values from -0.875 to 0.875
- out_bias: bfloat16 [2, 768], replicated, may hold values from -2 to 2
- ln1_gain: bfloat16 [2, 768], replicated, may hold values from 0.25 to 1.75
- ln1_bias: bfloat16 [2, 768], replicated, may hold values from -2 to 2
- w_up: bfloat16 [2, 768, 3072], replicated, may hold values from -0.21875 to 0.21875
- up_bias: bfloat16 [2, 3072], replicated, may hold values from -3 to 3
- w_down: bfloat16 [2, 3072, 768], replicated, may hold values from -0.109375 to 0.109375
- down_bias: bfloat16 [2, 768], replicated, may hold values from -2 to 2
- ln2_gain: bfloat16 [2, 768], replicated, may hold values from 0.25 to 1.75
- ln2_bias: bfloat16 [2, 768], replicated, may hold values from -2 to 2
- cotangent: bfloat16 [16384, 768], P(('dp', 'head')), may hold values from -6 to 6
Outputs:
- output: bfloat16 [16384, 768], P(('dp', 'head'))
- input_grad: float32 [16384, 768], P(('dp', 'head'))
- grad_qkv: float32 [2, 768, 3, 12, 64], P(None, 'dp', None, 'head')
- grad_qv_bias: float32 [2, 2, 12, 64], P(None, None, 'head', 'dp')
- grad_out_w: float32 [2, 768, 768], P(None, ('dp', 'head'))
- grad_out_bias: float32 [2, 768], P(None, ('dp', 'head'))
- grad_ln1_gain: float32 [2, 768], P(None, ('dp', 'head'))
- grad_ln1_bias: float32 [2, 768], P(None, ('dp', 'head'))
- grad_up: float32 [2, 768, 3072], P(None, ('dp', 'head'))
- grad_up_bias: float32 [2, 3072], P(None, ('dp', 'head'))
- grad_down: float32 [2, 3072, 768], P(None, ('dp', 'head'))
- grad_down_bias: float32 [2, 768], P(None, ('dp', 'head'))
- grad_ln2_gain: float32 [2, 768], P(None, ('dp', 'head'))
- grad_ln2_bias: float32 [2, 768], P(None, ('dp', 'head'))
The draws below stay inside these ranges and needn't reach their ends.
Inputs may be any that keep to these rules, and one draw needn't show every extreme that they name: Along each packed row segment numbers start at 0 and never fall; each of the 8 numbers holds 1 to 384 tokens of the row, some row has one of exactly 384.
All inputs are finite; a program needn't handle non-finite values.
Results may differ from the reference program's by a relative error of at most 0.028.
Values may be sent and summed in bfloat16 or wider, within the bound.
No kernel may reach another device: no remote copies, remote signals or barrier semaphores. Data moves between devices by JAX's collectives and lax.ppermute only.
A program may use at most 320 MiB of HBM per device.

```python
import math
import jax
import jax.numpy as jnp
import numpy as np
from jax import lax

D = 768
H = 12
DH = 64
FF = 3072
SEQ = 1024
LAYERS = 2
SEGMENTS = 8
ROWS_DEV = 2
SEG_MOST = 384
ROWS = 16
TOKENS = 16384


def spiked(drawn, key, source, target, blocks, factor):
    owner, partner = [(jnp.arange(drawn.shape[axis_at]) // (drawn.shape[axis_at] // blocks)).reshape([-1 if axis == axis_at else 1 for axis in range(drawn.ndim)]) for axis_at in (source, target)]
    chosen = jax.random.permutation(key, blocks)[partner]
    strong = (owner == chosen) | (owner == (partner + blocks // 2) % blocks)
    return jnp.where(strong, factor * drawn, drawn)


def levels(own_key, extent, split, low, largest):
    def one(axis_at, blocks):
        heights = jax.random.uniform(jax.random.fold_in(jax.random.fold_in(own_key, 6), axis_at), (blocks,), jnp.float32, low / len(split), largest / len(split))
        return jnp.repeat(jnp.exp(heights), extent[axis_at] // blocks).reshape((-1,) + (1,) * (len(extent) - axis_at - 1))

    level = one(*split[0])
    for cut in split[1:]:
        level = level * one(*cut)
    return level


def profile(count, total, most, skew):
    portions = [(1 << 20) // math.isqrt(standing ** skew) + 1 for standing in range(2, count + 1)]
    spare, counts = total - most - (count - 1), [1] * (count - 1)
    while spare > 0:
        free = [i for i in range(count - 1) if counts[i] < most]
        mass, remaining = sum([portions[i] for i in free]), spare
        for i in free:
            extra = min(most - counts[i], max(1, remaining * portions[i] // mass), spare)
            counts[i] = counts[i] + extra
            spare = spare - extra
    return np.array([most] + counts)


def ragged(own_key, amount, total, reach, skew):
    if amount == 2:
        one = jax.random.randint(own_key, (), max(1, total - reach), min(reach, total - 1) + 1)
        return jnp.stack([one, total - one])
    sizes = jnp.asarray(profile(amount, total, reach, skew), jnp.int32)
    twos = (amount - 1) // 2
    donor, taker = sizes[1:1 + 2 * twos:2], sizes[2:2 + 2 * twos:2]
    slack = jnp.minimum(donor - 1, reach - taker)
    moved = jax.random.randint(jax.random.fold_in(own_key, 1), (twos,), 0, 1 << 20) % (slack + 1)
    sizes = sizes.at[1:1 + 2 * twos:2].set(donor - moved).at[2:2 + 2 * twos:2].set(taker + moved)
    return sizes[jax.random.permutation(jax.random.fold_in(own_key, 2), amount)]


def centred(own_key, extent, scale, bound, pieces=(), held_as=jnp.bfloat16):
    level = levels(own_key, extent, pieces, -0.22, 0.18) if pieces else 1.0
    values = jax.random.normal(own_key, extent, jnp.float32) * scale * level
    return jnp.minimum(jnp.maximum(values, -bound), bound).astype(held_as)


def noise_with(stream_key, shape, deviation, reach, cuts, heavy, dtype=jnp.bfloat16):
    values = deviation * jax.random.normal(stream_key, shape, jnp.float32)
    if cuts:
        values = values * levels(stream_key, shape, cuts, -0.22, 0.18)
    return jnp.clip(spiked(values, jax.random.fold_in(stream_key, 3), *heavy), -reach, reach).astype(dtype)


def setup_inputs(seed: int = 0) -> dict:
    keys = jax.random.split(jax.random.key(seed), 16)
    tokens_in = centred(keys[0], (TOKENS, D), 1.0, 6.0, ((0, 32),))
    segment = jax.vmap(lambda own: jnp.searchsorted(jnp.cumsum(ragged(own, SEGMENTS, SEQ, SEG_MOST, 1)), jnp.arange(SEQ), side="right"))(jax.random.split(keys[1], ROWS)).reshape((ROWS, SEQ)).astype(jnp.int32)
    w_qkv = centred(keys[2], (LAYERS, D, 3, H, DH), D ** -0.5, 0.21875, ((3, 4),))
    qv_bias = centred(keys[3], (LAYERS, 2, H, DH), 0.5, 3.0, ((2, 4),))
    w_out = centred(keys[4], (LAYERS, D, D), (D // 16) ** -0.5, 0.875)
    out_bias = centred(keys[5], (LAYERS, D), 0.3, 2.0)
    ln1_gain = jnp.clip(1.0 + 0.15 * jax.random.normal(keys[6], (LAYERS, D), jnp.float32), 0.25, 1.75).astype(jnp.bfloat16)
    ln1_bias = centred(keys[7], (LAYERS, D), 0.3, 2.0)
    w_up = centred(keys[8], (LAYERS, D, FF), D ** -0.5, 0.21875)
    up_bias = centred(keys[9], (LAYERS, FF), 0.5, 3.0)
    w_down = centred(keys[10], (LAYERS, FF, D), FF ** -0.5, 0.109375)
    down_bias = centred(keys[11], (LAYERS, D), 0.3, 2.0)
    ln2_gain = jnp.clip(1.0 + 0.15 * jax.random.normal(keys[12], (LAYERS, D), jnp.float32), 0.25, 1.75).astype(jnp.bfloat16)
    ln2_bias = centred(keys[13], (LAYERS, D), 0.3, 2.0)
    cotangent = noise_with(keys[14], (TOKENS, D), 1.0, 6.0, ((0, 32),), (0, 1, 32, 2.75))
    return dict(tokens_in=tokens_in, segment=segment, w_qkv=w_qkv, qv_bias=qv_bias, w_out=w_out, out_bias=out_bias, ln1_gain=ln1_gain, ln1_bias=ln1_bias, w_up=w_up, up_bias=up_bias, w_down=w_down, down_bias=down_bias, ln2_gain=ln2_gain, ln2_bias=ln2_bias, cotangent=cotangent)


@jax.custom_vjp
def low(v):
    return lax.optimization_barrier(v.astype(jnp.bfloat16)).astype(jnp.float32)

@jax.custom_vjp
def low_back(v):
    return v

def low_keep(v):
    return (low(v), None)

def low_pass(kept, grad):
    return (grad,)

def back_keep(v):
    return (v, None)

def back_low(kept, grad):
    return (low(grad),)
low.defvjp(low_keep, low_pass)
low_back.defvjp(back_keep, back_low)
norm_eps = 1e-06
masked_score = -1000000000.0
highest = lax.Precision.HIGHEST

def product(left, right):
    return jnp.dot(left, right, precision=highest)

def norm_rows(rows, gain, shift):
    center = rows - lax.optimization_barrier(jnp.mean(rows, axis=-1, keepdims=True))
    spread = lax.optimization_barrier(jnp.mean(center * center, axis=-1, keepdims=True))
    return center * lax.rsqrt(spread + norm_eps) * gain + shift

def row_attention(item):
    queries, key_rows, value_rows, labels = item
    scores = low_back(jnp.einsum('qhd,khd->hqk', queries, key_rows, precision=highest))
    same = labels[:, None] == labels[None, :]
    scores = jnp.where(same[None], scores, masked_score)
    top = lax.optimization_barrier(jnp.max(scores, axis=-1, keepdims=True))
    expo = jnp.exp(scores - top)
    weights = low(expo / lax.optimization_barrier(jnp.sum(expo, axis=-1, keepdims=True)))
    return jnp.einsum('hqk,khd->qhd', weights, value_rows, precision=highest)

def by_heads(block):
    return block.reshape(ROWS_DEV, SEQ, H, DH)

def block_forward(tokens, labels, params):
    w_qkv, qv_bias, w_out, out_bias, ln1_gain, ln1_bias, w_up, up_bias, w_down, down_bias, ln2_gain, ln2_bias = params
    hidden = tokens
    for layer_idx in range(LAYERS):
        rounded = low(hidden)
        query_w = w_qkv[layer_idx, :, 0].reshape(D, D)
        key_w = w_qkv[layer_idx, :, 1].reshape(D, D)
        value_w = w_qkv[layer_idx, :, 2].reshape(D, D)
        queries = low(low_back((product(rounded, query_w) + qv_bias[layer_idx, 0].reshape(D)) * 0.125))
        key_rows = low(low_back(product(rounded, key_w)))
        value_rows = low(low_back(product(rounded, value_w) + qv_bias[layer_idx, 1].reshape(D)))
        context = lax.map(jax.checkpoint(row_attention), (by_heads(queries), by_heads(key_rows), by_heads(value_rows), labels))
        context = low(low_back(context.reshape(ROWS_DEV * SEQ, D)))
        attended = low_back(product(context, w_out[layer_idx]) + out_bias[layer_idx])
        first = norm_rows(hidden + attended, ln1_gain[layer_idx], ln1_bias[layer_idx])
        upward = low_back(product(low(first), w_up[layer_idx]) + up_bias[layer_idx])
        active = low(jax.nn.gelu(upward, approximate=False))
        downward = low_back(product(active, w_down[layer_idx]) + down_bias[layer_idx])
        hidden = norm_rows(first + downward, ln2_gain[layer_idx], ln2_bias[layer_idx])
    return hidden

def reference(tokens_in, segment, w_qkv, qv_bias, w_out, out_bias, ln1_gain, ln1_bias, w_up, up_bias, w_down, down_bias, ln2_gain, ln2_bias, cotangent):
    params = tuple((weight.astype(jnp.float32) for weight in (w_qkv, qv_bias, w_out, out_bias, ln1_gain, ln1_bias, w_up, up_bias, w_down, down_bias, ln2_gain, ln2_bias)))
    blocks = tokens_in.astype(jnp.float32).reshape(-1, ROWS_DEV * SEQ, D)
    labels = segment.reshape(-1, ROWS_DEV, SEQ)
    pulls = cotangent.astype(jnp.float32).reshape(-1, ROWS_DEV * SEQ, D)

    def step(carry, item):
        block_tokens, label_rows, grad_out = item
        result, pull = jax.vjp(lambda inputs, weights: block_forward(inputs, label_rows, weights), block_tokens, params)
        grad_tokens, grad_params = pull(grad_out)
        carry = jax.tree.map(lambda total, part_grad: total + part_grad, carry, grad_params)
        return (carry, (result.astype(jnp.bfloat16), grad_tokens))
    start = jax.tree.map(jnp.zeros_like, params)
    totals, (results, grads) = lax.scan(step, start, (blocks, labels, pulls))
    return (results.reshape(-1, D), grads.reshape(-1, D), totals[0], totals[1], totals[2], totals[3], totals[4], totals[5], totals[6], totals[7], totals[8], totals[9], totals[10], totals[11])
```

```python
import functools

import jax
import jax.numpy as jnp
from jax import lax
from jax.experimental import pallas as pl
from jax.experimental.pallas import tpu as pltpu
from jax.sharding import PartitionSpec as P

norm_eps = 1e-06
masked_score = -1000000000.0
f32 = jnp.float32
bf16 = jnp.bfloat16

BLK = 128
HALO = 384


def swap(value, axis, bit):
    size = lax.axis_size(axis)
    return lax.ppermute(value, axis, [(i, i ^ bit) for i in range(size)])


def bit_of(axis, place):
    return (lax.axis_index(axis) >> place) & 1


def pick(value, index, axis):
    return lax.dynamic_index_in_dim(value, index, axis, keepdims=False)


def add_low(*terms):
    total = terms[0].astype(f32)
    for term in terms[1:]:
        total = total + term.astype(f32)
    return total


def halve_dp(held, order, low):
    left = sorted(order, reverse=True)
    for place in order:
        axis = left.index(place)
        mine = bit_of("dp", place)
        got = swap(pick(held, 1 - mine, axis), "dp", 1 << place)
        held = add_low(pick(held, mine, axis), got)
        if low:
            held = held.astype(bf16)
        left.remove(place)
    return held


def finish_head(slot):
    size = lax.axis_size("head")
    me = lax.axis_index("head")
    got = [swap(slot(me ^ step), "head", step) for step in range(1, size)]
    return add_low(slot(me), *got)


def head_masks():
    lane = lax.broadcasted_iota(jnp.int32, (BLK, BLK), 1)
    return lane < BLK // 2


def stack_heads(pair, low):
    zero = jnp.zeros_like(pair)
    return jnp.concatenate([jnp.where(low, pair, zero), jnp.where(low, zero, pair)], axis=0)


def nt(left, right):
    return lax.dot_general(left, right, (((1,), (1,)), ((), ())), preferred_element_type=f32)


def nn(left, right):
    return lax.dot_general(left, right, (((1,), (0,)), ((), ())), preferred_element_type=f32)


def attend_kernel(pairs, own_blocks, halo_blocks, bounds, segq, segk, qkv, kvh, ctx, lse, vt, qs, top, total, acc):
    width = pairs * BLK
    low = head_masks()
    half = BLK // 2
    for j in range(own_blocks + halo_blocks):
        for p in range(pairs):
            if j < own_blocks:
                tile = qkv[j * BLK : (j + 1) * BLK, 2 * width + p * BLK : 2 * width + (p + 1) * BLK]
            else:
                at = j - own_blocks
                tile = kvh[at * BLK : (at + 1) * BLK, width + p * BLK : width + (p + 1) * BLK]
            vt[j, p * BLK : (p + 1) * BLK, :] = tile.T

    def q_block(i, carry):
        rows = pl.ds(pl.multiple_of(i * BLK, BLK), BLK)
        for p in range(pairs):
            qs[p] = stack_heads(qkv[rows, p * BLK : (p + 1) * BLK], low)
        top[...] = jnp.full(top.shape, -1e30, f32)
        total[...] = jnp.zeros(total.shape, f32)
        acc[...] = jnp.zeros(acc.shape, f32)
        labels = segq[i]

        def k_block(ref, first, base, j, carry):
            here = pl.ds(pl.multiple_of(j * BLK, BLK), BLK)
            there = pl.ds(pl.multiple_of((base + j) * BLK, BLK), BLK)
            same = segk[there, :] == labels
            for p in range(pairs):
                keys = ref[here, first + p * BLK : first + (p + 1) * BLK]
                scores = jnp.where(same, nt(keys, qs[p]), masked_score)
                old = top[p : p + 1, :]
                new = jnp.maximum(old, jnp.max(scores, axis=0, keepdims=True))
                expo = jnp.exp(scores - new)
                scale = jnp.exp(old - new)
                top[p : p + 1, :] = new
                total[p : p + 1, :] = total[p : p + 1, :] * scale + jnp.sum(expo, axis=0, keepdims=True)
                weights = expo.astype(bf16)
                for h in range(2):
                    values = vt[base + j, p * BLK + h * half : p * BLK + (h + 1) * half, :]
                    part = slice(h * half, (h + 1) * half)
                    cols = slice(h * BLK, (h + 1) * BLK)
                    acc[p, part, :] = acc[p, part, :] * scale[:, cols] + nn(values, weights[:, cols])
            return carry

        lax.fori_loop(bounds[i, 0], bounds[i, 1], functools.partial(k_block, qkv, width, 0), 0)
        lax.fori_loop(bounds[i, 2], bounds[i, 3], functools.partial(k_block, kvh, 0, own_blocks), 0)
        for p in range(pairs):
            inverse = 1.0 / total[p : p + 1, :]
            flat = jnp.concatenate(
                [acc[p, :half, :] * inverse[:, :BLK], acc[p, half:, :] * inverse[:, BLK:]], axis=0
            )
            ctx[rows, p * BLK : (p + 1) * BLK] = flat.T.astype(bf16)
        lse[i] = top[...] + jnp.log(total[...])
        return carry

    lax.fori_loop(0, own_blocks, q_block, 0)


def attend_back_kernel(
    pairs, own_blocks, halo_blocks,
    bounds, segq, segk, qkv, kvh, ctx, lse, dctx,
    dqkv, dkvh, sums,
    kt, qs, cs, delta, dqt, dk, dv,
):
    width = pairs * BLK
    low = head_masks()
    half = BLK // 2
    blocks = own_blocks + halo_blocks
    for j in range(blocks):
        for p in range(pairs):
            if j < own_blocks:
                tile = qkv[j * BLK : (j + 1) * BLK, width + p * BLK : width + (p + 1) * BLK]
            else:
                at = j - own_blocks
                tile = kvh[at * BLK : (at + 1) * BLK, p * BLK : (p + 1) * BLK]
            kt[j, p * BLK : (p + 1) * BLK, :] = tile.T
    dk[...] = jnp.zeros(dk.shape, f32)
    dv[...] = jnp.zeros(dv.shape, f32)
    sums[...] = jnp.zeros(sums.shape, f32)

    def q_block(i, carry):
        rows = pl.ds(pl.multiple_of(i * BLK, BLK), BLK)
        for p in range(pairs):
            cols = slice(p * BLK, (p + 1) * BLK)
            qs[p] = stack_heads(qkv[rows, cols], low)
            pull = dctx[rows, cols]
            cs[p] = stack_heads(pull, low)
            prod = (pull.astype(f32) * ctx[rows, cols].astype(f32)).T
            delta[p : p + 1, :] = jnp.concatenate(
                [jnp.sum(prod[:half], axis=0, keepdims=True), jnp.sum(prod[half:], axis=0, keepdims=True)], axis=1
            )
        dqt[...] = jnp.zeros(dqt.shape, f32)
        labels = segq[i]

        def k_block(ref, first, base, j, carry):
            here = pl.ds(pl.multiple_of(j * BLK, BLK), BLK)
            there = pl.ds(pl.multiple_of((base + j) * BLK, BLK), BLK)
            same = segk[there, :] == labels
            for p in range(pairs):
                cols = slice(p * BLK, (p + 1) * BLK)
                keys = ref[here, first + p * BLK : first + (p + 1) * BLK]
                values = ref[here, first + width + p * BLK : first + width + (p + 1) * BLK]
                scores = jnp.where(same, nt(keys, qs[p]), masked_score)
                probs = jnp.exp(scores - lse[i, p : p + 1, :])
                pulls = nt(values, cs[p])
                dscore = (probs * (pulls - delta[p : p + 1, :])).astype(bf16)
                dv[there, cols] += nn(probs.astype(bf16), cs[p])
                dk[there, cols] += nn(dscore, qs[p])
                for h in range(2):
                    part = slice(h * half, (h + 1) * half)
                    flip = kt[base + j, p * BLK + h * half : p * BLK + (h + 1) * half, :]
                    dqt[p, part, :] += nn(flip, dscore[:, h * BLK : (h + 1) * BLK])
            return carry

        lax.fori_loop(bounds[i, 0], bounds[i, 1], functools.partial(k_block, qkv, width, 0), 0)
        lax.fori_loop(bounds[i, 2], bounds[i, 3], functools.partial(k_block, kvh, 0, own_blocks), 0)
        for p in range(pairs):
            cols = slice(p * BLK, (p + 1) * BLK)
            grad = dqt[p].T.astype(bf16) * jnp.asarray(0.125, bf16)
            dqkv[rows, cols] = grad
            sums[0:1, cols] += jnp.sum(grad.astype(f32), axis=0, keepdims=True)
        return carry

    lax.fori_loop(0, own_blocks, q_block, 0)
    for j in range(blocks):
        rows = slice(j * BLK, (j + 1) * BLK)
        grad_k = dk[rows, :].astype(bf16)
        grad_v = dv[rows, :].astype(bf16)
        if j < own_blocks:
            dqkv[rows, width : 2 * width] = grad_k
            dqkv[rows, 2 * width :] = grad_v
        else:
            back = slice((j - own_blocks) * BLK, (j - own_blocks + 1) * BLK)
            dkvh[back, :width] = grad_k
            dkvh[back, width:] = grad_v
        sums[1:2, :] += jnp.sum(grad_v.astype(f32), axis=0, keepdims=True)


def vmem_specs(count):
    return [pl.BlockSpec(memory_space=pltpu.VMEM)] * count


def attend(bounds, segq, segk, qkv, kvh):
    tokens, width3 = qkv.shape
    width = width3 // 3
    pairs, own_blocks, halo_blocks = width // BLK, tokens // BLK, kvh.shape[0] // BLK
    blocks = own_blocks + halo_blocks
    return pl.pallas_call(
        functools.partial(attend_kernel, pairs, own_blocks, halo_blocks),
        out_shape=(
            jax.ShapeDtypeStruct((tokens, width), bf16),
            jax.ShapeDtypeStruct((own_blocks, 8, 2 * BLK), f32),
        ),
        in_specs=[pl.BlockSpec(memory_space=pltpu.SMEM)] + vmem_specs(4),
        out_specs=tuple(vmem_specs(2)),
        scratch_shapes=[
            pltpu.VMEM((blocks, width, BLK), bf16),
            pltpu.VMEM((pairs, 2 * BLK, BLK), bf16),
            pltpu.VMEM((8, 2 * BLK), f32),
            pltpu.VMEM((8, 2 * BLK), f32),
            pltpu.VMEM((pairs, BLK, BLK), f32),
        ],
        compiler_params=pltpu.CompilerParams(vmem_limit_bytes=32 * 2**20),
        cost_estimate=pl.CostEstimate(flops=2 * 10**9, bytes_accessed=6 * 10**6, transcendentals=10**6),
        name="attend",
    )(bounds, segq, segk, qkv, kvh)


def attend_back(bounds, segq, segk, qkv, kvh, ctx, lse, dctx):
    tokens, width3 = qkv.shape
    width = width3 // 3
    pairs, own_blocks, halo_blocks = width // BLK, tokens // BLK, kvh.shape[0] // BLK
    blocks = own_blocks + halo_blocks
    return pl.pallas_call(
        functools.partial(attend_back_kernel, pairs, own_blocks, halo_blocks),
        out_shape=(
            jax.ShapeDtypeStruct((tokens, width3), bf16),
            jax.ShapeDtypeStruct(kvh.shape, bf16),
            jax.ShapeDtypeStruct((8, width), f32),
        ),
        in_specs=[pl.BlockSpec(memory_space=pltpu.SMEM)] + vmem_specs(7),
        out_specs=tuple(vmem_specs(3)),
        scratch_shapes=[
            pltpu.VMEM((blocks, width, BLK), bf16),
            pltpu.VMEM((pairs, 2 * BLK, BLK), bf16),
            pltpu.VMEM((pairs, 2 * BLK, BLK), bf16),
            pltpu.VMEM((8, 2 * BLK), f32),
            pltpu.VMEM((pairs, BLK, BLK), f32),
            pltpu.VMEM((blocks * BLK, width), f32),
            pltpu.VMEM((blocks * BLK, width), f32),
        ],
        compiler_params=pltpu.CompilerParams(vmem_limit_bytes=40 * 2**20),
        cost_estimate=pl.CostEstimate(flops=6 * 10**9, bytes_accessed=12 * 10**6, transcendentals=10**6),
        name="attend_back",
    )(bounds, segq, segk, qkv, kvh, ctx, lse, dctx)


def erf_parts(values):
    density = jnp.exp(-0.5 * values * values) * 0.3989422804014327
    return 0.5 * (1.0 + lax.erf(values * 0.7071067811865476)), density


def normalized(rows):
    center = rows - jnp.mean(rows, axis=-1, keepdims=True)
    spread = jnp.mean(center * center, axis=-1, keepdims=True)
    scale = lax.rsqrt(spread + norm_eps)
    return center * scale, scale


def norm_back(grad, gain, unit, scale):
    lifted = grad * gain
    first = jnp.mean(lifted, axis=-1, keepdims=True)
    second = jnp.mean(lifted * unit, axis=-1, keepdims=True)
    return (
        scale * (lifted - first - unit * second),
        jnp.sum(grad * unit, axis=0),
        jnp.sum(grad, axis=0),
    )


def nt_low(left, right):
    return nt(left, right).astype(bf16)


def rows_by_core(block, bits):
    tokens, columns = block.shape
    return block.reshape(tokens, 1 << (bits - 1), 2, columns >> bits)


def grad_halves(left, right, bits):
    view = rows_by_core(left, bits)
    mine = bit_of("dp", 0)

    def part(index):
        chosen = pick(view, index, 2).reshape(left.shape[0], -1)
        return lax.dot_general(chosen, right, (((0,), (0,)), ((), ())), preferred_element_type=f32).astype(bf16)

    return part(1 - mine), part(mine)


def per_device(
    tokens_in,
    segment,
    w_qkv,
    qv_bias,
    w_out,
    out_bias,
    ln1_gain,
    ln1_bias,
    w_up,
    up_bias,
    w_down,
    down_bias,
    ln2_gain,
    ln2_bias,
    cotangent,
):
    layers, width = w_qkv.shape[0], w_qkv.shape[1]
    part = w_qkv.shape[3] * w_qkv.shape[4]
    head_size = w_qkv.shape[4]
    tokens = tokens_in.shape[0]
    seq = segment.shape[1]
    dp, head = lax.axis_size("dp"), lax.axis_size("head")
    bits = dp.bit_length() - 1
    shard = lax.axis_index("head")
    halves = seq // tokens
    row, half = shard // halves, shard % halves
    forward_order = list(range(1, bits))
    backward_order = forward_order[::-1]

    labels = pick(segment, row, 0)
    own_labels = lax.dynamic_slice_in_dim(labels, half * tokens, tokens)
    halo_start = jnp.where(half == 0, tokens, tokens - HALO)
    halo_labels = lax.dynamic_slice_in_dim(labels, halo_start, HALO)
    edge = jnp.where(half == 0, tokens - HALO, 0)
    blocks = tokens // BLK
    by_block = own_labels.reshape(blocks, BLK)
    least, most = by_block[:, :1], by_block[:, -1:]

    def count(flags):
        return jnp.sum(flags.astype(jnp.int32), axis=1)

    bounds = jnp.stack(
        [
            count(own_labels[None] < least) // BLK,
            (count(own_labels[None] <= most) + BLK - 1) // BLK,
            count(halo_labels[None] < least) // BLK,
            (count(halo_labels[None] <= most) + BLK - 1) // BLK,
        ],
        axis=1,
    )
    segq = jnp.concatenate([by_block, by_block], axis=1).reshape(blocks, 1, 2 * BLK)
    segk = jnp.concatenate([own_labels, halo_labels]).reshape(-1, 1)

    rows_w = 3 * part

    def gather_weights(layer_idx):
        mine = w_qkv[layer_idx].transpose(1, 2, 3, 0).reshape(rows_w, width)
        piece = pick(mine.reshape(dp, rows_w // dp, width), lax.axis_index("dp"), 0)
        got = jnp.stack([swap(piece, "head", step) for step in range(1, head)])
        grown = got[:, None]
        for place in forward_order + [0]:
            theirs = swap(grown, "dp", 1 << place)
            first = bit_of("dp", place) == 0
            grown = jnp.stack([jnp.where(first, grown, theirs), jnp.where(first, theirs, grown)], axis=1)
        left = forward_order + [0]
        shape = (head - 1,) + (2,) * bits + (rows_w // dp, width)
        grown = grown.reshape(shape)
        now = left[::-1]
        grown = grown.transpose([0] + [1 + now.index(place) for place in range(bits - 1, -1, -1)] + [bits + 1, bits + 2])
        grown = grown.reshape(head - 1, 3, part, width)
        whole = jnp.zeros((3, head, part, width), bf16)
        whole = lax.dynamic_update_slice(whole, mine.reshape(3, 1, part, width), (0, shard, 0, 0))
        for step in range(1, head):
            whole = lax.dynamic_update_slice(whole, grown[step - 1][:, None], (0, shard ^ step, 0, 0))
        return whole.reshape(3 * head * part, width)

    bias_all = lax.all_gather(qv_bias, "head", axis=2, tiled=True).reshape(layers, 2, -1).astype(f32)
    w_cats = [gather_weights(layer_idx) for layer_idx in range(layers)]

    hidden = tokens_in.astype(f32)
    saved = []
    for layer_idx in range(layers):
        w_cat = w_cats[layer_idx]
        low = hidden.astype(bf16)
        halo = swap(lax.dynamic_slice_in_dim(low, edge, HALO), "head", 1)
        zero = jnp.zeros((width,), f32)
        bias_q, bias_v = bias_all[layer_idx, 0], bias_all[layer_idx, 1]
        shift = jnp.concatenate([bias_q, zero, bias_v])
        factor = jnp.concatenate([zero + 0.125, zero + 1.0, zero + 1.0])
        qkv = ((nt(low, w_cat) + shift) * factor).astype(bf16)
        kvh = (nt(halo, w_cat[width:]) + shift[width:]).astype(bf16)
        ctx, lse = attend(bounds, segq, segk, qkv, kvh)
        first_rows = hidden + (nn(ctx, w_out[layer_idx]) + out_bias[layer_idx].astype(f32))
        unit_one, scale_one = normalized(first_rows)
        first = unit_one * ln1_gain[layer_idx].astype(f32) + ln1_bias[layer_idx].astype(f32)
        first_low = first.astype(bf16)
        upward = nn(first_low, w_up[layer_idx]) + up_bias[layer_idx].astype(f32)
        below, density = erf_parts(upward)
        active = (upward * below).astype(bf16)
        slope = below + upward * density
        second_rows = first + (nn(active, w_down[layer_idx]) + down_bias[layer_idx].astype(f32))
        unit_two, scale_two = normalized(second_rows)
        hidden = unit_two * ln2_gain[layer_idx].astype(f32) + ln2_bias[layer_idx].astype(f32)
        saved.append((low, halo, qkv, kvh, ctx, lse, unit_one, scale_one, first_low, active, slope, unit_two, scale_two))
    output = hidden.astype(bf16)

    grad_hidden = cotangent.astype(f32)
    sums_by_layer = []
    results = []
    for layer_idx in reversed(range(layers)):
        low, halo, qkv, kvh, ctx, lse, unit_one, scale_one, first_low, active, slope, unit_two, scale_two = saved[layer_idx]
        w_cat = w_cats[layer_idx]
        grad_two, gain_two, shift_two = norm_back(grad_hidden, ln2_gain[layer_idx].astype(f32), unit_two, scale_two)
        grad_two_low = grad_two.astype(bf16)
        down_bias_sum = jnp.sum(grad_two_low.astype(f32), axis=0)
        down_send, down_keep = grad_halves(active, grad_two_low, bits)
        grad_up_low = (nt(grad_two_low, w_down[layer_idx]) * slope).astype(bf16)
        up_bias_sum = jnp.sum(grad_up_low.astype(f32), axis=0)
        up_send, up_keep = grad_halves(first_low, grad_up_low, bits)
        grad_first = nt(grad_up_low, w_up[layer_idx]) + grad_two
        grad_one, gain_one, shift_one = norm_back(grad_first, ln1_gain[layer_idx].astype(f32), unit_one, scale_one)
        grad_att_low = grad_one.astype(bf16)
        out_bias_sum = jnp.sum(grad_att_low.astype(f32), axis=0)
        grad_ctx = nt_low(grad_att_low, w_out[layer_idx])
        out_send, out_keep = grad_halves(ctx, grad_att_low, bits)
        dqkv, dkvh, qv_sum = attend_back(bounds, segq, segk, qkv, kvh, ctx, lse, grad_ctx)
        part_halo = nn(dkvh, w_cat[width:]).astype(bf16)
        back = swap(part_halo, "head", 1)
        padded = lax.dynamic_update_slice(jnp.zeros((tokens, width), bf16), back, (edge, 0))
        grad_hidden = nn(dqkv, w_cat) + grad_one + padded.astype(f32)

        view, view_halo = rows_by_core(low, bits), rows_by_core(halo, bits)
        mine = bit_of("dp", 0)

        def qkv_part(index, view=view, view_halo=view_halo, dqkv=dqkv, dkvh=dkvh):
            chosen = pick(view, index, 2).reshape(tokens, -1)
            chosen_halo = pick(view_halo, index, 2).reshape(HALO, -1)

            def tn(left, right):
                return lax.dot_general(left, right, (((0,), (0,)), ((), ())), preferred_element_type=f32)

            both = jnp.concatenate([chosen, chosen_halo], axis=0)
            both_kv = jnp.concatenate([dqkv[:, width:], dkvh], axis=0)
            return tn(chosen, dqkv[:, :width]).astype(bf16), tn(both, both_kv).astype(bf16)

        send_q, send_kv = qkv_part(1 - mine)
        keep_q, keep_kv = qkv_part(mine)

        def reduced(send, keep, order):
            got = swap(send, "dp", 1)
            held = add_low(keep, got).astype(bf16)
            held = held.reshape((2,) * (bits - 1) + (held.shape[0] >> (bits - 1), held.shape[1]))
            return halve_dp(held, order, True)

        def by_rows(held):
            view = held.reshape(head, held.shape[0] // head, held.shape[1])
            return finish_head(lambda k: pick(view, k, 0))

        def by_heads(held, count):
            view = held.reshape(held.shape[0], count, head, part)
            return finish_head(lambda k: pick(view, k, 2))

        out_down = by_rows(reduced(down_send, down_keep, backward_order))
        out_up = by_rows(reduced(up_send, up_keep, forward_order))
        out_out = by_rows(reduced(out_send, out_keep, forward_order))
        out_q = by_heads(reduced(send_q, keep_q, forward_order), 1)
        out_kv = by_heads(reduced(send_kv, keep_kv, backward_order), 2)
        out_qkv = jnp.concatenate([out_q, out_kv], axis=1)
        results.append((out_qkv, out_out, out_up, out_down))

        vectors = jnp.stack([out_bias_sum, gain_one, shift_one, down_bias_sum, gain_two, shift_two])
        sums_by_layer.append((vectors, up_bias_sum, qv_sum[:2]))

    results, sums_by_layer = results[::-1], sums_by_layer[::-1]
    out_qkv, out_w_out, out_up, out_down = (jnp.stack([r[k] for r in results]) for k in range(4))
    out_qkv = out_qkv.reshape(layers, out_qkv.shape[1], 3, part // head_size, head_size)

    vectors = jnp.stack([s[0] for s in sums_by_layer])
    ups = jnp.stack([s[1] for s in sums_by_layer])
    qvs = jnp.stack([s[2] for s in sums_by_layer])
    devices = dp * head
    flat = jnp.concatenate(
        [
            vectors.reshape(layers, 6, devices, -1).transpose(2, 0, 1, 3).reshape(devices, -1),
            ups.reshape(layers, devices, -1).transpose(1, 0, 2).reshape(devices, -1),
            qvs.reshape(layers, 2, head, part // head_size, dp, head_size // dp)
            .transpose(4, 2, 0, 1, 3, 5)
            .reshape(devices, -1),
        ],
        axis=1,
    )
    held = flat.reshape((2,) * bits + (head, flat.shape[1]))
    held = halve_dp(held, list(range(bits)), False)
    flat = finish_head(lambda k: pick(held, k, 0))
    cut_one = layers * 6 * (width // devices)
    cut_two = cut_one + layers * (up_bias.shape[1] // devices)
    out_vectors = flat[:cut_one].reshape(layers, 6, -1)
    out_ups = flat[cut_one:cut_two].reshape(layers, -1)
    out_qv = flat[cut_two:].reshape(layers, 2, part // head_size, head_size // dp)
    return (
        output,
        grad_hidden,
        out_qkv,
        out_qv,
        out_w_out,
        out_vectors[:, 0],
        out_vectors[:, 1],
        out_vectors[:, 2],
        out_up,
        out_ups,
        out_down,
        out_vectors[:, 3],
        out_vectors[:, 4],
        out_vectors[:, 5],
    )


def solution(mesh):
    return jax.shard_map(
        per_device,
        mesh=mesh,
        in_specs=(
            P(("dp", "head"), None),
            P("dp", None),
            P(None, None, None, "head", None),
            P(None, None, "head", None),
            P(),
            P(),
            P(),
            P(),
            P(),
            P(),
            P(),
            P(),
            P(),
            P(),
            P(("dp", "head"), None),
        ),
        out_specs=(
            P(("dp", "head"), None),
            P(("dp", "head"), None),
            P(None, "dp", None, "head", None),
            P(None, None, "head", "dp"),
            P(None, ("dp", "head"), None),
            P(None, ("dp", "head")),
            P(None, ("dp", "head")),
            P(None, ("dp", "head")),
            P(None, ("dp", "head"), None),
            P(None, ("dp", "head")),
            P(None, ("dp", "head"), None),
            P(None, ("dp", "head")),
            P(None, ("dp", "head")),
            P(None, ("dp", "head")),
        ),
        check_vma=False,
    )
```

```python
import functools

import jax
import jax.numpy as jnp
from jax import lax
from jax.experimental import pallas as pl
from jax.experimental.pallas import tpu as pltpu
from jax.sharding import PartitionSpec as P

norm_eps = 1e-06
masked_score = -1000000000.0
f32 = jnp.float32
bf16 = jnp.bfloat16

BLK = 128
TILE = 8
SCALE = 1.0
HALO = 384


def cost(microseconds):
    return pl.CostEstimate(flops=int(microseconds * SCALE * 1.15e9), bytes_accessed=1000, transcendentals=0)


def swap(value, axis, bit):
    size = lax.axis_size(axis)
    return lax.ppermute(value, axis, [(i, i ^ bit) for i in range(size)])


def bit_of(axis, place):
    return (lax.axis_index(axis) >> place) & 1


def pick(value, index, axis):
    return lax.dynamic_index_in_dim(value, index, axis, keepdims=False)


def add_low(*terms):
    total = terms[0].astype(f32)
    for term in terms[1:]:
        total = total + term.astype(f32)
    return total


def finish_head(slot):
    size = lax.axis_size("head")
    me = lax.axis_index("head")
    got = [swap(slot(me ^ step), "head", step) for step in range(1, size)]
    return add_low(slot(me), *got)


def head_masks():
    lane = lax.broadcasted_iota(jnp.int32, (BLK, BLK), 1)
    return lane < BLK // 2


def stack_heads(pair, low):
    zero = jnp.zeros_like(pair)
    return jnp.concatenate([jnp.where(low, pair, zero), jnp.where(low, zero, pair)], axis=0)


def nt(left, right):
    return lax.dot_general(left, right, (((1,), (1,)), ((), ())), preferred_element_type=f32)


def nn(left, right):
    return lax.dot_general(left, right, (((1,), (0,)), ((), ())), preferred_element_type=f32)


def attend_kernel(pairs, own_blocks, halo_blocks, bounds, segq, segk, qkv, kvh, ctx, ctx_t, ctx_low, lse, vt, qs, top, total, acc):
    width = pairs * BLK
    low = head_masks()
    half = BLK // 2
    for j in range(own_blocks + halo_blocks):
        for p in range(pairs):
            if j < own_blocks:
                tile = qkv[j * BLK : (j + 1) * BLK, 2 * width + p * BLK : 2 * width + (p + 1) * BLK]
            else:
                at = j - own_blocks
                tile = kvh[at * BLK : (at + 1) * BLK, width + p * BLK : width + (p + 1) * BLK]
            vt[j, p * BLK : (p + 1) * BLK, :] = tile.T

    def q_block(i, carry):
        rows = pl.ds(pl.multiple_of(i * BLK, BLK), BLK)
        for p in range(pairs):
            qs[p] = stack_heads(qkv[rows, p * BLK : (p + 1) * BLK], low)
        top[...] = jnp.full(top.shape, -1e30, f32)
        total[...] = jnp.zeros(total.shape, f32)
        acc[...] = jnp.zeros(acc.shape, f32)
        labels = segq[i]

        def k_block(ref, first, base, j, carry):
            here = pl.ds(pl.multiple_of(j * BLK, BLK), BLK)
            there = pl.ds(pl.multiple_of((base + j) * BLK, BLK), BLK)
            same = segk[there, :] == labels
            for p in range(pairs):
                keys = ref[here, first + p * BLK : first + (p + 1) * BLK]
                scores = jnp.where(same, nt(keys, qs[p]), masked_score)
                old = top[p : p + 1, :]
                new = jnp.maximum(old, jnp.max(scores, axis=0, keepdims=True))
                expo = jnp.exp(scores - new)
                scale = jnp.exp(old - new)
                top[p : p + 1, :] = new
                total[p : p + 1, :] = total[p : p + 1, :] * scale + jnp.sum(expo, axis=0, keepdims=True)
                weights = expo.astype(bf16)
                for h in range(2):
                    values = vt[base + j, p * BLK + h * half : p * BLK + (h + 1) * half, :]
                    part = slice(h * half, (h + 1) * half)
                    cols = slice(h * BLK, (h + 1) * BLK)
                    acc[p, part, :] = acc[p, part, :] * scale[:, cols] + nn(values, weights[:, cols])
            return carry

        lax.fori_loop(bounds[i, 0], bounds[i, 1], functools.partial(k_block, qkv, width, 0), 0)
        lax.fori_loop(bounds[i, 2], bounds[i, 3], functools.partial(k_block, kvh, 0, own_blocks), 0)
        for p in range(pairs):
            inverse = 1.0 / total[p : p + 1, :]
            flat = jnp.concatenate(
                [acc[p, :half, :] * inverse[:, :BLK], acc[p, half:, :] * inverse[:, BLK:]], axis=0
            )
            rounded = flat.astype(bf16)
            ctx_t[p * BLK : (p + 1) * BLK, rows] = flat
            ctx_low[p * BLK : (p + 1) * BLK, rows] = rounded
            ctx[rows, p * BLK : (p + 1) * BLK] = rounded.T
        lse[i] = top[...] + jnp.log(total[...])
        return carry

    lax.fori_loop(0, own_blocks, q_block, 0)


def attend_back_kernel(
    pairs, own_blocks, halo_blocks,
    bounds, segq, segk, qkv, kvh, ctx_t, lse, dctx, norm_sums, up_sum,
    dqkv, dkvh, sums,
    kt, qs, cs, delta, dqt, dk, dv,
):
    width = pairs * BLK
    low = head_masks()
    half = BLK // 2
    blocks = own_blocks + halo_blocks
    for j in range(blocks):
        for p in range(pairs):
            if j < own_blocks:
                tile = qkv[j * BLK : (j + 1) * BLK, width + p * BLK : width + (p + 1) * BLK]
            else:
                at = j - own_blocks
                tile = kvh[at * BLK : (at + 1) * BLK, p * BLK : (p + 1) * BLK]
            kt[j, p * BLK : (p + 1) * BLK, :] = tile.T
    dk[...] = jnp.zeros(dk.shape, f32)
    dv[...] = jnp.zeros(dv.shape, f32)
    sums[...] = jnp.zeros(sums.shape, f32)
    sums[0:8, :] = norm_sums[...]
    for at in range(up_sum.shape[1] // width):
        sums[8 + at : 9 + at, :] = up_sum[:, at * width : (at + 1) * width]

    def q_block(i, carry):
        rows = pl.ds(pl.multiple_of(i * BLK, BLK), BLK)
        for p in range(pairs):
            cols = slice(p * BLK, (p + 1) * BLK)
            qs[p] = stack_heads(qkv[rows, cols], low)
            pull = dctx[rows, cols]
            cs[p] = stack_heads(pull, low)
            prod = pull.astype(f32).T * ctx_t[cols, rows]
            delta[p : p + 1, :] = jnp.concatenate(
                [jnp.sum(prod[:half], axis=0, keepdims=True), jnp.sum(prod[half:], axis=0, keepdims=True)], axis=1
            )
        dqt[...] = jnp.zeros(dqt.shape, f32)
        labels = segq[i]

        def k_block(ref, first, base, j, carry):
            here = pl.ds(pl.multiple_of(j * BLK, BLK), BLK)
            there = pl.ds(pl.multiple_of((base + j) * BLK, BLK), BLK)
            same = segk[there, :] == labels
            for p in range(pairs):
                cols = slice(p * BLK, (p + 1) * BLK)
                keys = ref[here, first + p * BLK : first + (p + 1) * BLK]
                values = ref[here, first + width + p * BLK : first + width + (p + 1) * BLK]
                scores = jnp.where(same, nt(keys, qs[p]), masked_score)
                probs = jnp.exp(scores - lse[i, p : p + 1, :])
                pulls = nt(values, cs[p])
                dscore = (probs * (pulls - delta[p : p + 1, :])).astype(bf16)
                dv[there, cols] += nn(probs.astype(bf16), cs[p])
                dk[there, cols] += nn(dscore, qs[p])
                for h in range(2):
                    part = slice(h * half, (h + 1) * half)
                    flip = kt[base + j, p * BLK + h * half : p * BLK + (h + 1) * half, :]
                    dqt[p, part, :] += nn(flip, dscore[:, h * BLK : (h + 1) * BLK])
            return carry

        lax.fori_loop(bounds[i, 0], bounds[i, 1], functools.partial(k_block, qkv, width, 0), 0)
        lax.fori_loop(bounds[i, 2], bounds[i, 3], functools.partial(k_block, kvh, 0, own_blocks), 0)
        for p in range(pairs):
            cols = slice(p * BLK, (p + 1) * BLK)
            grad = dqt[p].T.astype(bf16) * jnp.asarray(0.125, bf16)
            dqkv[rows, cols] = grad
            sums[6:7, cols] += jnp.sum(grad.astype(f32), axis=0, keepdims=True)
        return carry

    lax.fori_loop(0, own_blocks, q_block, 0)
    for j in range(blocks):
        rows = slice(j * BLK, (j + 1) * BLK)
        grad_k = dk[rows, :].astype(bf16)
        grad_v = dv[rows, :].astype(bf16)
        if j < own_blocks:
            dqkv[rows, width : 2 * width] = grad_k
            dqkv[rows, 2 * width :] = grad_v
        else:
            back = slice((j - own_blocks) * BLK, (j - own_blocks + 1) * BLK)
            dkvh[back, :width] = grad_k
            dkvh[back, width:] = grad_v
        sums[7:8, :] += jnp.sum(grad_v.astype(f32), axis=0, keepdims=True)


def vmem_specs(count):
    return [pl.BlockSpec(memory_space=pltpu.VMEM)] * count


def any_specs(count):
    return [pl.BlockSpec(memory_space=pl.ANY)] * count


def ordered_call(kernel, args, waits, passes, out_shape, in_specs, out_specs, **options):
    waits, passes = tuple(waits) + tuple(turn.last), tuple(passes)
    given, made = len(args), len(out_shape)
    skipped = len(waits) + len(passes)

    def body(*refs):
        outs = given + skipped
        refs[outs + made][...] = jnp.zeros((8, BLK), f32)
        kernel(*refs[:given], *refs[outs : outs + made], *refs[outs + made + 1 + len(passes) :])

    out = pl.pallas_call(
        body,
        out_shape=tuple(out_shape)
        + (jax.ShapeDtypeStruct((8, BLK), f32),)
        + tuple(jax.ShapeDtypeStruct(p.shape, p.dtype) for p in passes),
        in_specs=list(in_specs) + any_specs(skipped),
        out_specs=tuple(out_specs) + (pl.BlockSpec((8, BLK), lambda *step: (0, 0)),) + tuple(any_specs(len(passes))),
        input_output_aliases={given + len(waits) + k: made + 1 + k for k in range(len(passes))},
        **options,
    )(*args, *waits, *passes)
    turn.last = [out[made]]
    return out[:made], out[made + 1 :]


class Turn:
    last = []


turn = Turn()


def attend(bounds, segq, segk, qkv, kvh, waits, passes):
    tokens, width3 = qkv.shape
    width = width3 // 3
    pairs, own_blocks, halo_blocks = width // BLK, tokens // BLK, kvh.shape[0] // BLK
    blocks = own_blocks + halo_blocks
    return ordered_call(
        functools.partial(attend_kernel, pairs, own_blocks, halo_blocks),
        (bounds, segq, segk, qkv, kvh),
        waits,
        passes,
        out_shape=(
            jax.ShapeDtypeStruct((tokens, width), bf16),
            jax.ShapeDtypeStruct((width, tokens), f32),
            jax.ShapeDtypeStruct((width, tokens), bf16),
            jax.ShapeDtypeStruct((own_blocks, 8, 2 * BLK), f32),
        ),
        in_specs=[pl.BlockSpec(memory_space=pltpu.SMEM)] + vmem_specs(4),
        out_specs=tuple(vmem_specs(4)),
        scratch_shapes=[
            pltpu.VMEM((blocks, width, BLK), bf16),
            pltpu.VMEM((pairs, 2 * BLK, BLK), bf16),
            pltpu.VMEM((8, 2 * BLK), f32),
            pltpu.VMEM((8, 2 * BLK), f32),
            pltpu.VMEM((pairs, BLK, BLK), f32),
        ],
        compiler_params=pltpu.CompilerParams(vmem_limit_bytes=32 * 2**20),
        cost_estimate=cost(9),
        name="attend",
    )


def attend_back(bounds, segq, segk, qkv, kvh, ctx_t, lse, dctx, norm_sums, up_sum, waits, passes):
    tokens, width3 = qkv.shape
    width = width3 // 3
    pairs, own_blocks, halo_blocks = width // BLK, tokens // BLK, kvh.shape[0] // BLK
    blocks = own_blocks + halo_blocks
    return ordered_call(
        functools.partial(attend_back_kernel, pairs, own_blocks, halo_blocks),
        (bounds, segq, segk, qkv, kvh, ctx_t, lse, dctx, norm_sums, up_sum),
        waits,
        passes,
        out_shape=(
            jax.ShapeDtypeStruct((tokens, width3), bf16),
            jax.ShapeDtypeStruct(kvh.shape, bf16),
            jax.ShapeDtypeStruct((16, width), f32),
        ),
        in_specs=[pl.BlockSpec(memory_space=pltpu.SMEM)] + vmem_specs(9),
        out_specs=tuple(vmem_specs(3)),
        scratch_shapes=[
            pltpu.VMEM((blocks, width, BLK), bf16),
            pltpu.VMEM((pairs, 2 * BLK, BLK), bf16),
            pltpu.VMEM((pairs, 2 * BLK, BLK), bf16),
            pltpu.VMEM((8, 2 * BLK), f32),
            pltpu.VMEM((pairs, BLK, BLK), f32),
            pltpu.VMEM((blocks * BLK, width), f32),
            pltpu.VMEM((blocks * BLK, width), f32),
        ],
        compiler_params=pltpu.CompilerParams(vmem_limit_bytes=40 * 2**20),
        cost_estimate=cost(21),
        name="attend_back",
    )


CHUNK = 512


def normalized(rows):
    center = rows - jnp.mean(rows, axis=-1, keepdims=True)
    spread = jnp.mean(center * center, axis=-1, keepdims=True)
    scale = lax.rsqrt(spread + norm_eps)
    return center * scale, scale


def feed_kernel(last, tokens, hidden, ctx, w_out, vec, w_up, up_bias, w_down, *rest):
    if last:
        first_rows, first_t, active_t, slope, second_rows, low, low_rows, first, total = rest
    else:
        first_rows, first_t, active_t, slope, second_rows, low, after, low_t, low_rows, first, total = rest
    step = pl.program_id(0)
    tiles = [slice(at, at + BLK) for at in range(0, tokens, BLK)]

    @pl.when(step == 0)
    def _():
        for rows in tiles:
            resid = hidden[rows, :].astype(f32) + (nn(ctx[rows, :], w_out[...]) + vec[0:1, :])
            first_rows[rows, :] = resid
            unit, _ = normalized(resid)
            value = unit * vec[1:2, :] + vec[2:3, :]
            first[rows, :] = value
            total[rows, :] = jnp.zeros_like(value)
            rounded = value.astype(bf16)
            low_rows[rows, :] = rounded
            first_t[:, rows] = rounded.T

    for rows in tiles:
        upward = nn(low_rows[rows, :], w_up[...]) + up_bias[...]
        density = jnp.exp(-0.5 * upward * upward) * 0.3989422804014327
        below = 0.5 + 0.5 * lax.erf(upward * 0.7071067811865476)
        active = (upward * below).astype(bf16)
        slope[rows, :] = below + upward * density
        active_t[:, rows] = active.T
        total[rows, :] += nn(active, w_down[...])

    @pl.when(step == pl.num_programs(0) - 1)
    def _():
        for rows in tiles:
            resid = first[rows, :] + (total[rows, :] + vec[3:4, :])
            second_rows[rows, :] = resid
            unit, _ = normalized(resid)
            value = unit * vec[4:5, :] + vec[5:6, :]
            rounded = value.astype(bf16)
            low[rows, :] = rounded
            if not last:
                after[rows, :] = value
                low_t[:, rows] = rounded.T


def whole(shape):
    return pl.BlockSpec(shape, lambda step: (0,) * len(shape))


def feed(last, layer_idx, hidden, ctx, w_out, vec, w_up, up_bias, w_down, waits, passes):
    tokens, width = hidden.shape
    wide = w_up.shape[-1]
    rows = whole((tokens, width))
    shapes = [
        jax.ShapeDtypeStruct((tokens, width), f32),
        jax.ShapeDtypeStruct((width, tokens), bf16),
        jax.ShapeDtypeStruct((wide, tokens), bf16),
        jax.ShapeDtypeStruct((tokens, wide), f32),
        jax.ShapeDtypeStruct((tokens, width), f32),
        jax.ShapeDtypeStruct((tokens, width), bf16),
    ]
    specs = [
        rows,
        whole((width, tokens)),
        pl.BlockSpec((CHUNK, tokens), lambda step: (step, 0)),
        pl.BlockSpec((tokens, CHUNK), lambda step: (0, step)),
        rows,
        rows,
    ]
    if not last:
        shapes.append(jax.ShapeDtypeStruct((tokens, width), f32))
        shapes.append(jax.ShapeDtypeStruct((width, tokens), bf16))
        specs.append(rows)
        specs.append(whole((width, tokens)))
    return ordered_call(
        functools.partial(feed_kernel, last, tokens),
        (hidden, ctx, w_out, vec, w_up, up_bias, w_down),
        waits,
        passes,
        grid=(wide // CHUNK,),
        out_shape=tuple(shapes),
        in_specs=[
            rows,
            rows,
            pl.BlockSpec((None, width, width), lambda step: (layer_idx, 0, 0)),
            whole(vec.shape),
            pl.BlockSpec((None, width, CHUNK), lambda step: (layer_idx, 0, step)),
            pl.BlockSpec((1, CHUNK), lambda step: (0, step)),
            pl.BlockSpec((None, CHUNK, width), lambda step: (layer_idx, step, 0)),
        ],
        out_specs=tuple(specs),
        scratch_shapes=[
            pltpu.VMEM((tokens, width), bf16),
            pltpu.VMEM((tokens, width), f32),
            pltpu.VMEM((tokens, width), f32),
        ],
        compiler_params=pltpu.CompilerParams(vmem_limit_bytes=48 * 2**20),
        cost_estimate=cost(17),
        name="feed",
    )


def norm_back(grad, gain, rows):
    unit, scale = normalized(rows)
    lifted = grad * gain
    first = jnp.mean(lifted, axis=-1, keepdims=True)
    second = jnp.mean(lifted * unit, axis=-1, keepdims=True)
    return scale * (lifted - first - unit * second), unit


def over_rows(value):
    return jnp.sum(value, axis=0, keepdims=True)


def feed_back_kernel(
    tokens, grad, second_rows, first_rows, slope, w_down, w_up, w_out, vec,
    dz, du, da, dr, dc, sums, up_sum, dr_two, total,
):
    step = pl.program_id(0)
    tiles = [slice(at, at + BLK) for at in range(0, tokens, BLK)]

    @pl.when(step == 0)
    def _():
        sums[...] = jnp.zeros(sums.shape, f32)
        for rows in tiles:
            pull = grad[rows, :].astype(f32)
            value, unit = norm_back(pull, vec[4:5, :], second_rows[rows, :])
            dr_two[rows, :] = value
            total[rows, :] = jnp.zeros_like(value)
            rounded = value.astype(bf16)
            dz[rows, :] = rounded
            sums[3:4, :] += over_rows(rounded.astype(f32))
            sums[4:5, :] += over_rows(pull * unit)
            sums[5:6, :] += over_rows(pull)

    up_sum[...] = jnp.zeros(up_sum.shape, f32)
    for rows in tiles:
        pull = (nt(dz[rows, :], w_down[...]) * slope[rows, :]).astype(bf16)
        du[rows, :] = pull
        up_sum[...] += over_rows(pull.astype(f32))
        total[rows, :] += nt(pull, w_up[...])

    @pl.when(step == pl.num_programs(0) - 1)
    def _():
        for rows in tiles:
            pull = total[rows, :] + dr_two[rows, :]
            value, unit = norm_back(pull, vec[1:2, :], first_rows[rows, :])
            dr[rows, :] = value
            rounded = value.astype(bf16)
            da[rows, :] = rounded
            sums[0:1, :] += over_rows(rounded.astype(f32))
            sums[1:2, :] += over_rows(pull * unit)
            sums[2:3, :] += over_rows(pull)
            dc[rows, :] = nt(rounded, w_out[...]).astype(bf16)


def feed_back(layer_idx, grad, second_rows, first_rows, slope, w_down, w_up, w_out, vec, waits, passes):
    tokens, width = grad.shape
    wide = w_up.shape[-1]
    rows = whole((tokens, width))
    return ordered_call(
        functools.partial(feed_back_kernel, tokens),
        (grad, second_rows, first_rows, slope, w_down, w_up, w_out, vec),
        waits,
        passes,
        grid=(wide // CHUNK,),
        out_shape=(
            jax.ShapeDtypeStruct((tokens, width), bf16),
            jax.ShapeDtypeStruct((tokens, wide), bf16),
            jax.ShapeDtypeStruct((tokens, width), bf16),
            jax.ShapeDtypeStruct((tokens, width), f32),
            jax.ShapeDtypeStruct((tokens, width), bf16),
            jax.ShapeDtypeStruct((8, width), f32),
            jax.ShapeDtypeStruct((1, wide), f32),
        ),
        in_specs=[
            rows,
            rows,
            rows,
            pl.BlockSpec((tokens, CHUNK), lambda step: (0, step)),
            pl.BlockSpec((None, CHUNK, width), lambda step: (layer_idx, step, 0)),
            pl.BlockSpec((None, width, CHUNK), lambda step: (layer_idx, 0, step)),
            pl.BlockSpec((None, width, width), lambda step: (layer_idx, 0, 0)),
            whole(vec.shape),
        ],
        out_specs=(
            rows,
            pl.BlockSpec((tokens, CHUNK), lambda step: (0, step)),
            rows,
            rows,
            rows,
            whole((8, width)),
            pl.BlockSpec((1, CHUNK), lambda step: (0, step)),
        ),
        scratch_shapes=[pltpu.VMEM((tokens, width), f32), pltpu.VMEM((tokens, width), f32)],
        compiler_params=pltpu.CompilerParams(vmem_limit_bytes=48 * 2**20),
        cost_estimate=cost(21),
        name="feed_back",
    )


def grad_feed_kernel(core, active_t, dz, first_t, du, send, keep, lhs):
    groups, head, _, parts, thin, width = send.shape
    rows = head * thin
    mine = core[0]
    for which, out in ((1 - mine, send), (mine, keep)):
        for group in range(groups):
            value = nn(active_t[2 * group + which], dz[...])
            for shard in range(head):
                for at in range(parts):
                    here = (shard * parts + at) * thin
                    out[group, shard, 0, at] = value[here : here + thin].astype(bf16)
        if rows % 16 == 0:
            for group in range(groups):
                lhs[group * rows : (group + 1) * rows, :] = first_t[2 * group + which]
        for at in range(parts):
            pulls = du[:, at * width : (at + 1) * width]
            if rows % 16 == 0:
                value = nn(lhs[...], pulls)
                values = [value[group * rows : (group + 1) * rows] for group in range(groups)]
            else:
                values = [nn(first_t[2 * group + which], pulls) for group in range(groups)]
            for group in range(groups):
                for shard in range(head):
                    out[group, shard, 1, at] = values[group][shard * thin : (shard + 1) * thin].astype(bf16)


def grad_feed(core, active_t, dz, first_t, du, devices, head, waits, passes):
    tokens, width = dz.shape
    wide = du.shape[1]
    parts, rows = wide // width, width // devices
    out = jax.ShapeDtypeStruct((devices // 2, head, 2, parts, rows // head, width), bf16)
    return ordered_call(
        grad_feed_kernel,
        (core, active_t.reshape(devices, wide // devices, tokens), dz, first_t.reshape(devices, rows, tokens), du),
        waits,
        passes,
        out_shape=(out, out),
        in_specs=[pl.BlockSpec(memory_space=pltpu.SMEM)] + vmem_specs(4),
        out_specs=tuple(vmem_specs(2)),
        scratch_shapes=[pltpu.VMEM((width // 2, tokens), bf16)],
        compiler_params=pltpu.CompilerParams(vmem_limit_bytes=48 * 2**20),
        cost_estimate=cost(10),
        name="grad_feed",
    )


def grad_heads_kernel(core, ctx_t, low_t, halo_t, da, dqkv, dkvh, sums, send, keep, one, two, three):
    groups, thin = ctx_t.shape[0] // 2, ctx_t.shape[1]
    width = send.shape[2] // 4
    high = thin // TILE
    for r in range(sums.shape[0] // TILE):
        value = sums[r * TILE : (r + 1) * TILE, :].astype(bf16)
        for out in (send, keep):
            out[groups * high, :, r * width : (r + 1) * width] = value
    mine = core[0]
    for which, out in ((1 - mine, send), (mine, keep)):
        if thin % 16 == 0:
            for group in range(groups):
                here = slice(group * thin, (group + 1) * thin)
                one[here, :] = ctx_t[2 * group + which]
                two[here, :] = low_t[2 * group + which]
                three[here, :] = halo_t[2 * group + which]
            parts = [(range(groups), one, two, three)]
        else:
            parts = [
                ([group], ctx_t.at[2 * group + which], low_t.at[2 * group + which], halo_t.at[2 * group + which])
                for group in range(groups)
            ]
        for members, left_one, left_two, left_three in parts:
            for at in range(0, 4 * width, width):
                if at < width:
                    value = nn(left_one[...], da[...])
                else:
                    value = nn(left_two[...], dqkv[:, at - width : at])
                    if at >= 2 * width:
                        value = value + nn(left_three[...], dkvh[:, at - 2 * width : at - width])
                for place, group in enumerate(members):
                    here = value[place * thin : (place + 1) * thin].reshape(high, TILE, width)
                    out[group * high : (group + 1) * high, :, at : at + width] = here.astype(bf16)


def grad_heads(core, ctx_t, low_t, halo_t, da, dqkv, dkvh, sums, devices, waits, passes):
    tokens, width = da.shape
    thin = width // devices
    out = jax.ShapeDtypeStruct((devices // 2 * thin // TILE + 1, TILE, 4 * width), bf16)
    extent = halo_t.shape[1]
    return ordered_call(
        grad_heads_kernel,
        (
            core,
            ctx_t.reshape(devices, thin, tokens),
            low_t.reshape(devices, thin, tokens),
            halo_t.reshape(devices, thin, extent),
            da,
            dqkv,
            dkvh,
            sums,
        ),
        waits,
        passes,
        out_shape=(out, out),
        in_specs=[pl.BlockSpec(memory_space=pltpu.SMEM)] + vmem_specs(7),
        out_specs=tuple(vmem_specs(2)),
        scratch_shapes=[
            pltpu.VMEM((width // 2, tokens), bf16),
            pltpu.VMEM((width // 2, tokens), bf16),
            pltpu.VMEM((width // 2, extent), bf16),
        ],
        compiler_params=pltpu.CompilerParams(vmem_limit_bytes=48 * 2**20),
        cost_estimate=cost(8),
        name="grad_heads",
    )


def assemble_kernel(relative, place, own, *refs):
    *refs, out = refs
    shard, group = place[0], place[1]
    kinds = own.shape[0]
    out[:, pl.ds(shard, 1)] = own[...].reshape(kinds, 1, *own.shape[1:])
    lane = 0
    for ref, order in zip(refs, relative):
        lanes = slice(lane, lane + ref.shape[-1])
        lane = lanes.stop % own.shape[-1]
        for at, change in enumerate(order):
            for step in range(ref.shape[1]):
                for kind in range(kinds):
                    out[kind, shard ^ (step + 1), group ^ change, :, lanes] = ref[at, step, kind]


def assemble(relative, place, own, refs):
    head = lax.axis_size("head")
    (out,), _ = ordered_call(
        functools.partial(assemble_kernel, relative),
        (place, own, *refs),
        (),
        (),
        out_shape=(jax.ShapeDtypeStruct((own.shape[0], head) + own.shape[1:], bf16),),
        in_specs=[pl.BlockSpec(memory_space=pltpu.SMEM)] + vmem_specs(1 + len(refs)),
        out_specs=vmem_specs(1),
        compiler_params=pltpu.CompilerParams(vmem_limit_bytes=32 * 2**20),
        cost_estimate=cost(1.5),
        name="assemble",
    )
    return out


def grow(value, order):
    value, relative = value[None], [0]
    for place in order:
        value = jnp.concatenate([value, swap(value, "dp", 1 << place)], axis=0)
        relative = relative + [other ^ (1 << place) for other in relative]
    return value, relative


def flip_kernel(count, *refs):
    for source, target in zip(refs[:count], refs[count:]):
        for at in range(0, source.shape[0], BLK):
            target[:, at : at + BLK] = source[at : at + BLK, :].T


def flip(values, passes):
    return ordered_call(
        functools.partial(flip_kernel, len(values)),
        values,
        (),
        passes,
        out_shape=[jax.ShapeDtypeStruct(v.shape[::-1], v.dtype) for v in values],
        in_specs=vmem_specs(len(values)),
        out_specs=vmem_specs(len(values)),
        compiler_params=pltpu.CompilerParams(vmem_limit_bytes=32 * 2**20),
        cost_estimate=cost(1.5),
        name="flip",
    )


def collect_kernel(*refs):
    *parts, out = refs
    for k, ref in enumerate(parts):
        out[k] = ref[...]


def collect(values):
    (out,), _ = ordered_call(
        collect_kernel,
        values,
        (),
        (),
        out_shape=(jax.ShapeDtypeStruct((len(values),) + values[0].shape, values[0].dtype),),
        in_specs=vmem_specs(len(values)),
        out_specs=vmem_specs(1),
        compiler_params=pltpu.CompilerParams(vmem_limit_bytes=32 * 2**20),
        cost_estimate=cost(1.4),
        name="collect",
    )
    return out


def from_heads_in_turn(piece):
    got = [swap(piece, "head", 1)]
    step = 2
    while step < lax.axis_size("head"):
        far = [swap(value, "head", step) for value in [piece]]
        for value in far:
            got = got + [value, swap(value, "head", 1)]
        step *= 2
    return got


def from_heads(piece):
    return [swap(piece, "head", step) for step in range(1, lax.axis_size("head"))]


def added(keep, got):
    return keep.astype(f32) + got.astype(f32)


def advance_kernel(counts, size, tail, scalars, keep, got, send, out):
    core, mine = scalars[0], scalars[1]
    blocks = (keep.shape[0] - tail) // size
    for target, which in ((send, 1 - mine), (out, mine)):
        for k in range(blocks // 2):
            spots = [2 * (k // after) * after + k % after for after in counts]
            at = jnp.where(core == 0, spots[0] + which * counts[0], spots[1] + which * counts[1])
            here = pl.ds(at * size, size)
            target[k * size : (k + 1) * size] = added(keep[here], got[here]).astype(bf16)
        if tail:
            value = added(keep[blocks * size :], got[blocks * size :]).astype(bf16)
            target[blocks // 2 * size :] = value


def turn_heads_kernel(head, scalars, keep, got, send, out):
    mine = scalars[1]
    tiles, _, columns = keep.shape
    rows, width = (tiles - 1) * TILE, columns // 4
    held = added(keep[: tiles - 1], got[: tiles - 1]).reshape(rows, columns)
    part, thin = width // head, rows // head
    kinds = []
    if rows < BLK:
        filler = jnp.zeros((BLK - rows, width), f32)
    for kind in range(1, 4):
        value = held[:, kind * width : (kind + 1) * width]
        value = jnp.concatenate([value, filler], axis=0) if rows < BLK else value
        kinds.append(value.T)
    high = part // (width // BLK)
    count = part // TILE
    for shard in range(head):
        pieces = [value[shard * part : (shard + 1) * part] for value in kinds]
        own = held[shard * thin : (shard + 1) * thin, :width]
        own = jnp.concatenate([own, jnp.zeros((high - thin, width), f32)], axis=0)
        pieces.append(jnp.concatenate([own[:, at : at + BLK] for at in range(0, width, BLK)], axis=0))
        for chosen, target in ((1 - mine, send), (mine, out)):

            @pl.when(chosen == shard % 2)
            def _(target=target, pieces=pieces, shard=shard):
                for kind, piece in enumerate(pieces):
                    at = (shard // 2 * 4 + kind) * count
                    target[at : at + count] = piece.reshape(count, TILE, BLK).astype(bf16)

    last = added(keep[tiles - 1], got[tiles - 1])
    for target in (send, out):
        for k in range(2 * width // BLK):
            target[head // 2 * 4 * count + k] = last[:, k * BLK : (k + 1) * BLK].astype(bf16)


class Flight:
    def __init__(self, send, keep, turned):
        dp, head = lax.axis_size("dp"), lax.axis_size("head")
        bits = dp.bit_length() - 1
        upper = list(range(1, bits))
        self.orders = [list(upper), list(upper)[::-1]]
        self.left = [upper[::-1], upper[::-1]]
        self.head_bits = list(range(head.bit_length() - 1))
        self.turned = turned
        self.keep, self.got = keep, swap(send, "dp", 1)
        self.tail, self.size = 0, 1
        if turned:
            self.tail, self.size = 1, (keep.shape[0] - 1) // (dp // 2)
        else:
            shape = (keep.shape[0] * keep.shape[1],) + keep.shape[2:]
            self.keep, self.got = self.keep.reshape(shape), self.got.reshape(shape)

    def step(self, waits=(), passes=()):
        blocks = (self.keep.shape[0] - self.tail) // self.size
        core = bit_of("dp", 0)
        rest = self.keep.shape[1:]
        devices = lax.axis_size("dp")
        counts = [1, 1]
        if self.orders[0]:
            places = [order.pop(0) for order in self.orders]
            counts = []
            for left, place in zip(self.left, places):
                axis = left.index(place)
                left.remove(place)
                counts.append((blocks // 2) >> axis)
            mine = jnp.where(core == 0, bit_of("dp", places[0]), bit_of("dp", places[1]))
            axis_name, pairs = "dp", [(i, i ^ (1 << places[i & 1])) for i in range(devices)]
        else:
            place = self.head_bits.pop(0)
            mine = bit_of("head", place)
            head = lax.axis_size("head")
            axis_name, pairs = "head", [(i, i ^ (1 << place)) for i in range(head)]
        if axis_name == "head" and self.turned:
            width = rest[1] // 4
            self.turned = False
            self.size, self.tail = 4 * (width // head) // TILE, 2 * width // BLK
            out_shape = (head // 2 * self.size + self.tail, TILE, BLK)
            kernel = functools.partial(turn_heads_kernel, head)
        else:
            out_shape = (blocks // 2 * self.size + self.tail,) + rest
            kernel = functools.partial(advance_kernel, counts, self.size, self.tail)
        out = jax.ShapeDtypeStruct(out_shape, bf16)
        (send, keep), passed = ordered_call(
            kernel,
            (jnp.stack([core, mine]).astype(jnp.int32), self.keep, self.got),
            waits,
            passes,
            out_shape=[out] * 2,
            in_specs=[pl.BlockSpec(memory_space=pltpu.SMEM)] + vmem_specs(2),
            out_specs=vmem_specs(2),
            compiler_params=pltpu.CompilerParams(vmem_limit_bytes=48 * 2**20),
            cost_estimate=cost(4),
            name="advance",
        )
        self.keep, self.got = keep, lax.ppermute(send, axis_name, pairs)
        return passed

    def finish(self):
        while self.orders[0] or self.head_bits:
            self.step()
        total = added(self.keep, self.got)
        return total if self.tail else total[0]


def per_device(
    tokens_in,
    segment,
    w_qkv,
    qv_bias,
    w_out,
    out_bias,
    ln1_gain,
    ln1_bias,
    w_up,
    up_bias,
    w_down,
    down_bias,
    ln2_gain,
    ln2_bias,
    cotangent,
):
    turn.last = []
    layers, width = w_qkv.shape[0], w_qkv.shape[1]
    part = w_qkv.shape[3] * w_qkv.shape[4]
    head_size = w_qkv.shape[4]
    tokens = tokens_in.shape[0]
    seq = segment.shape[1]
    dp, head = lax.axis_size("dp"), lax.axis_size("head")
    bits = dp.bit_length() - 1
    shard, group = lax.axis_index("head"), lax.axis_index("dp")
    halves = seq // tokens
    row, half = shard // halves, shard % halves
    upper = list(range(1, bits))

    edge = jnp.where(half == 0, tokens - HALO, 0)
    core = bit_of("dp", 0)

    own_w = w_qkv.transpose(0, 2, 3, 4, 1).reshape(layers, 3, part, width)
    own_first = own_w[0].reshape(3, dp, part // dp, width)
    piece = pick(own_first, group, 1).reshape(-1, width)
    rows_w = piece.shape[0]
    bias_own = qv_bias.reshape(1, layers * 2 * part)
    bias_own = jnp.pad(bias_own, ((0, 7), (0, width - bias_own.shape[1])))
    piece = jnp.concatenate([piece, bias_own])
    got = from_heads(piece)
    halo = swap(lax.dynamic_slice_in_dim(tokens_in, edge, HALO), "head", 1)
    biases = jnp.stack([other[rows_w, : layers * 2 * part] for other in [piece] + got])
    biases = biases.reshape(head, layers * 2, 1, part).astype(f32)
    members = jnp.arange(head)
    matches = (members[:, None] ^ shard) == members[None, :]
    bias_all = jnp.sum(jnp.where(matches[:, None, :, None], biases, 0.0), axis=0).reshape(layers, 2, -1)
    got = jnp.stack([other[:rows_w] for other in got]).reshape(head - 1, 3, part // dp, width)
    left, relative_left = grow(got[..., : width // 2], upper)
    right, relative_right = grow(got[..., width // 2 :], upper[::-1])
    both = jnp.stack([left, right])
    both = jnp.concatenate([both, swap(both, "dp", 1)], axis=1)
    relative = [order + [other ^ 1 for other in order] for order in (relative_left, relative_right)]
    place = jnp.stack([shard, group]).astype(jnp.int32)
    own_later = [own_w[k].reshape(3, 2, part // 2, width) for k in range(1, layers)]
    (low_t, halo_t), pieces = flip([tokens_in, halo], [pick(own, core, 1) for own in own_later])
    later_got = [from_heads_in_turn(value) for value in pieces]
    w_cats = [assemble(relative, place, own_first, [both[0], both[1]]).reshape(3 * head * part, width)]

    def later_weights(own, got):
        theirs = swap(got, "dp", 1)
        whole = assemble([[0], [1]], jnp.stack([shard, core]).astype(jnp.int32), own, [got[None], theirs[None]])
        return whole.reshape(3 * head * part, width)

    labels = pick(segment, row, 0)
    own_labels = lax.dynamic_slice_in_dim(labels, half * tokens, tokens)
    halo_start = jnp.where(half == 0, tokens, tokens - HALO)
    halo_labels = lax.dynamic_slice_in_dim(labels, halo_start, HALO)
    blocks = tokens // BLK
    by_block = own_labels.reshape(blocks, BLK)
    least, most = by_block[:, :1], by_block[:, -1:]

    def count(flags):
        return jnp.sum(flags.astype(jnp.int32), axis=1)

    bounds = jnp.stack(
        [
            count(own_labels[None] < least) // BLK,
            (count(own_labels[None] <= most) + BLK - 1) // BLK,
            count(halo_labels[None] < least) // BLK,
            (count(halo_labels[None] <= most) + BLK - 1) // BLK,
        ],
        axis=1,
    )
    segq = jnp.concatenate([by_block, by_block], axis=1).reshape(blocks, 1, 2 * BLK)
    segk = jnp.concatenate([own_labels, halo_labels]).reshape(-1, 1)
    core_at = core.reshape(1).astype(jnp.int32)

    vecs = jnp.stack(
        [out_bias, ln1_gain, ln1_bias, down_bias, ln2_gain, ln2_bias, out_bias, out_bias], axis=1
    ).astype(f32)
    up_bias_wide = up_bias.astype(f32)

    hidden, low = tokens_in, tokens_in
    saved = []
    for layer_idx in range(layers):
        last = layer_idx == layers - 1
        w_cat = w_cats[layer_idx]
        zero = jnp.zeros((width,), f32)
        bias_q, bias_v = bias_all[layer_idx, 0], bias_all[layer_idx, 1]
        shift = jnp.concatenate([bias_q, zero, bias_v])
        factor = jnp.concatenate([zero + 0.125, zero + 1.0, zero + 1.0])
        qkv = ((nt(low, w_cat) + shift) * factor).astype(bf16)
        kvh = (nt(halo, w_cat[width:]) + shift[width:]).astype(bf16)
        (ctx, ctx_t, ctx_low, lse), _ = attend(bounds, segq, segk, qkv, kvh, (), ())
        if not last:
            got = collect(later_got[layer_idx])
        fed, _ = feed(
            last, layer_idx, hidden, ctx, w_out, vecs[layer_idx], w_up, up_bias_wide[layer_idx : layer_idx + 1], w_down, (), ()
        )
        first_rows, first_t, active_t, slope, second_rows, after_low = fed[:6]
        saved.append((low_t, halo_t, qkv, kvh, ctx_t, ctx_low, lse, first_rows, first_t, active_t, slope, second_rows))
        if last:
            output = after_low
        else:
            low, hidden, low_t = after_low, fed[6], fed[7]
            halo = swap(lax.dynamic_slice_in_dim(low, edge, HALO), "head", 1)
            halo_t = halo.T
            w_cats.append(later_weights(own_later[layer_idx], got))

    grad_hidden = cotangent
    flights = []
    for layer_idx in reversed(range(layers)):
        low_t, halo_t, qkv, kvh, ctx_t, ctx_low, lse, first_rows, first_t, active_t, slope, second_rows = saved[layer_idx]
        w_cat = w_cats[layer_idx]
        (dz, du, da, dr, dc, sums, up_sum), _ = feed_back(
            layer_idx, grad_hidden, second_rows, first_rows, slope, w_down, w_up, w_out, vecs[layer_idx], (), ()
        )
        if flights:
            flights[1].step()
        (send, keep), _ = grad_feed(core_at, active_t, dz, first_t, du, dp, head, (), ())
        fed = Flight(send, keep, False)
        if flights:
            flights[0].step()
        (dqkv, dkvh, sums), _ = attend_back(bounds, segq, segk, qkv, kvh, ctx_t, lse, dc, sums, up_sum, (), ())
        part_halo = nn(dkvh, w_cat[width:]).astype(bf16)
        (part_halo,) = fed.step(passes=(part_halo,))
        back = swap(part_halo, "head", 1)
        if flights:
            flights[1].step()
        (send, keep), _ = grad_heads(core_at, ctx_low, low_t, halo_t, da, dqkv, dkvh, sums, dp, (), ())
        heads = Flight(send, keep, True)
        padded = lax.dynamic_update_slice(jnp.zeros((tokens, width), bf16), back, (edge, 0))
        grad_hidden = nn(dqkv, w_cat) + dr + padded.astype(f32)
        if flights:
            flights[0].step()
            flights[1].step()
            heads.step()
            flights[0].step()
            flights[1].step()
            fed.step()
            heads.step()
            fed.step()
            heads.step()
            fed.step()
            heads.step()
        flights = flights + [fed, heads]

    results = []
    for place in range(layers):
        fed, heads = flights[2 * place], flights[2 * place + 1]
        thin = width // (dp * head)
        total = fed.finish()
        out_down = total[0].reshape(-1, width)
        out_up = total[1].transpose(1, 0, 2).reshape(thin, -1)
        total = heads.finish()
        pieces = total[: 4 * part // TILE].reshape(4, part, BLK)
        out_out = pieces[3].reshape(width // BLK, -1, BLK)[:, :thin].transpose(1, 0, 2).reshape(thin, width)
        sums = total[4 * part // TILE :].transpose(1, 0, 2).reshape(TILE, 2, width).transpose(1, 0, 2)
        results.append((pieces[:3, :, : width // dp], out_out, out_up, out_down, sums.reshape(2 * TILE, width)))
    results = results[::-1]
    out_qkv, out_w_out, out_up, out_down, total = (jnp.stack([r[k] for r in results]) for k in range(5))
    out_qkv = out_qkv.reshape(layers, 3, part // head_size, head_size, -1).transpose(0, 4, 1, 2, 3)

    device = group * head + shard
    thin = width // (dp * head)
    mine = lax.dynamic_slice_in_dim(total[:, :6], device * thin, thin, axis=2)
    ups = total[:, 8 : 8 + up_bias.shape[1] // width].reshape(layers, -1)
    thick = ups.shape[1] // (dp * head)
    out_ups = lax.dynamic_slice_in_dim(ups, device * thick, thick, axis=1)
    qvs = total[:, 6:8].reshape(layers, 2, head, part // head_size, dp, head_size // dp)
    out_qv = pick(pick(qvs, shard, 2), group, 3)
    return (
        output,
        grad_hidden,
        out_qkv,
        out_qv,
        out_w_out,
        mine[:, 0],
        mine[:, 1],
        mine[:, 2],
        out_up,
        out_ups,
        out_down,
        mine[:, 3],
        mine[:, 4],
        mine[:, 5],
    )


def solution(mesh):
    return jax.shard_map(
        per_device,
        mesh=mesh,
        in_specs=(
            P(("dp", "head"), None),
            P("dp", None),
            P(None, None, None, "head", None),
            P(None, None, "head", None),
            P(),
            P(),
            P(),
            P(),
            P(),
            P(),
            P(),
            P(),
            P(),
            P(),
            P(("dp", "head"), None),
        ),
        out_specs=(
            P(("dp", "head"), None),
            P(("dp", "head"), None),
            P(None, "dp", None, "head", None),
            P(None, None, "head", "dp"),
            P(None, ("dp", "head"), None),
            P(None, ("dp", "head")),
            P(None, ("dp", "head")),
            P(None, ("dp", "head")),
            P(None, ("dp", "head"), None),
            P(None, ("dp", "head")),
            P(None, ("dp", "head"), None),
            P(None, ("dp", "head")),
            P(None, ("dp", "head")),
            P(None, ("dp", "head")),
        ),
        check_vma=False,
    )
```

```python
import functools

import jax
import jax.numpy as jnp
from jax import lax
from jax.experimental import pallas as pl
from jax.experimental.pallas import tpu as pltpu
from jax.sharding import PartitionSpec as P

norm_eps = 1e-06
masked_score = -1000000000.0
f32 = jnp.float32
bf16 = jnp.bfloat16

BLK = 128
TILE = 8
SCALE = 0.5
HALO = 384


def cost(microseconds):
    return pl.CostEstimate(flops=int(microseconds * SCALE * 1.15e9), bytes_accessed=1000, transcendentals=0)


def swap(value, axis, bit):
    size = lax.axis_size(axis)
    return lax.ppermute(value, axis, [(i, i ^ bit) for i in range(size)])


def bit_of(axis, place):
    return (lax.axis_index(axis) >> place) & 1


def pick(value, index, axis):
    return lax.dynamic_index_in_dim(value, index, axis, keepdims=False)


def add_low(*terms):
    total = terms[0].astype(f32)
    for term in terms[1:]:
        total = total + term.astype(f32)
    return total


def finish_head(slot):
    size = lax.axis_size("head")
    me = lax.axis_index("head")
    got = [swap(slot(me ^ step), "head", step) for step in range(1, size)]
    return add_low(slot(me), *got)


def head_masks():
    lane = lax.broadcasted_iota(jnp.int32, (BLK, BLK), 1)
    return lane < BLK // 2


def stack_heads(pair, low):
    zero = jnp.zeros_like(pair)
    return jnp.concatenate([jnp.where(low, pair, zero), jnp.where(low, zero, pair)], axis=0)


def nt(left, right):
    return lax.dot_general(left, right, (((1,), (1,)), ((), ())), preferred_element_type=f32)


def nn(left, right):
    return lax.dot_general(left, right, (((1,), (0,)), ((), ())), preferred_element_type=f32)


def attend_kernel(pairs, own_blocks, halo_blocks, bounds, segq, segk, qkv, kvh, ctx, ctx_t, ctx_low, lse, vt, qs, top, total, acc):
    width = pairs * BLK
    low = head_masks()
    half = BLK // 2
    for j in range(own_blocks + halo_blocks):
        for p in range(pairs):
            if j < own_blocks:
                tile = qkv[j * BLK : (j + 1) * BLK, 2 * width + p * BLK : 2 * width + (p + 1) * BLK]
            else:
                at = j - own_blocks
                tile = kvh[at * BLK : (at + 1) * BLK, width + p * BLK : width + (p + 1) * BLK]
            vt[j, p * BLK : (p + 1) * BLK, :] = tile.T

    def q_block(i, carry):
        rows = pl.ds(pl.multiple_of(i * BLK, BLK), BLK)
        for p in range(pairs):
            qs[p] = stack_heads(qkv[rows, p * BLK : (p + 1) * BLK], low)
        top[...] = jnp.full(top.shape, -1e30, f32)
        total[...] = jnp.zeros(total.shape, f32)
        acc[...] = jnp.zeros(acc.shape, f32)
        labels = segq[i]

        def k_block(ref, first, base, j, carry):
            here = pl.ds(pl.multiple_of(j * BLK, BLK), BLK)
            there = pl.ds(pl.multiple_of((base + j) * BLK, BLK), BLK)
            same = segk[there, :] == labels
            for p in range(pairs):
                keys = ref[here, first + p * BLK : first + (p + 1) * BLK]
                scores = jnp.where(same, nt(keys, qs[p]), masked_score)
                old = top[p : p + 1, :]
                new = jnp.maximum(old, jnp.max(scores, axis=0, keepdims=True))
                expo = jnp.exp(scores - new)
                scale = jnp.exp(old - new)
                top[p : p + 1, :] = new
                total[p : p + 1, :] = total[p : p + 1, :] * scale + jnp.sum(expo, axis=0, keepdims=True)
                weights = expo.astype(bf16)
                for h in range(2):
                    values = vt[base + j, p * BLK + h * half : p * BLK + (h + 1) * half, :]
                    part = slice(h * half, (h + 1) * half)
                    cols = slice(h * BLK, (h + 1) * BLK)
                    acc[p, part, :] = acc[p, part, :] * scale[:, cols] + nn(values, weights[:, cols])
            return carry

        lax.fori_loop(bounds[i, 0], bounds[i, 1], functools.partial(k_block, qkv, width, 0), 0)
        lax.fori_loop(bounds[i, 2], bounds[i, 3], functools.partial(k_block, kvh, 0, own_blocks), 0)
        for p in range(pairs):
            inverse = 1.0 / total[p : p + 1, :]
            flat = jnp.concatenate(
                [acc[p, :half, :] * inverse[:, :BLK], acc[p, half:, :] * inverse[:, BLK:]], axis=0
            )
            rounded = flat.astype(bf16)
            ctx_t[p * BLK : (p + 1) * BLK, rows] = flat
            ctx_low[p * BLK : (p + 1) * BLK, rows] = rounded
            ctx[rows, p * BLK : (p + 1) * BLK] = rounded.T
        lse[i] = top[...] + jnp.log(total[...])
        return carry

    lax.fori_loop(0, own_blocks, q_block, 0)


def attend_back_kernel(
    pairs, own_blocks, halo_blocks,
    bounds, segq, segk, qkv, kvh, ctx_t, lse, dctx, norm_sums, up_sum,
    dqkv, dkvh, sums,
    kt, qs, cs, delta, dqt, dk, dv,
):
    width = pairs * BLK
    low = head_masks()
    half = BLK // 2
    blocks = own_blocks + halo_blocks
    for j in range(blocks):
        for p in range(pairs):
            if j < own_blocks:
                tile = qkv[j * BLK : (j + 1) * BLK, width + p * BLK : width + (p + 1) * BLK]
            else:
                at = j - own_blocks
                tile = kvh[at * BLK : (at + 1) * BLK, p * BLK : (p + 1) * BLK]
            kt[j, p * BLK : (p + 1) * BLK, :] = tile.T
    dk[...] = jnp.zeros(dk.shape, f32)
    dv[...] = jnp.zeros(dv.shape, f32)
    sums[...] = jnp.zeros(sums.shape, f32)
    sums[0:8, :] = norm_sums[...]
    for at in range(up_sum.shape[1] // width):
        sums[8 + at : 9 + at, :] = up_sum[:, at * width : (at + 1) * width]

    def q_block(i, carry):
        rows = pl.ds(pl.multiple_of(i * BLK, BLK), BLK)
        for p in range(pairs):
            cols = slice(p * BLK, (p + 1) * BLK)
            qs[p] = stack_heads(qkv[rows, cols], low)
            pull = dctx[rows, cols]
            cs[p] = stack_heads(pull, low)
            prod = pull.astype(f32).T * ctx_t[cols, rows]
            delta[p : p + 1, :] = jnp.concatenate(
                [jnp.sum(prod[:half], axis=0, keepdims=True), jnp.sum(prod[half:], axis=0, keepdims=True)], axis=1
            )
        dqt[...] = jnp.zeros(dqt.shape, f32)
        labels = segq[i]

        def k_block(ref, first, base, j, carry):
            here = pl.ds(pl.multiple_of(j * BLK, BLK), BLK)
            there = pl.ds(pl.multiple_of((base + j) * BLK, BLK), BLK)
            same = segk[there, :] == labels
            for p in range(pairs):
                cols = slice(p * BLK, (p + 1) * BLK)
                keys = ref[here, first + p * BLK : first + (p + 1) * BLK]
                values = ref[here, first + width + p * BLK : first + width + (p + 1) * BLK]
                scores = jnp.where(same, nt(keys, qs[p]), masked_score)
                probs = jnp.exp(scores - lse[i, p : p + 1, :])
                pulls = nt(values, cs[p])
                dscore = (probs * (pulls - delta[p : p + 1, :])).astype(bf16)
                dv[there, cols] += nn(probs.astype(bf16), cs[p])
                dk[there, cols] += nn(dscore, qs[p])
                for h in range(2):
                    part = slice(h * half, (h + 1) * half)
                    flip = kt[base + j, p * BLK + h * half : p * BLK + (h + 1) * half, :]
                    dqt[p, part, :] += nn(flip, dscore[:, h * BLK : (h + 1) * BLK])
            return carry

        lax.fori_loop(bounds[i, 0], bounds[i, 1], functools.partial(k_block, qkv, width, 0), 0)
        lax.fori_loop(bounds[i, 2], bounds[i, 3], functools.partial(k_block, kvh, 0, own_blocks), 0)
        for p in range(pairs):
            cols = slice(p * BLK, (p + 1) * BLK)
            grad = dqt[p].T.astype(bf16) * jnp.asarray(0.125, bf16)
            dqkv[rows, cols] = grad
            sums[6:7, cols] += jnp.sum(grad.astype(f32), axis=0, keepdims=True)
        return carry

    lax.fori_loop(0, own_blocks, q_block, 0)
    for j in range(blocks):
        rows = slice(j * BLK, (j + 1) * BLK)
        grad_k = dk[rows, :].astype(bf16)
        grad_v = dv[rows, :].astype(bf16)
        if j < own_blocks:
            dqkv[rows, width : 2 * width] = grad_k
            dqkv[rows, 2 * width :] = grad_v
        else:
            back = slice((j - own_blocks) * BLK, (j - own_blocks + 1) * BLK)
            dkvh[back, :width] = grad_k
            dkvh[back, width:] = grad_v
        sums[7:8, :] += jnp.sum(grad_v.astype(f32), axis=0, keepdims=True)


def vmem_specs(count):
    return [pl.BlockSpec(memory_space=pltpu.VMEM)] * count


def any_specs(count):
    return [pl.BlockSpec(memory_space=pl.ANY)] * count


def ordered_call(kernel, args, waits, passes, out_shape, in_specs, out_specs, **options):
    waits, passes = tuple(waits) + tuple(turn.last), tuple(passes)
    given, made = len(args), len(out_shape)
    skipped = len(waits) + len(passes)

    def body(*refs):
        outs = given + skipped
        refs[outs + made][...] = jnp.zeros((8, BLK), f32)
        kernel(*refs[:given], *refs[outs : outs + made], *refs[outs + made + 1 + len(passes) :])

    out = pl.pallas_call(
        body,
        out_shape=tuple(out_shape)
        + (jax.ShapeDtypeStruct((8, BLK), f32),)
        + tuple(jax.ShapeDtypeStruct(p.shape, p.dtype) for p in passes),
        in_specs=list(in_specs) + any_specs(skipped),
        out_specs=tuple(out_specs) + (pl.BlockSpec((8, BLK), lambda *step: (0, 0)),) + tuple(any_specs(len(passes))),
        input_output_aliases={given + len(waits) + k: made + 1 + k for k in range(len(passes))},
        **options,
    )(*args, *waits, *passes)
    turn.last = [out[made]]
    return out[:made], out[made + 1 :]


class Turn:
    last = []


turn = Turn()


def attend(bounds, segq, segk, qkv, kvh, waits, passes):
    tokens, width3 = qkv.shape
    width = width3 // 3
    pairs, own_blocks, halo_blocks = width // BLK, tokens // BLK, kvh.shape[0] // BLK
    blocks = own_blocks + halo_blocks
    return ordered_call(
        functools.partial(attend_kernel, pairs, own_blocks, halo_blocks),
        (bounds, segq, segk, qkv, kvh),
        waits,
        passes,
        out_shape=(
            jax.ShapeDtypeStruct((tokens, width), bf16),
            jax.ShapeDtypeStruct((width, tokens), f32),
            jax.ShapeDtypeStruct((width, tokens), bf16),
            jax.ShapeDtypeStruct((own_blocks, 8, 2 * BLK), f32),
        ),
        in_specs=[pl.BlockSpec(memory_space=pltpu.SMEM)] + vmem_specs(4),
        out_specs=tuple(vmem_specs(4)),
        scratch_shapes=[
            pltpu.VMEM((blocks, width, BLK), bf16),
            pltpu.VMEM((pairs, 2 * BLK, BLK), bf16),
            pltpu.VMEM((8, 2 * BLK), f32),
            pltpu.VMEM((8, 2 * BLK), f32),
            pltpu.VMEM((pairs, BLK, BLK), f32),
        ],
        compiler_params=pltpu.CompilerParams(vmem_limit_bytes=32 * 2**20),
        cost_estimate=cost(9),
        name="attend",
    )


def attend_back(bounds, segq, segk, qkv, kvh, ctx_t, lse, dctx, norm_sums, up_sum, waits, passes):
    tokens, width3 = qkv.shape
    width = width3 // 3
    pairs, own_blocks, halo_blocks = width // BLK, tokens // BLK, kvh.shape[0] // BLK
    blocks = own_blocks + halo_blocks
    return ordered_call(
        functools.partial(attend_back_kernel, pairs, own_blocks, halo_blocks),
        (bounds, segq, segk, qkv, kvh, ctx_t, lse, dctx, norm_sums, up_sum),
        waits,
        passes,
        out_shape=(
            jax.ShapeDtypeStruct((tokens, width3), bf16),
            jax.ShapeDtypeStruct(kvh.shape, bf16),
            jax.ShapeDtypeStruct((16, width), f32),
        ),
        in_specs=[pl.BlockSpec(memory_space=pltpu.SMEM)] + vmem_specs(9),
        out_specs=tuple(vmem_specs(3)),
        scratch_shapes=[
            pltpu.VMEM((blocks, width, BLK), bf16),
            pltpu.VMEM((pairs, 2 * BLK, BLK), bf16),
            pltpu.VMEM((pairs, 2 * BLK, BLK), bf16),
            pltpu.VMEM((8, 2 * BLK), f32),
            pltpu.VMEM((pairs, BLK, BLK), f32),
            pltpu.VMEM((blocks * BLK, width), f32),
            pltpu.VMEM((blocks * BLK, width), f32),
        ],
        compiler_params=pltpu.CompilerParams(vmem_limit_bytes=40 * 2**20),
        cost_estimate=cost(21),
        name="attend_back",
    )


CHUNK = 1536
ROWS = 256


def normalized(rows):
    center = rows - jnp.mean(rows, axis=-1, keepdims=True)
    spread = jnp.mean(center * center, axis=-1, keepdims=True)
    scale = lax.rsqrt(spread + norm_eps)
    return center * scale, scale


def feed_kernel(last, tokens, hidden, ctx, w_out, vec, w_up, up_bias, w_down, *rest):
    if last:
        first_rows, first_t, active_t, slope, second_rows, low, low_rows, first, total = rest
    else:
        first_rows, first_t, active_t, slope, second_rows, low, after, low_t, low_rows, first, total = rest
    step = pl.program_id(0)
    tiles = [slice(at, at + BLK) for at in range(0, tokens, BLK)]
    passes = [slice(at, at + ROWS) for at in range(0, tokens, ROWS)]

    @pl.when(step == 0)
    def _():
        for rows in tiles:
            resid = hidden[rows, :].astype(f32) + (nn(ctx[rows, :], w_out[...]) + vec[0:1, :])
            first_rows[rows, :] = resid
            unit, _ = normalized(resid)
            value = unit * vec[1:2, :] + vec[2:3, :]
            first[rows, :] = value
            total[rows, :] = jnp.zeros_like(value)
            rounded = value.astype(bf16)
            low_rows[rows, :] = rounded
            first_t[:, rows] = rounded.T

    for rows in passes:
        upward = nn(low_rows[rows, :], w_up[...]) + up_bias[...]
        density = jnp.exp(-0.5 * upward * upward) * 0.3989422804014327
        below = 0.5 + 0.5 * lax.erf(upward * 0.7071067811865476)
        active = (upward * below).astype(bf16)
        slope[rows, :] = below + upward * density
        active_t[:, rows] = active.T
        total[rows, :] += nn(active, w_down[...])

    @pl.when(step == pl.num_programs(0) - 1)
    def _():
        for rows in tiles:
            resid = first[rows, :] + (total[rows, :] + vec[3:4, :])
            second_rows[rows, :] = resid
            unit, _ = normalized(resid)
            value = unit * vec[4:5, :] + vec[5:6, :]
            rounded = value.astype(bf16)
            low[rows, :] = rounded
            if not last:
                after[rows, :] = value
                low_t[:, rows] = rounded.T


def whole(shape):
    return pl.BlockSpec(shape, lambda step: (0,) * len(shape))


def feed(last, layer_idx, hidden, ctx, w_out, vec, w_up, up_bias, w_down, waits, passes):
    tokens, width = hidden.shape
    wide = w_up.shape[-1]
    rows = whole((tokens, width))
    shapes = [
        jax.ShapeDtypeStruct((tokens, width), f32),
        jax.ShapeDtypeStruct((width, tokens), bf16),
        jax.ShapeDtypeStruct((wide, tokens), bf16),
        jax.ShapeDtypeStruct((tokens, wide), f32),
        jax.ShapeDtypeStruct((tokens, width), f32),
        jax.ShapeDtypeStruct((tokens, width), bf16),
    ]
    specs = [
        rows,
        whole((width, tokens)),
        pl.BlockSpec((CHUNK, tokens), lambda step: (step, 0)),
        pl.BlockSpec((tokens, CHUNK), lambda step: (0, step)),
        rows,
        rows,
    ]
    if not last:
        shapes.append(jax.ShapeDtypeStruct((tokens, width), f32))
        shapes.append(jax.ShapeDtypeStruct((width, tokens), bf16))
        specs.append(rows)
        specs.append(whole((width, tokens)))
    return ordered_call(
        functools.partial(feed_kernel, last, tokens),
        (hidden, ctx, w_out, vec, w_up, up_bias, w_down),
        waits,
        passes,
        grid=(wide // CHUNK,),
        out_shape=tuple(shapes),
        in_specs=[
            rows,
            rows,
            pl.BlockSpec((None, width, width), lambda step: (layer_idx, 0, 0)),
            whole(vec.shape),
            pl.BlockSpec((None, width, CHUNK), lambda step: (layer_idx, 0, step)),
            pl.BlockSpec((1, CHUNK), lambda step: (0, step)),
            pl.BlockSpec((None, CHUNK, width), lambda step: (layer_idx, step, 0)),
        ],
        out_specs=tuple(specs),
        scratch_shapes=[
            pltpu.VMEM((tokens, width), bf16),
            pltpu.VMEM((tokens, width), f32),
            pltpu.VMEM((tokens, width), f32),
        ],
        compiler_params=pltpu.CompilerParams(vmem_limit_bytes=48 * 2**20),
        cost_estimate=cost(15),
        name="feed",
    )


def norm_back(grad, gain, rows):
    unit, scale = normalized(rows)
    lifted = grad * gain
    first = jnp.mean(lifted, axis=-1, keepdims=True)
    second = jnp.mean(lifted * unit, axis=-1, keepdims=True)
    return scale * (lifted - first - unit * second), unit


def over_rows(value):
    return jnp.sum(value, axis=0, keepdims=True)


def feed_back_kernel(
    tokens, grad, second_rows, first_rows, slope, w_down, w_up, w_out, vec,
    dz, du, da, dr, dc, sums, up_sum, dr_two, total,
):
    step = pl.program_id(0)
    tiles = [slice(at, at + BLK) for at in range(0, tokens, BLK)]
    passes = [slice(at, at + ROWS) for at in range(0, tokens, ROWS)]

    @pl.when(step == 0)
    def _():
        sums[...] = jnp.zeros(sums.shape, f32)
        for rows in tiles:
            pull = grad[rows, :].astype(f32)
            value, unit = norm_back(pull, vec[4:5, :], second_rows[rows, :])
            dr_two[rows, :] = value
            total[rows, :] = jnp.zeros_like(value)
            rounded = value.astype(bf16)
            dz[rows, :] = rounded
            sums[3:4, :] += over_rows(rounded.astype(f32))
            sums[4:5, :] += over_rows(pull * unit)
            sums[5:6, :] += over_rows(pull)

    up_sum[...] = jnp.zeros(up_sum.shape, f32)
    for rows in passes:
        pull = (nt(dz[rows, :], w_down[...]) * slope[rows, :]).astype(bf16)
        du[rows, :] = pull
        up_sum[...] += over_rows(pull.astype(f32))
        total[rows, :] += nt(pull, w_up[...])

    @pl.when(step == pl.num_programs(0) - 1)
    def _():
        for rows in tiles:
            pull = total[rows, :] + dr_two[rows, :]
            value, unit = norm_back(pull, vec[1:2, :], first_rows[rows, :])
            dr[rows, :] = value
            rounded = value.astype(bf16)
            da[rows, :] = rounded
            sums[0:1, :] += over_rows(rounded.astype(f32))
            sums[1:2, :] += over_rows(pull * unit)
            sums[2:3, :] += over_rows(pull)
            dc[rows, :] = nt(rounded, w_out[...]).astype(bf16)


def feed_back(layer_idx, grad, second_rows, first_rows, slope, w_down, w_up, w_out, vec, waits, passes):
    tokens, width = grad.shape
    wide = w_up.shape[-1]
    rows = whole((tokens, width))
    return ordered_call(
        functools.partial(feed_back_kernel, tokens),
        (grad, second_rows, first_rows, slope, w_down, w_up, w_out, vec),
        waits,
        passes,
        grid=(wide // CHUNK,),
        out_shape=(
            jax.ShapeDtypeStruct((tokens, width), bf16),
            jax.ShapeDtypeStruct((tokens, wide), bf16),
            jax.ShapeDtypeStruct((tokens, width), bf16),
            jax.ShapeDtypeStruct((tokens, width), f32),
            jax.ShapeDtypeStruct((tokens, width), bf16),
            jax.ShapeDtypeStruct((8, width), f32),
            jax.ShapeDtypeStruct((1, wide), f32),
        ),
        in_specs=[
            rows,
            rows,
            rows,
            pl.BlockSpec((tokens, CHUNK), lambda step: (0, step)),
            pl.BlockSpec((None, CHUNK, width), lambda step: (layer_idx, step, 0)),
            pl.BlockSpec((None, width, CHUNK), lambda step: (layer_idx, 0, step)),
            pl.BlockSpec((None, width, width), lambda step: (layer_idx, 0, 0)),
            whole(vec.shape),
        ],
        out_specs=(
            rows,
            pl.BlockSpec((tokens, CHUNK), lambda step: (0, step)),
            rows,
            rows,
            rows,
            whole((8, width)),
            pl.BlockSpec((1, CHUNK), lambda step: (0, step)),
        ),
        scratch_shapes=[pltpu.VMEM((tokens, width), f32), pltpu.VMEM((tokens, width), f32)],
        compiler_params=pltpu.CompilerParams(vmem_limit_bytes=48 * 2**20),
        cost_estimate=cost(17),
        name="feed_back",
    )


def grad_down_kernel(core, active_t, dz, send, keep):
    groups, head, parts, thin, width = send.shape
    mine = core[0]
    for which, out in ((1 - mine, send), (mine, keep)):
        for group in range(groups):
            value = nn(active_t[2 * group + which], dz[...])
            for shard in range(head):
                for at in range(parts):
                    here = (shard * parts + at) * thin
                    out[group, shard, at] = value[here : here + thin].astype(bf16)


def grad_up_kernel(core, first_t, du, send, keep, lhs):
    groups, head, parts, thin, width = send.shape
    rows = head * thin
    mine = core[0]
    for which, out in ((1 - mine, send), (mine, keep)):
        if rows % 16 == 0:
            for group in range(groups):
                lhs[group * rows : (group + 1) * rows, :] = first_t[2 * group + which]
        for at in range(parts):
            pulls = du[:, at * width : (at + 1) * width]
            if rows % 16 == 0:
                value = nn(lhs[...], pulls)
                values = [value[group * rows : (group + 1) * rows] for group in range(groups)]
            else:
                values = [nn(first_t[2 * group + which], pulls) for group in range(groups)]
            for group in range(groups):
                for shard in range(head):
                    out[group, shard, at] = values[group][shard * thin : (shard + 1) * thin].astype(bf16)


def grad_feed(core, left_t, right, parts, devices, head, scratch):
    rows, tokens = left_t.shape
    thin = rows // devices // head // (1 if scratch else parts)
    width = right.shape[1] // (parts if scratch else 1)
    out = jax.ShapeDtypeStruct((devices // 2, head, parts, thin, width), bf16)
    halves, _ = ordered_call(
        grad_up_kernel if scratch else grad_down_kernel,
        (core, left_t.reshape(devices, rows // devices, tokens), right),
        (),
        (),
        out_shape=(out, out),
        in_specs=[pl.BlockSpec(memory_space=pltpu.SMEM)] + vmem_specs(2),
        out_specs=tuple(vmem_specs(2)),
        scratch_shapes=[pltpu.VMEM((rows // 2, tokens), bf16)] if scratch else [],
        compiler_params=pltpu.CompilerParams(vmem_limit_bytes=48 * 2**20),
        cost_estimate=cost(5),
        name="grad_up" if scratch else "grad_down",
    )
    return halves


def grad_heads_kernel(core, ctx_t, low_t, halo_t, da, dqkv, dkvh, sums, send, keep, one, two, three):
    groups, thin = ctx_t.shape[0] // 2, ctx_t.shape[1]
    width = send.shape[2] // 4
    high = thin // TILE
    for r in range(sums.shape[0] // TILE):
        value = sums[r * TILE : (r + 1) * TILE, :].astype(bf16)
        for out in (send, keep):
            out[groups * high, :, r * width : (r + 1) * width] = value
    mine = core[0]
    for which, out in ((1 - mine, send), (mine, keep)):
        if thin % 16 == 0:
            for group in range(groups):
                here = slice(group * thin, (group + 1) * thin)
                one[here, :] = ctx_t[2 * group + which]
                two[here, :] = low_t[2 * group + which]
                three[here, :] = halo_t[2 * group + which]
            parts = [(range(groups), one, two, three)]
        else:
            parts = [
                ([group], ctx_t.at[2 * group + which], low_t.at[2 * group + which], halo_t.at[2 * group + which])
                for group in range(groups)
            ]
        for members, left_one, left_two, left_three in parts:
            for at in range(0, 4 * width, width):
                if at < width:
                    value = nn(left_one[...], da[...])
                else:
                    value = nn(left_two[...], dqkv[:, at - width : at])
                    if at >= 2 * width:
                        value = value + nn(left_three[...], dkvh[:, at - 2 * width : at - width])
                for place, group in enumerate(members):
                    here = value[place * thin : (place + 1) * thin].reshape(high, TILE, width)
                    out[group * high : (group + 1) * high, :, at : at + width] = here.astype(bf16)


def grad_heads(core, ctx_t, low_t, halo_t, da, dqkv, dkvh, sums, devices, waits, passes):
    tokens, width = da.shape
    thin = width // devices
    out = jax.ShapeDtypeStruct((devices // 2 * thin // TILE + 1, TILE, 4 * width), bf16)
    extent = halo_t.shape[1]
    return ordered_call(
        grad_heads_kernel,
        (
            core,
            ctx_t.reshape(devices, thin, tokens),
            low_t.reshape(devices, thin, tokens),
            halo_t.reshape(devices, thin, extent),
            da,
            dqkv,
            dkvh,
            sums,
        ),
        waits,
        passes,
        out_shape=(out, out),
        in_specs=[pl.BlockSpec(memory_space=pltpu.SMEM)] + vmem_specs(7),
        out_specs=tuple(vmem_specs(2)),
        scratch_shapes=[
            pltpu.VMEM((width // 2, tokens), bf16),
            pltpu.VMEM((width // 2, tokens), bf16),
            pltpu.VMEM((width // 2, extent), bf16),
        ],
        compiler_params=pltpu.CompilerParams(vmem_limit_bytes=48 * 2**20),
        cost_estimate=cost(8),
        name="grad_heads",
    )


def assemble_kernel(relative, place, own, *refs):
    *refs, out = refs
    shard, group = place[0], place[1]
    kinds = own.shape[0]
    out[:, pl.ds(shard, 1)] = own[...].reshape(kinds, 1, *own.shape[1:])
    lane = 0
    for ref, order in zip(refs, relative):
        lanes = slice(lane, lane + ref.shape[-1])
        lane = lanes.stop % own.shape[-1]
        for at, change in enumerate(order):
            for step in range(ref.shape[1]):
                for kind in range(kinds):
                    out[kind, shard ^ (step + 1), group ^ change, :, lanes] = ref[at, step, kind]


def assemble(relative, place, own, refs, passes):
    head = lax.axis_size("head")
    (out,), passed = ordered_call(
        functools.partial(assemble_kernel, relative),
        (place, own, *refs),
        (),
        passes,
        out_shape=(jax.ShapeDtypeStruct((own.shape[0], head) + own.shape[1:], bf16),),
        in_specs=[pl.BlockSpec(memory_space=pltpu.SMEM)] + vmem_specs(1 + len(refs)),
        out_specs=vmem_specs(1),
        compiler_params=pltpu.CompilerParams(vmem_limit_bytes=32 * 2**20),
        cost_estimate=cost(1.5),
        name="assemble",
    )
    return out, passed


def grow(value, order):
    value, relative = value[None], [0]
    for place in order:
        value = jnp.concatenate([value, swap(value, "dp", 1 << place)], axis=0)
        relative = relative + [other ^ (1 << place) for other in relative]
    return value, relative


def flip_kernel(count, *refs):
    for source, target in zip(refs[:count], refs[count:]):
        for at in range(0, source.shape[0], BLK):
            target[:, at : at + BLK] = source[at : at + BLK, :].T


def flip(values, passes):
    return ordered_call(
        functools.partial(flip_kernel, len(values)),
        values,
        (),
        passes,
        out_shape=[jax.ShapeDtypeStruct(v.shape[::-1], v.dtype) for v in values],
        in_specs=vmem_specs(len(values)),
        out_specs=vmem_specs(len(values)),
        compiler_params=pltpu.CompilerParams(vmem_limit_bytes=32 * 2**20),
        cost_estimate=cost(1.5),
        name="flip",
    )


def collect_kernel(*refs):
    *parts, out = refs
    for k, ref in enumerate(parts):
        out[k] = ref[...]


def collect(values):
    (out,), _ = ordered_call(
        collect_kernel,
        values,
        (),
        (),
        out_shape=(jax.ShapeDtypeStruct((len(values),) + values[0].shape, values[0].dtype),),
        in_specs=vmem_specs(len(values)),
        out_specs=vmem_specs(1),
        compiler_params=pltpu.CompilerParams(vmem_limit_bytes=32 * 2**20),
        cost_estimate=cost(1.4),
        name="collect",
    )
    return out


def from_heads_in_turn(piece):
    got = [swap(piece, "head", 1)]
    step = 2
    while step < lax.axis_size("head"):
        far = [swap(value, "head", step) for value in [piece]]
        for value in far:
            got = got + [value, swap(value, "head", 1)]
        step *= 2
    return got


def from_heads(piece):
    return [swap(piece, "head", step) for step in range(1, lax.axis_size("head"))]


def added(keep, got):
    return keep.astype(f32) + got.astype(f32)


def advance_kernel(counts, size, tail, sources, scalars, *refs):
    core, mine = scalars[0], scalars[1]
    keeps, gots, (send, out) = refs[:sources], refs[sources : 2 * sources], refs[2 * sources :]
    blocks = (keeps[0].shape[0] - tail) // size
    for target, which in ((send, 1 - mine), (out, mine)):
        for k in range(blocks // 2):
            spots = [2 * (k // after) * after + k % after for after in counts]
            at = jnp.where(core == 0, spots[0] + which * counts[0], spots[1] + which * counts[1])
            here = pl.ds(at * size, size)
            for source, (keep, got) in enumerate(zip(keeps, gots)):
                value = added(keep[here], got[here]).astype(bf16)
                if sources > 1:
                    target[k * size : (k + 1) * size, source] = value
                else:
                    target[k * size : (k + 1) * size] = value
        if tail:
            value = added(keeps[0][blocks * size :], gots[0][blocks * size :]).astype(bf16)
            target[blocks // 2 * size :] = value


def turn_heads_kernel(head, scalars, keep, got, send, out):
    mine = scalars[1]
    tiles, _, columns = keep.shape
    rows, width = (tiles - 1) * TILE, columns // 4
    held = added(keep[: tiles - 1], got[: tiles - 1]).reshape(rows, columns)
    part, thin = width // head, rows // head
    kinds = []
    if rows < BLK:
        filler = jnp.zeros((BLK - rows, width), f32)
    for kind in range(1, 4):
        value = held[:, kind * width : (kind + 1) * width]
        value = jnp.concatenate([value, filler], axis=0) if rows < BLK else value
        kinds.append(value.T)
    high = part // (width // BLK)
    count = part // TILE
    for shard in range(head):
        pieces = [value[shard * part : (shard + 1) * part] for value in kinds]
        own = held[shard * thin : (shard + 1) * thin, :width]
        own = jnp.concatenate([own, jnp.zeros((high - thin, width), f32)], axis=0)
        pieces.append(jnp.concatenate([own[:, at : at + BLK] for at in range(0, width, BLK)], axis=0))
        for chosen, target in ((1 - mine, send), (mine, out)):

            @pl.when(chosen == shard % 2)
            def _(target=target, pieces=pieces, shard=shard):
                for kind, piece in enumerate(pieces):
                    at = (shard // 2 * 4 + kind) * count
                    target[at : at + count] = piece.reshape(count, TILE, BLK).astype(bf16)

    last = added(keep[tiles - 1], got[tiles - 1])
    for target in (send, out):
        for k in range(2 * width // BLK):
            target[head // 2 * 4 * count + k] = last[:, k * BLK : (k + 1) * BLK].astype(bf16)


class Flight:
    def __init__(self, keeps, gots, turned):
        dp, head = lax.axis_size("dp"), lax.axis_size("head")
        bits = dp.bit_length() - 1
        upper = list(range(1, bits))
        self.orders = [list(upper), list(upper)[::-1]]
        self.left = [upper[::-1], upper[::-1]]
        self.head_bits = list(range(head.bit_length() - 1))
        self.turned = turned
        self.tail, self.size = 0, 1
        if turned:
            self.tail, self.size = 1, (keeps[0].shape[0] - 1) // (dp // 2)
        else:
            shape = (keeps[0].shape[0] * keeps[0].shape[1],) + keeps[0].shape[2:]
            keeps, gots = [k.reshape(shape) for k in keeps], [g.reshape(shape) for g in gots]
        self.keeps, self.gots = list(keeps), list(gots)

    def step(self, waits=(), passes=()):
        blocks = (self.keeps[0].shape[0] - self.tail) // self.size
        sources = len(self.keeps)
        core = bit_of("dp", 0)
        rest = self.keeps[0].shape[1:]
        if sources > 1:
            rest = (sources,) + rest
        devices = lax.axis_size("dp")
        counts = [1, 1]
        if self.orders[0]:
            places = [order.pop(0) for order in self.orders]
            counts = []
            for left, place in zip(self.left, places):
                axis = left.index(place)
                left.remove(place)
                counts.append((blocks // 2) >> axis)
            mine = jnp.where(core == 0, bit_of("dp", places[0]), bit_of("dp", places[1]))
            axis_name, pairs = "dp", [(i, i ^ (1 << places[i & 1])) for i in range(devices)]
        else:
            place = self.head_bits.pop(0)
            mine = bit_of("head", place)
            head = lax.axis_size("head")
            axis_name, pairs = "head", [(i, i ^ (1 << place)) for i in range(head)]
        if axis_name == "head" and self.turned:
            width = rest[1] // 4
            self.turned = False
            self.size, self.tail = 4 * (width // head) // TILE, 2 * width // BLK
            out_shape = (head // 2 * self.size + self.tail, TILE, BLK)
            kernel = functools.partial(turn_heads_kernel, head)
        else:
            out_shape = (blocks // 2 * self.size + self.tail,) + rest
            kernel = functools.partial(advance_kernel, counts, self.size, self.tail, sources)
        out = jax.ShapeDtypeStruct(out_shape, bf16)
        (send, keep), passed = ordered_call(
            kernel,
            (jnp.stack([core, mine]).astype(jnp.int32), *self.keeps, *self.gots),
            waits,
            passes,
            out_shape=[out] * 2,
            in_specs=[pl.BlockSpec(memory_space=pltpu.SMEM)] + vmem_specs(2 * sources),
            out_specs=vmem_specs(2),
            compiler_params=pltpu.CompilerParams(vmem_limit_bytes=48 * 2**20),
            cost_estimate=cost(1 + 2e-6 * out.size),
            name="advance",
        )
        self.keeps, self.gots = [keep], [lax.ppermute(send, axis_name, pairs)]
        return passed

    def finish(self):
        while self.orders[0] or self.head_bits:
            self.step()
        total = added(self.keeps[0], self.gots[0])
        return total if self.tail else total[0]


def per_device(
    tokens_in,
    segment,
    w_qkv,
    qv_bias,
    w_out,
    out_bias,
    ln1_gain,
    ln1_bias,
    w_up,
    up_bias,
    w_down,
    down_bias,
    ln2_gain,
    ln2_bias,
    cotangent,
):
    turn.last = []
    layers, width = w_qkv.shape[0], w_qkv.shape[1]
    part = w_qkv.shape[3] * w_qkv.shape[4]
    head_size = w_qkv.shape[4]
    tokens = tokens_in.shape[0]
    seq = segment.shape[1]
    dp, head = lax.axis_size("dp"), lax.axis_size("head")
    bits = dp.bit_length() - 1
    shard, group = lax.axis_index("head"), lax.axis_index("dp")
    halves = seq // tokens
    row, half = shard // halves, shard % halves
    upper = list(range(1, bits))

    edge = jnp.where(half == 0, tokens - HALO, 0)
    core = bit_of("dp", 0)

    own_w = w_qkv.transpose(0, 2, 3, 4, 1).reshape(layers, 3, part, width)
    own_first = own_w[0].reshape(3, dp, part // dp, width)
    piece = pick(own_first, group, 1).reshape(-1, width)
    rows_w = piece.shape[0]
    bias_own = qv_bias.reshape(1, layers * 2 * part)
    bias_own = jnp.pad(bias_own, ((0, 7), (0, width - bias_own.shape[1])))
    piece = jnp.concatenate([piece, bias_own])
    got = from_heads(piece)
    halo = swap(lax.dynamic_slice_in_dim(tokens_in, edge, HALO), "head", 1)
    biases = jnp.stack([other[rows_w, : layers * 2 * part] for other in [piece] + got])
    biases = biases.reshape(head, layers * 2, 1, part).astype(f32)
    members = jnp.arange(head)
    matches = (members[:, None] ^ shard) == members[None, :]
    bias_all = jnp.sum(jnp.where(matches[:, None, :, None], biases, 0.0), axis=0).reshape(layers, 2, -1)
    got = jnp.stack([other[:rows_w] for other in got]).reshape(head - 1, 3, part // dp, width)
    left, relative_left = grow(got[..., : width // 2], upper)
    right, relative_right = grow(got[..., width // 2 :], upper[::-1])
    both = jnp.stack([left, right])
    both = jnp.concatenate([both, swap(both, "dp", 1)], axis=1)
    relative = [order + [other ^ 1 for other in order] for order in (relative_left, relative_right)]
    place = jnp.stack([shard, group]).astype(jnp.int32)
    own_later = [own_w[k].reshape(3, 2, part // 2, width) for k in range(1, layers)]
    (low_t, halo_t), _ = flip([tokens_in, halo], [])
    w_first, pieces = assemble(relative, place, own_first, [both[0], both[1]], [pick(own, core, 1) for own in own_later])
    later_got = [from_heads_in_turn(value) for value in pieces]
    w_cats = [w_first.reshape(3 * head * part, width)]

    def later_weights(own, got):
        theirs = swap(got, "dp", 1)
        whole = assemble([[0], [1]], jnp.stack([shard, core]).astype(jnp.int32), own, [got[None], theirs[None]], [])[0]
        return whole.reshape(3 * head * part, width)

    labels = pick(segment, row, 0)
    own_labels = lax.dynamic_slice_in_dim(labels, half * tokens, tokens)
    halo_start = jnp.where(half == 0, tokens, tokens - HALO)
    halo_labels = lax.dynamic_slice_in_dim(labels, halo_start, HALO)
    blocks = tokens // BLK
    by_block = own_labels.reshape(blocks, BLK)
    least, most = by_block[:, :1], by_block[:, -1:]

    def count(flags):
        return jnp.sum(flags.astype(jnp.int32), axis=1)

    bounds = jnp.stack(
        [
            count(own_labels[None] < least) // BLK,
            (count(own_labels[None] <= most) + BLK - 1) // BLK,
            count(halo_labels[None] < least) // BLK,
            (count(halo_labels[None] <= most) + BLK - 1) // BLK,
        ],
        axis=1,
    )
    segq = jnp.concatenate([by_block, by_block], axis=1).reshape(blocks, 1, 2 * BLK)
    segk = jnp.concatenate([own_labels, halo_labels]).reshape(-1, 1)
    core_at = core.reshape(1).astype(jnp.int32)

    vecs = jnp.stack(
        [out_bias, ln1_gain, ln1_bias, down_bias, ln2_gain, ln2_bias, out_bias, out_bias], axis=1
    ).astype(f32)
    up_bias_wide = up_bias.astype(f32)

    hidden, low = tokens_in, tokens_in
    saved = []
    for layer_idx in range(layers):
        last = layer_idx == layers - 1
        w_cat = w_cats[layer_idx]
        zero = jnp.zeros((width,), f32)
        bias_q, bias_v = bias_all[layer_idx, 0], bias_all[layer_idx, 1]
        shift = jnp.concatenate([bias_q, zero, bias_v])
        factor = jnp.concatenate([zero + 0.125, zero + 1.0, zero + 1.0])
        qkv = ((nt(low, w_cat) + shift) * factor).astype(bf16)
        kvh = (nt(halo, w_cat[width:]) + shift[width:]).astype(bf16)
        (ctx, ctx_t, ctx_low, lse), _ = attend(bounds, segq, segk, qkv, kvh, (), ())
        fed, _ = feed(
            last, layer_idx, hidden, ctx, w_out, vecs[layer_idx], w_up, up_bias_wide[layer_idx : layer_idx + 1], w_down, (), ()
        )
        first_rows, first_t, active_t, slope, second_rows, after_low = fed[:6]
        saved.append((low_t, halo_t, qkv, kvh, ctx_t, ctx_low, lse, first_rows, first_t, active_t, slope, second_rows))
        if last:
            output = after_low
        else:
            low, hidden, low_t = after_low, fed[6], fed[7]
            halo = swap(lax.dynamic_slice_in_dim(low, edge, HALO), "head", 1)
            halo_t = halo.T
            w_cats.append(later_weights(own_later[layer_idx], collect(later_got[layer_idx])))

    grad_hidden = cotangent
    flights = []
    for layer_idx in reversed(range(layers)):
        low_t, halo_t, qkv, kvh, ctx_t, ctx_low, lse, first_rows, first_t, active_t, slope, second_rows = saved[layer_idx]
        w_cat = w_cats[layer_idx]
        (dz, du, da, dr, dc, sums, up_sum), _ = feed_back(
            layer_idx, grad_hidden, second_rows, first_rows, slope, w_down, w_up, w_out, vecs[layer_idx], (), ()
        )
        if flights:
            flights[1].step()
            flights[0].step()
        parts = du.shape[1] // width
        down_send, down_keep = grad_feed(core_at, active_t, dz, parts, dp, head, False)
        down_got = swap(down_send, "dp", 1)
        up_send, up_keep = grad_feed(core_at, first_t, du, parts, dp, head, True)
        up_got = swap(up_send, "dp", 1)
        fed = Flight([down_keep, up_keep], [down_got, up_got], False)
        if flights:
            flights[0].step()
        fed.step()
        (dqkv, dkvh, sums), _ = attend_back(bounds, segq, segk, qkv, kvh, ctx_t, lse, dc, sums, up_sum, (), ())
        part_halo = nn(dkvh, w_cat[width:]).astype(bf16)
        back = swap(part_halo, "head", 1)
        if flights:
            flights[1].step()
        (send, keep), _ = grad_heads(core_at, ctx_low, low_t, halo_t, da, dqkv, dkvh, sums, dp, (part_halo,), ())
        heads = Flight([keep], [swap(send, "dp", 1)], True)
        padded = lax.dynamic_update_slice(jnp.zeros((tokens, width), bf16), back, (edge, 0))
        grad_hidden = nn(dqkv, w_cat) + dr + padded.astype(f32)
        fed.step()
        if flights:
            flights[1].step()
            heads.step()
            flights[1].step()
            fed.step()
            heads.step()
            fed.step()
            heads.step()
            heads.step()
        flights = flights + [fed, heads]

    results = []
    for place in range(layers):
        fed, heads = flights[2 * place], flights[2 * place + 1]
        thin = width // (dp * head)
        total = fed.finish()
        out_down = total[0].reshape(-1, width)
        out_up = total[1].transpose(1, 0, 2).reshape(thin, -1)
        total = heads.finish()
        pieces = total[: 4 * part // TILE].reshape(4, part, BLK)
        out_out = pieces[3].reshape(width // BLK, -1, BLK)[:, :thin].transpose(1, 0, 2).reshape(thin, width)
        sums = total[4 * part // TILE :].transpose(1, 0, 2).reshape(TILE, 2, width).transpose(1, 0, 2)
        results.append((pieces[:3, :, : width // dp], out_out, out_up, out_down, sums.reshape(2 * TILE, width)))
    results = results[::-1]
    out_qkv, out_w_out, out_up, out_down, total = (jnp.stack([r[k] for r in results]) for k in range(5))
    out_qkv = out_qkv.reshape(layers, 3, part // head_size, head_size, -1).transpose(0, 4, 1, 2, 3)

    device = group * head + shard
    thin = width // (dp * head)
    mine = lax.dynamic_slice_in_dim(total[:, :6], device * thin, thin, axis=2)
    ups = total[:, 8 : 8 + up_bias.shape[1] // width].reshape(layers, -1)
    thick = ups.shape[1] // (dp * head)
    out_ups = lax.dynamic_slice_in_dim(ups, device * thick, thick, axis=1)
    qvs = total[:, 6:8].reshape(layers, 2, head, part // head_size, dp, head_size // dp)
    out_qv = pick(pick(qvs, shard, 2), group, 3)
    return (
        output,
        grad_hidden,
        out_qkv,
        out_qv,
        out_w_out,
        mine[:, 0],
        mine[:, 1],
        mine[:, 2],
        out_up,
        out_ups,
        out_down,
        mine[:, 3],
        mine[:, 4],
        mine[:, 5],
    )


def solution(mesh):
    return jax.shard_map(
        per_device,
        mesh=mesh,
        in_specs=(
            P(("dp", "head"), None),
            P("dp", None),
            P(None, None, None, "head", None),
            P(None, None, "head", None),
            P(),
            P(),
            P(),
            P(),
            P(),
            P(),
            P(),
            P(),
            P(),
            P(),
            P(("dp", "head"), None),
        ),
        out_specs=(
            P(("dp", "head"), None),
            P(("dp", "head"), None),
            P(None, "dp", None, "head", None),
            P(None, None, "head", "dp"),
            P(None, ("dp", "head"), None),
            P(None, ("dp", "head")),
            P(None, ("dp", "head")),
            P(None, ("dp", "head")),
            P(None, ("dp", "head"), None),
            P(None, ("dp", "head")),
            P(None, ("dp", "head"), None),
            P(None, ("dp", "head")),
            P(None, ("dp", "head")),
            P(None, ("dp", "head")),
        ),
        check_vma=False,
    )
```

```python
import functools

import jax
import jax.numpy as jnp
from jax import lax
from jax.experimental import pallas as pl
from jax.experimental.pallas import tpu as pltpu
from jax.sharding import PartitionSpec as P

norm_eps = 1e-06
masked_score = -1000000000.0
f32 = jnp.float32
bf16 = jnp.bfloat16

BLK = 128
TILE = 8
SCALE = 0.5
HALO = 384


def cost(microseconds):
    return pl.CostEstimate(flops=int(microseconds * SCALE * 1.15e9), bytes_accessed=1000, transcendentals=0)


def swap(value, axis, bit):
    size = lax.axis_size(axis)
    return lax.ppermute(value, axis, [(i, i ^ bit) for i in range(size)])


def bit_of(axis, place):
    return (lax.axis_index(axis) >> place) & 1


def pick(value, index, axis):
    return lax.dynamic_index_in_dim(value, index, axis, keepdims=False)


def add_low(*terms):
    total = terms[0].astype(f32)
    for term in terms[1:]:
        total = total + term.astype(f32)
    return total


def finish_head(slot):
    size = lax.axis_size("head")
    me = lax.axis_index("head")
    got = [swap(slot(me ^ step), "head", step) for step in range(1, size)]
    return add_low(slot(me), *got)


def head_masks():
    lane = lax.broadcasted_iota(jnp.int32, (BLK, BLK), 1)
    return lane < BLK // 2


def stack_heads(pair, low):
    zero = jnp.zeros_like(pair)
    return jnp.concatenate([jnp.where(low, pair, zero), jnp.where(low, zero, pair)], axis=0)


def nt(left, right):
    return lax.dot_general(left, right, (((1,), (1,)), ((), ())), preferred_element_type=f32)


def nn(left, right):
    return lax.dot_general(left, right, (((1,), (0,)), ((), ())), preferred_element_type=f32)


def each_block(step, low, high):
    def one(j, carry):
        step(j, 1)
        return carry

    lax.fori_loop(low, high, one, 0)


def all_blocks(step, low, high, most):
    for count in range(1, most + 1):

        @pl.when(high - low == count)
        def _(count=count):
            step(low, count)


def beside(ref, j, count, rows):
    return jnp.concatenate([ref[j + k, rows, :] for k in range(count)], axis=1)


def attend_kernel(pairs, own_blocks, halo_blocks, bounds, segq, segk, qkv, kvh, ctx, ctx_t, ctx_low, lse, vt, qs, top, total, acc):
    width = pairs * BLK
    low = head_masks()
    half = BLK // 2
    for j in range(own_blocks + halo_blocks):
        for p in range(pairs):
            if j < own_blocks:
                tile = qkv[j * BLK : (j + 1) * BLK, 2 * width + p * BLK : 2 * width + (p + 1) * BLK]
            else:
                at = j - own_blocks
                tile = kvh[at * BLK : (at + 1) * BLK, width + p * BLK : width + (p + 1) * BLK]
            vt[j, p * BLK : (p + 1) * BLK, :] = tile.T

    def q_block(i, carry):
        rows = pl.ds(pl.multiple_of(i * BLK, BLK), BLK)
        for p in range(pairs):
            qs[p] = stack_heads(qkv[rows, p * BLK : (p + 1) * BLK], low)
        top[...] = jnp.full(top.shape, -1e30, f32)
        total[...] = jnp.zeros(total.shape, f32)
        acc[...] = jnp.zeros(acc.shape, f32)
        labels = segq[i]

        def k_block(ref, first, base, j, count):
            here = pl.ds(pl.multiple_of(j * BLK, BLK), count * BLK)
            there = pl.ds(pl.multiple_of((base + j) * BLK, BLK), count * BLK)
            same = segk[there, :] == labels
            for p in range(pairs):
                keys = ref[here, first + p * BLK : first + (p + 1) * BLK]
                scores = jnp.where(same, nt(keys, qs[p]), masked_score)
                old = top[p : p + 1, :]
                new = jnp.maximum(old, jnp.max(scores, axis=0, keepdims=True))
                expo = jnp.exp(scores - new)
                scale = jnp.exp(old - new)
                top[p : p + 1, :] = new
                total[p : p + 1, :] = total[p : p + 1, :] * scale + jnp.sum(expo, axis=0, keepdims=True)
                weights = expo.astype(bf16)
                for h in range(2):
                    values = beside(vt, base + j, count, slice(p * BLK + h * half, p * BLK + (h + 1) * half))
                    part = slice(h * half, (h + 1) * half)
                    cols = slice(h * BLK, (h + 1) * BLK)
                    acc[p, part, :] = acc[p, part, :] * scale[:, cols] + nn(values, weights[:, cols])

        each_block(functools.partial(k_block, qkv, width, 0), bounds[i, 0], bounds[i, 1])
        each_block(functools.partial(k_block, kvh, 0, own_blocks), bounds[i, 2], bounds[i, 3])
        for p in range(pairs):
            inverse = 1.0 / total[p : p + 1, :]
            flat = jnp.concatenate(
                [acc[p, :half, :] * inverse[:, :BLK], acc[p, half:, :] * inverse[:, BLK:]], axis=0
            )
            rounded = flat.astype(bf16)
            ctx_t[p * BLK : (p + 1) * BLK, rows] = flat
            ctx_low[p * BLK : (p + 1) * BLK, rows] = rounded
            ctx[rows, p * BLK : (p + 1) * BLK] = rounded.T
        lse[i] = top[...] + jnp.log(total[...])
        return carry

    lax.fori_loop(0, own_blocks, q_block, 0)


def attend_back_kernel(
    pairs, own_blocks, halo_blocks,
    bounds, segq, segk, qkv, kvh, ctx_t, lse, dctx, norm_sums, up_sum,
    dqkv, dkvh, sums,
    kt, qs, cs, delta, dqt, dk, dv,
):
    width = pairs * BLK
    low = head_masks()
    half = BLK // 2
    blocks = own_blocks + halo_blocks
    for j in range(blocks):
        for p in range(pairs):
            if j < own_blocks:
                tile = qkv[j * BLK : (j + 1) * BLK, width + p * BLK : width + (p + 1) * BLK]
            else:
                at = j - own_blocks
                tile = kvh[at * BLK : (at + 1) * BLK, p * BLK : (p + 1) * BLK]
            kt[j, p * BLK : (p + 1) * BLK, :] = tile.T
    dk[...] = jnp.zeros(dk.shape, f32)
    dv[...] = jnp.zeros(dv.shape, f32)
    sums[...] = jnp.zeros(sums.shape, f32)
    sums[0:8, :] = norm_sums[...]
    for at in range(up_sum.shape[1] // width):
        sums[8 + at : 9 + at, :] = up_sum[:, at * width : (at + 1) * width]

    def q_block(i, carry):
        rows = pl.ds(pl.multiple_of(i * BLK, BLK), BLK)
        for p in range(pairs):
            cols = slice(p * BLK, (p + 1) * BLK)
            qs[p] = stack_heads(qkv[rows, cols], low)
            pull = dctx[rows, cols]
            cs[p] = stack_heads(pull, low)
            prod = pull.T.astype(f32) * ctx_t[cols, rows]
            delta[p : p + 1, :] = jnp.concatenate(
                [jnp.sum(prod[:half], axis=0, keepdims=True), jnp.sum(prod[half:], axis=0, keepdims=True)], axis=1
            )
        dqt[...] = jnp.zeros(dqt.shape, f32)
        labels = segq[i]

        def k_block(ref, first, base, j, count):
            here = pl.ds(pl.multiple_of(j * BLK, BLK), count * BLK)
            there = pl.ds(pl.multiple_of((base + j) * BLK, BLK), count * BLK)
            same = segk[there, :] == labels
            for p in range(pairs):
                cols = slice(p * BLK, (p + 1) * BLK)
                keys = ref[here, first + p * BLK : first + (p + 1) * BLK]
                values = ref[here, first + width + p * BLK : first + width + (p + 1) * BLK]
                scores = jnp.where(same, nt(keys, qs[p]), masked_score)
                probs = jnp.exp(scores - lse[i, p : p + 1, :])
                pulls = nt(values, cs[p])
                dscore = (probs * (pulls - delta[p : p + 1, :])).astype(bf16)
                dv[there, cols] += nn(probs.astype(bf16), cs[p])
                dk[there, cols] += nn(dscore, qs[p])
                for h in range(2):
                    part = slice(h * half, (h + 1) * half)
                    flip = beside(kt, base + j, count, slice(p * BLK + h * half, p * BLK + (h + 1) * half))
                    dqt[p, part, :] += nn(flip, dscore[:, h * BLK : (h + 1) * BLK])

        all_blocks(functools.partial(k_block, qkv, width, 0), bounds[i, 0], bounds[i, 1], own_blocks)
        all_blocks(functools.partial(k_block, kvh, 0, own_blocks), bounds[i, 2], bounds[i, 3], halo_blocks)
        for p in range(pairs):
            cols = slice(p * BLK, (p + 1) * BLK)
            grad = dqt[p].astype(bf16).T * jnp.asarray(0.125, bf16)
            dqkv[rows, cols] = grad
            sums[6:7, cols] += jnp.sum(grad.astype(f32), axis=0, keepdims=True)
        return carry

    lax.fori_loop(0, own_blocks, q_block, 0)
    for j in range(blocks):
        rows = slice(j * BLK, (j + 1) * BLK)
        grad_k = dk[rows, :].astype(bf16)
        grad_v = dv[rows, :].astype(bf16)
        if j < own_blocks:
            dqkv[rows, width : 2 * width] = grad_k
            dqkv[rows, 2 * width :] = grad_v
        else:
            back = slice((j - own_blocks) * BLK, (j - own_blocks + 1) * BLK)
            dkvh[back, :width] = grad_k
            dkvh[back, width:] = grad_v
        sums[7:8, :] += jnp.sum(grad_v.astype(f32), axis=0, keepdims=True)


def vmem_specs(count):
    return [pl.BlockSpec(memory_space=pltpu.VMEM)] * count


def any_specs(count):
    return [pl.BlockSpec(memory_space=pl.ANY)] * count


def ordered_call(kernel, args, waits, passes, out_shape, in_specs, out_specs, **options):
    waits, passes = tuple(waits) + tuple(turn.last), tuple(passes)
    given, made = len(args), len(out_shape)
    skipped = len(waits) + len(passes)

    def body(*refs):
        outs = given + skipped
        refs[outs + made][...] = jnp.zeros((8, BLK), f32)
        kernel(*refs[:given], *refs[outs : outs + made], *refs[outs + made + 1 + len(passes) :])

    out = pl.pallas_call(
        body,
        out_shape=tuple(out_shape)
        + (jax.ShapeDtypeStruct((8, BLK), f32),)
        + tuple(jax.ShapeDtypeStruct(p.shape, p.dtype) for p in passes),
        in_specs=list(in_specs) + any_specs(skipped),
        out_specs=tuple(out_specs) + (pl.BlockSpec((8, BLK), lambda *step: (0, 0)),) + tuple(any_specs(len(passes))),
        input_output_aliases={given + len(waits) + k: made + 1 + k for k in range(len(passes))},
        **options,
    )(*args, *waits, *passes)
    turn.last = [out[made]]
    return out[:made], out[made + 1 :]


class Turn:
    last = []


turn = Turn()


def attend(bounds, segq, segk, qkv, kvh, waits, passes):
    tokens, width3 = qkv.shape
    width = width3 // 3
    pairs, own_blocks, halo_blocks = width // BLK, tokens // BLK, kvh.shape[0] // BLK
    blocks = own_blocks + halo_blocks
    return ordered_call(
        functools.partial(attend_kernel, pairs, own_blocks, halo_blocks),
        (bounds, segq, segk, qkv, kvh),
        waits,
        passes,
        out_shape=(
            jax.ShapeDtypeStruct((tokens, width), bf16),
            jax.ShapeDtypeStruct((width, tokens), f32),
            jax.ShapeDtypeStruct((width, tokens), bf16),
            jax.ShapeDtypeStruct((own_blocks, 8, 2 * BLK), f32),
        ),
        in_specs=[pl.BlockSpec(memory_space=pltpu.SMEM)] + vmem_specs(4),
        out_specs=tuple(vmem_specs(4)),
        scratch_shapes=[
            pltpu.VMEM((blocks, width, BLK), bf16),
            pltpu.VMEM((pairs, 2 * BLK, BLK), bf16),
            pltpu.VMEM((8, 2 * BLK), f32),
            pltpu.VMEM((8, 2 * BLK), f32),
            pltpu.VMEM((pairs, BLK, BLK), f32),
        ],
        compiler_params=pltpu.CompilerParams(vmem_limit_bytes=16 * 2**20),
        cost_estimate=cost(9),
        name="attend",
    )


def attend_back(bounds, segq, segk, qkv, kvh, ctx_t, lse, dctx, norm_sums, up_sum, waits, passes):
    tokens, width3 = qkv.shape
    width = width3 // 3
    pairs, own_blocks, halo_blocks = width // BLK, tokens // BLK, kvh.shape[0] // BLK
    blocks = own_blocks + halo_blocks
    return ordered_call(
        functools.partial(attend_back_kernel, pairs, own_blocks, halo_blocks),
        (bounds, segq, segk, qkv, kvh, ctx_t, lse, dctx, norm_sums, up_sum),
        waits,
        passes,
        out_shape=(
            jax.ShapeDtypeStruct((tokens, width3), bf16),
            jax.ShapeDtypeStruct(kvh.shape, bf16),
            jax.ShapeDtypeStruct((16, width), f32),
        ),
        in_specs=[pl.BlockSpec(memory_space=pltpu.SMEM)] + vmem_specs(9),
        out_specs=tuple(vmem_specs(3)),
        scratch_shapes=[
            pltpu.VMEM((blocks, width, BLK), bf16),
            pltpu.VMEM((pairs, 2 * BLK, BLK), bf16),
            pltpu.VMEM((pairs, 2 * BLK, BLK), bf16),
            pltpu.VMEM((8, 2 * BLK), f32),
            pltpu.VMEM((pairs, BLK, BLK), f32),
            pltpu.VMEM((blocks * BLK, width), f32),
            pltpu.VMEM((blocks * BLK, width), f32),
        ],
        compiler_params=pltpu.CompilerParams(vmem_limit_bytes=24 * 2**20),
        cost_estimate=cost(21),
        name="attend_back",
    )


CHUNK = 1536
ROWS = 256


def normalized(rows):
    center = rows - jnp.mean(rows, axis=-1, keepdims=True)
    spread = jnp.mean(center * center, axis=-1, keepdims=True)
    scale = lax.rsqrt(spread + norm_eps)
    return center * scale, scale


def feed_kernel(last, tokens, hidden, ctx, w_out, vec, w_up, up_bias, w_down, *rest):
    if last:
        first_rows, first_t, active_t, slope, second_rows, low, low_rows, first, total = rest
    else:
        first_rows, first_t, active_t, slope, second_rows, low, after, low_t, low_rows, first, total = rest
    step = pl.program_id(0)
    tiles = [slice(at, at + BLK) for at in range(0, tokens, BLK)]
    passes = [slice(at, at + ROWS) for at in range(0, tokens, ROWS)]

    @pl.when(step == 0)
    def _():
        for rows in tiles:
            resid = hidden[rows, :].astype(f32) + (nn(ctx[rows, :], w_out[...]) + vec[0:1, :])
            first_rows[rows, :] = resid
            unit, _ = normalized(resid)
            value = unit * vec[1:2, :] + vec[2:3, :]
            first[rows, :] = value
            total[rows, :] = jnp.zeros_like(value)
            rounded = value.astype(bf16)
            low_rows[rows, :] = rounded
            first_t[:, rows] = rounded.T

    for rows in passes:
        upward = nn(low_rows[rows, :], w_up[...]) + up_bias[...]
        density = jnp.exp(-0.5 * upward * upward) * 0.3989422804014327
        below = 0.5 + 0.5 * lax.erf(upward * 0.7071067811865476)
        active = (upward * below).astype(bf16)
        slope[rows, :] = below + upward * density
        active_t[:, rows] = active.T
        total[rows, :] += nn(active, w_down[...])

    @pl.when(step == pl.num_programs(0) - 1)
    def _():
        for rows in tiles:
            resid = first[rows, :] + (total[rows, :] + vec[3:4, :])
            second_rows[rows, :] = resid
            unit, _ = normalized(resid)
            value = unit * vec[4:5, :] + vec[5:6, :]
            rounded = value.astype(bf16)
            low[rows, :] = rounded
            if not last:
                after[rows, :] = value
                low_t[:, rows] = rounded.T


def whole(shape):
    return pl.BlockSpec(shape, lambda step: (0,) * len(shape))


def feed(last, layer_idx, hidden, ctx, w_out, vec, w_up, up_bias, w_down, waits, passes):
    tokens, width = hidden.shape
    wide = w_up.shape[-1]
    rows = whole((tokens, width))
    shapes = [
        jax.ShapeDtypeStruct((tokens, width), f32),
        jax.ShapeDtypeStruct((width, tokens), bf16),
        jax.ShapeDtypeStruct((wide, tokens), bf16),
        jax.ShapeDtypeStruct((tokens, wide), f32),
        jax.ShapeDtypeStruct((tokens, width), f32),
        jax.ShapeDtypeStruct((tokens, width), bf16),
    ]
    specs = [
        rows,
        whole((width, tokens)),
        pl.BlockSpec((CHUNK, tokens), lambda step: (step, 0)),
        pl.BlockSpec((tokens, CHUNK), lambda step: (0, step)),
        rows,
        rows,
    ]
    if not last:
        shapes.append(jax.ShapeDtypeStruct((tokens, width), f32))
        shapes.append(jax.ShapeDtypeStruct((width, tokens), bf16))
        specs.append(rows)
        specs.append(whole((width, tokens)))
    return ordered_call(
        functools.partial(feed_kernel, last, tokens),
        (hidden, ctx, w_out, vec, w_up, up_bias, w_down),
        waits,
        passes,
        grid=(wide // CHUNK,),
        out_shape=tuple(shapes),
        in_specs=[
            rows,
            rows,
            pl.BlockSpec((None, width, width), lambda step: (layer_idx, 0, 0)),
            whole(vec.shape),
            pl.BlockSpec((None, width, CHUNK), lambda step: (layer_idx, 0, step)),
            pl.BlockSpec((1, CHUNK), lambda step: (0, step)),
            pl.BlockSpec((None, CHUNK, width), lambda step: (layer_idx, step, 0)),
        ],
        out_specs=tuple(specs),
        scratch_shapes=[
            pltpu.VMEM((tokens, width), bf16),
            pltpu.VMEM((tokens, width), f32),
            pltpu.VMEM((tokens, width), f32),
        ],
        compiler_params=pltpu.CompilerParams(vmem_limit_bytes=48 * 2**20),
        cost_estimate=cost(15),
        name="feed",
    )


def norm_back(grad, gain, rows):
    unit, scale = normalized(rows)
    lifted = grad * gain
    first = jnp.mean(lifted, axis=-1, keepdims=True)
    second = jnp.mean(lifted * unit, axis=-1, keepdims=True)
    return scale * (lifted - first - unit * second), unit


def over_rows(value):
    return jnp.sum(value, axis=0, keepdims=True)


def feed_back_kernel(
    tokens, grad, second_rows, first_rows, slope, w_down, w_up, w_out, vec,
    dz, du, da, dr, dc, sums, up_sum, dr_two, total,
):
    step = pl.program_id(0)
    tiles = [slice(at, at + BLK) for at in range(0, tokens, BLK)]
    passes = [slice(at, at + ROWS) for at in range(0, tokens, ROWS)]

    @pl.when(step == 0)
    def _():
        sums[...] = jnp.zeros(sums.shape, f32)
        for rows in tiles:
            pull = grad[rows, :].astype(f32)
            value, unit = norm_back(pull, vec[4:5, :], second_rows[rows, :])
            dr_two[rows, :] = value
            total[rows, :] = jnp.zeros_like(value)
            rounded = value.astype(bf16)
            dz[rows, :] = rounded
            sums[3:4, :] += over_rows(rounded.astype(f32))
            sums[4:5, :] += over_rows(pull * unit)
            sums[5:6, :] += over_rows(pull)

    up_sum[...] = jnp.zeros(up_sum.shape, f32)
    for rows in passes:
        pull = (nt(dz[rows, :], w_down[...]) * slope[rows, :]).astype(bf16)
        du[rows, :] = pull
        up_sum[...] += over_rows(pull.astype(f32))
        total[rows, :] += nt(pull, w_up[...])

    @pl.when(step == pl.num_programs(0) - 1)
    def _():
        for rows in tiles:
            pull = total[rows, :] + dr_two[rows, :]
            value, unit = norm_back(pull, vec[1:2, :], first_rows[rows, :])
            dr[rows, :] = value
            rounded = value.astype(bf16)
            da[rows, :] = rounded
            sums[0:1, :] += over_rows(rounded.astype(f32))
            sums[1:2, :] += over_rows(pull * unit)
            sums[2:3, :] += over_rows(pull)
            dc[rows, :] = nt(rounded, w_out[...]).astype(bf16)


def feed_back(layer_idx, grad, second_rows, first_rows, slope, w_down, w_up, w_out, vec, waits, passes):
    tokens, width = grad.shape
    wide = w_up.shape[-1]
    rows = whole((tokens, width))
    return ordered_call(
        functools.partial(feed_back_kernel, tokens),
        (grad, second_rows, first_rows, slope, w_down, w_up, w_out, vec),
        waits,
        passes,
        grid=(wide // CHUNK,),
        out_shape=(
            jax.ShapeDtypeStruct((tokens, width), bf16),
            jax.ShapeDtypeStruct((tokens, wide), bf16),
            jax.ShapeDtypeStruct((tokens, width), bf16),
            jax.ShapeDtypeStruct((tokens, width), f32),
            jax.ShapeDtypeStruct((tokens, width), bf16),
            jax.ShapeDtypeStruct((8, width), f32),
            jax.ShapeDtypeStruct((1, wide), f32),
        ),
        in_specs=[
            rows,
            rows,
            rows,
            pl.BlockSpec((tokens, CHUNK), lambda step: (0, step)),
            pl.BlockSpec((None, CHUNK, width), lambda step: (layer_idx, step, 0)),
            pl.BlockSpec((None, width, CHUNK), lambda step: (layer_idx, 0, step)),
            pl.BlockSpec((None, width, width), lambda step: (layer_idx, 0, 0)),
            whole(vec.shape),
        ],
        out_specs=(
            rows,
            pl.BlockSpec((tokens, CHUNK), lambda step: (0, step)),
            rows,
            rows,
            rows,
            whole((8, width)),
            pl.BlockSpec((1, CHUNK), lambda step: (0, step)),
        ),
        scratch_shapes=[pltpu.VMEM((tokens, width), f32), pltpu.VMEM((tokens, width), f32)],
        compiler_params=pltpu.CompilerParams(vmem_limit_bytes=48 * 2**20),
        cost_estimate=cost(17),
        name="feed_back",
    )


def grad_down_kernel(core, active_t, dz, send, keep):
    groups, head, parts, thin, width = send.shape
    mine = core[0]
    for which, out in ((1 - mine, send), (mine, keep)):
        for group in range(groups):
            value = nn(active_t[2 * group + which], dz[...])
            for shard in range(head):
                for at in range(parts):
                    here = (shard * parts + at) * thin
                    out[group, shard, at] = value[here : here + thin].astype(bf16)


def grad_up_kernel(core, first_t, du, send, keep, lhs):
    groups, head, parts, thin, width = send.shape
    rows = head * thin
    mine = core[0]
    for which, out in ((1 - mine, send), (mine, keep)):
        if rows % 16 == 0:
            for group in range(groups):
                lhs[group * rows : (group + 1) * rows, :] = first_t[2 * group + which]
        for at in range(parts):
            pulls = du[:, at * width : (at + 1) * width]
            if rows % 16 == 0:
                value = nn(lhs[...], pulls)
                values = [value[group * rows : (group + 1) * rows] for group in range(groups)]
            else:
                values = [nn(first_t[2 * group + which], pulls) for group in range(groups)]
            for group in range(groups):
                for shard in range(head):
                    out[group, shard, at] = values[group][shard * thin : (shard + 1) * thin].astype(bf16)


def grad_feed(core, left_t, right, parts, devices, head, scratch):
    rows, tokens = left_t.shape
    thin = rows // devices // head // (1 if scratch else parts)
    width = right.shape[1] // (parts if scratch else 1)
    out = jax.ShapeDtypeStruct((devices // 2, head, parts, thin, width), bf16)
    halves, _ = ordered_call(
        grad_up_kernel if scratch else grad_down_kernel,
        (core, left_t.reshape(devices, rows // devices, tokens), right),
        (),
        (),
        out_shape=(out, out),
        in_specs=[pl.BlockSpec(memory_space=pltpu.SMEM)] + vmem_specs(2),
        out_specs=tuple(vmem_specs(2)),
        scratch_shapes=[pltpu.VMEM((rows // 2, tokens), bf16)] if scratch else [],
        compiler_params=pltpu.CompilerParams(vmem_limit_bytes=18 * 2**20),
        cost_estimate=cost(5),
        name="grad_up" if scratch else "grad_down",
    )
    return halves


def grad_heads_kernel(core, ctx_t, low_t, halo_t, da, dqkv, dkvh, sums, send, keep, one, two, three):
    groups, thin = ctx_t.shape[0] // 2, ctx_t.shape[1]
    width = send.shape[2] // 4
    high = thin // TILE
    for r in range(sums.shape[0] // TILE):
        value = sums[r * TILE : (r + 1) * TILE, :].astype(bf16)
        for out in (send, keep):
            out[groups * high, :, r * width : (r + 1) * width] = value
    mine = core[0]
    for which, out in ((1 - mine, send), (mine, keep)):
        if thin % 16 == 0:
            for group in range(groups):
                here = slice(group * thin, (group + 1) * thin)
                one[here, :] = ctx_t[2 * group + which]
                two[here, :] = low_t[2 * group + which]
                three[here, :] = halo_t[2 * group + which]
            parts = [(range(groups), one, two, three)]
        else:
            parts = [
                ([group], ctx_t.at[2 * group + which], low_t.at[2 * group + which], halo_t.at[2 * group + which])
                for group in range(groups)
            ]
        for members, left_one, left_two, left_three in parts:
            for at in range(0, 4 * width, width):
                if at < width:
                    value = nn(left_one[...], da[...])
                else:
                    value = nn(left_two[...], dqkv[:, at - width : at])
                    if at >= 2 * width:
                        value = value + nn(left_three[...], dkvh[:, at - 2 * width : at - width])
                for place, group in enumerate(members):
                    here = value[place * thin : (place + 1) * thin].reshape(high, TILE, width)
                    out[group * high : (group + 1) * high, :, at : at + width] = here.astype(bf16)


def grad_heads(core, ctx_t, low_t, halo_t, da, dqkv, dkvh, sums, devices, waits, passes):
    tokens, width = da.shape
    thin = width // devices
    out = jax.ShapeDtypeStruct((devices // 2 * thin // TILE + 1, TILE, 4 * width), bf16)
    extent = halo_t.shape[1]
    return ordered_call(
        grad_heads_kernel,
        (
            core,
            ctx_t.reshape(devices, thin, tokens),
            low_t.reshape(devices, thin, tokens),
            halo_t.reshape(devices, thin, extent),
            da,
            dqkv,
            dkvh,
            sums,
        ),
        waits,
        passes,
        out_shape=(out, out),
        in_specs=[pl.BlockSpec(memory_space=pltpu.SMEM)] + vmem_specs(7),
        out_specs=tuple(vmem_specs(2)),
        scratch_shapes=[
            pltpu.VMEM((width // 2, tokens), bf16),
            pltpu.VMEM((width // 2, tokens), bf16),
            pltpu.VMEM((width // 2, extent), bf16),
        ],
        compiler_params=pltpu.CompilerParams(vmem_limit_bytes=20 * 2**20),
        cost_estimate=cost(8),
        name="grad_heads",
    )


def assemble_kernel(relative, place, own, *refs):
    *refs, out = refs
    shard, group = place[0], place[1]
    kinds = own.shape[0]
    out[:, pl.ds(shard, 1)] = own[...].reshape(kinds, 1, *own.shape[1:])
    lane = 0
    for ref, order in zip(refs, relative):
        lanes = slice(lane, lane + ref.shape[-1])
        lane = lanes.stop % own.shape[-1]
        for at, change in enumerate(order):
            for step in range(ref.shape[1]):
                for kind in range(kinds):
                    out[kind, shard ^ (step + 1), group ^ change, :, lanes] = ref[at, step, kind]


def assemble(relative, place, own, refs, passes):
    head = lax.axis_size("head")
    (out,), passed = ordered_call(
        functools.partial(assemble_kernel, relative),
        (place, own, *refs),
        (),
        passes,
        out_shape=(jax.ShapeDtypeStruct((own.shape[0], head) + own.shape[1:], bf16),),
        in_specs=[pl.BlockSpec(memory_space=pltpu.SMEM)] + vmem_specs(1 + len(refs)),
        out_specs=vmem_specs(1),
        compiler_params=pltpu.CompilerParams(vmem_limit_bytes=16 * 2**20),
        cost_estimate=cost(1.5),
        name="assemble",
    )
    return out, passed


def grow(value, order):
    value, relative = value[None], [0]
    for place in order:
        value = jnp.concatenate([value, swap(value, "dp", 1 << place)], axis=0)
        relative = relative + [other ^ (1 << place) for other in relative]
    return value, relative


def flip_kernel(count, shard, biases, *refs):
    for source, target in zip(refs[:count], refs[count : 2 * count]):
        for at in range(0, source.shape[0], BLK):
            target[:, at : at + BLK] = source[at : at + BLK, :].T
    shifts = refs[2 * count]
    members, _, width = biases.shape
    layers, part = shifts.shape[0], width // members
    shifts[...] = jnp.zeros(shifts.shape, f32)
    rows = [biases[step].astype(f32) for step in range(members)]
    for member in range(members):
        value = jnp.zeros((1, width), f32)
        for step, row in enumerate(rows):
            value = jnp.where((shard[0] ^ step) == member, row, value)
        for layer_idx in range(layers):
            for at, kind in ((0, 0), (1, 2)):
                here = (2 * layer_idx + at) * part
                there = kind * width + member * part
                shifts[layer_idx, :, there : there + part] = value[:, here : here + part]


def flip(values, shard, biases, layers):
    width = biases.shape[2]
    shapes = [jax.ShapeDtypeStruct(v.shape[::-1], v.dtype) for v in values]
    return ordered_call(
        functools.partial(flip_kernel, len(values)),
        (shard, biases, *values),
        (),
        (),
        out_shape=shapes + [jax.ShapeDtypeStruct((layers, 1, 3 * width), f32)],
        in_specs=[pl.BlockSpec(memory_space=pltpu.SMEM)] + vmem_specs(1 + len(values)),
        out_specs=vmem_specs(1 + len(values)),
        compiler_params=pltpu.CompilerParams(vmem_limit_bytes=8 * 2**20),
        cost_estimate=cost(1.5),
        name="flip",
    )


def collect_kernel(*refs):
    *parts, out = refs
    for k, ref in enumerate(parts):
        out[k] = ref[...]


def collect(values):
    (out,), _ = ordered_call(
        collect_kernel,
        values,
        (),
        (),
        out_shape=(jax.ShapeDtypeStruct((len(values),) + values[0].shape, values[0].dtype),),
        in_specs=vmem_specs(len(values)),
        out_specs=vmem_specs(1),
        compiler_params=pltpu.CompilerParams(vmem_limit_bytes=8 * 2**20),
        cost_estimate=cost(1.4),
        name="collect",
    )
    return out


def from_heads_in_turn(piece):
    got = [swap(piece, "head", 1)]
    step = 2
    while step < lax.axis_size("head"):
        far = [swap(value, "head", step) for value in [piece]]
        for value in far:
            got = got + [value, swap(value, "head", 1)]
        step *= 2
    return got


def from_heads(piece):
    return [swap(piece, "head", step) for step in range(1, lax.axis_size("head"))]


def added(keep, got):
    return keep.astype(f32) + got.astype(f32)


def advance_kernel(counts, size, tail, sources, scalars, *refs):
    core, mine = scalars[0], scalars[1]
    keeps, gots, (send, out) = refs[:sources], refs[sources : 2 * sources], refs[2 * sources :]
    blocks = (keeps[0].shape[0] - tail) // size
    for target, which in ((send, 1 - mine), (out, mine)):
        for k in range(blocks // 2):
            spots = [2 * (k // after) * after + k % after for after in counts]
            at = jnp.where(core == 0, spots[0] + which * counts[0], spots[1] + which * counts[1])
            here = pl.ds(at * size, size)
            for source, (keep, got) in enumerate(zip(keeps, gots)):
                value = added(keep[here], got[here]).astype(bf16)
                if sources > 1:
                    target[k * size : (k + 1) * size, source] = value
                else:
                    target[k * size : (k + 1) * size] = value
        if tail:
            value = added(keeps[0][blocks * size :], gots[0][blocks * size :]).astype(bf16)
            target[blocks // 2 * size :] = value


def turn_heads_kernel(head, scalars, keep, got, send, out):
    mine = scalars[1]
    tiles, _, columns = keep.shape
    rows, width = (tiles - 1) * TILE, columns // 4
    held = added(keep[: tiles - 1], got[: tiles - 1]).reshape(rows, columns)
    part, thin = width // head, rows // head
    kinds = []
    if rows < BLK:
        filler = jnp.zeros((BLK - rows, width), f32)
    for kind in range(1, 4):
        value = held[:, kind * width : (kind + 1) * width]
        value = jnp.concatenate([value, filler], axis=0) if rows < BLK else value
        kinds.append(value.T)
    high = part // (width // BLK)
    count = part // TILE
    for shard in range(head):
        pieces = [value[shard * part : (shard + 1) * part] for value in kinds]
        own = held[shard * thin : (shard + 1) * thin, :width]
        own = jnp.concatenate([own, jnp.zeros((high - thin, width), f32)], axis=0)
        pieces.append(jnp.concatenate([own[:, at : at + BLK] for at in range(0, width, BLK)], axis=0))
        for chosen, target in ((1 - mine, send), (mine, out)):

            @pl.when(chosen == shard % 2)
            def _(target=target, pieces=pieces, shard=shard):
                for kind, piece in enumerate(pieces):
                    at = (shard // 2 * 4 + kind) * count
                    target[at : at + count] = piece.reshape(count, TILE, BLK).astype(bf16)

    last = added(keep[tiles - 1], got[tiles - 1])
    for target in (send, out):
        for k in range(2 * width // BLK):
            target[head // 2 * 4 * count + k] = last[:, k * BLK : (k + 1) * BLK].astype(bf16)


class Flight:
    def __init__(self, keeps, gots, turned):
        dp, head = lax.axis_size("dp"), lax.axis_size("head")
        bits = dp.bit_length() - 1
        upper = list(range(1, bits))
        self.orders = [list(upper), list(upper)[::-1]]
        self.left = [upper[::-1], upper[::-1]]
        self.head_bits = list(range(head.bit_length() - 1))
        self.turned = turned
        self.tail, self.size = 0, 1
        if turned:
            self.tail, self.size = 1, (keeps[0].shape[0] - 1) // (dp // 2)
        else:
            shape = (keeps[0].shape[0] * keeps[0].shape[1],) + keeps[0].shape[2:]
            keeps, gots = [k.reshape(shape) for k in keeps], [g.reshape(shape) for g in gots]
        self.keeps, self.gots = list(keeps), list(gots)

    def step(self, waits=(), passes=()):
        blocks = (self.keeps[0].shape[0] - self.tail) // self.size
        sources = len(self.keeps)
        core = bit_of("dp", 0)
        rest = self.keeps[0].shape[1:]
        if sources > 1:
            rest = (sources,) + rest
        devices = lax.axis_size("dp")
        counts = [1, 1]
        if self.orders[0]:
            places = [order.pop(0) for order in self.orders]
            counts = []
            for left, place in zip(self.left, places):
                axis = left.index(place)
                left.remove(place)
                counts.append((blocks // 2) >> axis)
            mine = jnp.where(core == 0, bit_of("dp", places[0]), bit_of("dp", places[1]))
            axis_name, pairs = "dp", [(i, i ^ (1 << places[i & 1])) for i in range(devices)]
        else:
            place = self.head_bits.pop(0)
            mine = bit_of("head", place)
            head = lax.axis_size("head")
            axis_name, pairs = "head", [(i, i ^ (1 << place)) for i in range(head)]
        if axis_name == "head" and self.turned:
            width = rest[1] // 4
            self.turned = False
            self.size, self.tail = 4 * (width // head) // TILE, 2 * width // BLK
            out_shape = (head // 2 * self.size + self.tail, TILE, BLK)
            kernel = functools.partial(turn_heads_kernel, head)
        else:
            out_shape = (blocks // 2 * self.size + self.tail,) + rest
            kernel = functools.partial(advance_kernel, counts, self.size, self.tail, sources)
        out = jax.ShapeDtypeStruct(out_shape, bf16)
        (send, keep), passed = ordered_call(
            kernel,
            (jnp.stack([core, mine]).astype(jnp.int32), *self.keeps, *self.gots),
            waits,
            passes,
            out_shape=[out] * 2,
            in_specs=[pl.BlockSpec(memory_space=pltpu.SMEM)] + vmem_specs(2 * sources),
            out_specs=vmem_specs(2),
            compiler_params=pltpu.CompilerParams(vmem_limit_bytes=20 * 2**20),
            cost_estimate=cost(1 + 2e-6 * out.size),
            name="advance",
        )
        self.keeps, self.gots = [keep], [lax.ppermute(send, axis_name, pairs)]
        return passed

    def finish(self):
        while self.orders[0] or self.head_bits:
            self.step()
        total = added(self.keeps[0], self.gots[0])
        return total if self.tail else total[0]


def per_device(
    tokens_in,
    segment,
    w_qkv,
    qv_bias,
    w_out,
    out_bias,
    ln1_gain,
    ln1_bias,
    w_up,
    up_bias,
    w_down,
    down_bias,
    ln2_gain,
    ln2_bias,
    cotangent,
):
    turn.last = []
    layers, width = w_qkv.shape[0], w_qkv.shape[1]
    part = w_qkv.shape[3] * w_qkv.shape[4]
    head_size = w_qkv.shape[4]
    tokens = tokens_in.shape[0]
    seq = segment.shape[1]
    dp, head = lax.axis_size("dp"), lax.axis_size("head")
    bits = dp.bit_length() - 1
    shard, group = lax.axis_index("head"), lax.axis_index("dp")
    halves = seq // tokens
    row, half = shard // halves, shard % halves
    upper = list(range(1, bits))

    edge = jnp.where(half == 0, tokens - HALO, 0)
    core = bit_of("dp", 0)

    own_w = w_qkv.transpose(0, 2, 3, 4, 1).reshape(layers, 3, part, width)
    own_first = own_w[0].reshape(3, dp, part // dp, width)
    piece = pick(own_first, group, 1).reshape(-1, width)
    rows_w = piece.shape[0]
    bias_own = qv_bias.reshape(1, layers * 2 * part)
    bias_own = jnp.pad(bias_own, ((0, 7), (0, width - bias_own.shape[1])))
    piece = jnp.concatenate([piece, bias_own])
    got = from_heads(piece)
    halo = swap(lax.dynamic_slice_in_dim(tokens_in, edge, HALO), "head", 1)
    biases = jnp.stack([other[rows_w : rows_w + 1] for other in [piece] + got])
    got = jnp.stack([other[:rows_w] for other in got]).reshape(head - 1, 3, part // dp, width)
    left, relative_left = grow(got[..., : width // 2], upper)
    right, relative_right = grow(got[..., width // 2 :], upper[::-1])
    both = jnp.stack([left, right])
    both = jnp.concatenate([both, swap(both, "dp", 1)], axis=1)
    relative = [order + [other ^ 1 for other in order] for order in (relative_left, relative_right)]
    place = jnp.stack([shard, group]).astype(jnp.int32)
    own_later = [own_w[k].reshape(3, 2, part // 2, width) for k in range(1, layers)]
    (low_t, halo_t, shifts), _ = flip([tokens_in, halo], shard.reshape(1).astype(jnp.int32), biases, layers)
    w_first, pieces = assemble(relative, place, own_first, [both[0], both[1]], [pick(own, core, 1) for own in own_later])
    later_got = [from_heads_in_turn(value) for value in pieces]
    w_cats = [w_first.reshape(3 * head * part, width)]

    def later_weights(own, got):
        theirs = swap(got, "dp", 1)
        whole = assemble([[0], [1]], jnp.stack([shard, core]).astype(jnp.int32), own, [got[None], theirs[None]], [])[0]
        return whole.reshape(3 * head * part, width)

    labels = pick(segment, row, 0)
    own_labels = lax.dynamic_slice_in_dim(labels, half * tokens, tokens)
    halo_start = jnp.where(half == 0, tokens, tokens - HALO)
    halo_labels = lax.dynamic_slice_in_dim(labels, halo_start, HALO)
    blocks = tokens // BLK
    by_block = own_labels.reshape(blocks, BLK)
    least, most = by_block[:, :1], by_block[:, -1:]

    def count(flags):
        return jnp.sum(flags.astype(jnp.int32), axis=1)

    bounds = jnp.stack(
        [
            count(own_labels[None] < least) // BLK,
            (count(own_labels[None] <= most) + BLK - 1) // BLK,
            count(halo_labels[None] < least) // BLK,
            (count(halo_labels[None] <= most) + BLK - 1) // BLK,
        ],
        axis=1,
    )
    segq = jnp.concatenate([by_block, by_block], axis=1).reshape(blocks, 1, 2 * BLK)
    segk = jnp.concatenate([own_labels, halo_labels]).reshape(-1, 1)
    core_at = core.reshape(1).astype(jnp.int32)

    vecs = jnp.stack(
        [out_bias, ln1_gain, ln1_bias, down_bias, ln2_gain, ln2_bias, out_bias, out_bias], axis=1
    ).astype(f32)
    up_bias_wide = up_bias.astype(f32)

    hidden, low = tokens_in, tokens_in
    saved = []
    for layer_idx in range(layers):
        last = layer_idx == layers - 1
        w_cat = w_cats[layer_idx]
        shift = shifts[layer_idx]
        factor = jnp.where(jnp.arange(3 * width) < width, 0.125, 1.0).astype(f32)
        qkv = ((nt(low, w_cat) + shift) * factor).astype(bf16)
        kvh = (nt(halo, w_cat[width:]) + shift[:, width:]).astype(bf16)
        (ctx, ctx_t, ctx_low, lse), _ = attend(bounds, segq, segk, qkv, kvh, (), ())
        fed, _ = feed(
            last, layer_idx, hidden, ctx, w_out, vecs[layer_idx], w_up, up_bias_wide[layer_idx : layer_idx + 1], w_down, (), ()
        )
        first_rows, first_t, active_t, slope, second_rows, after_low = fed[:6]
        saved.append((low_t, halo_t, qkv, kvh, ctx_t, ctx_low, lse, first_rows, first_t, active_t, slope, second_rows))
        if last:
            output = after_low
        else:
            low, hidden, low_t = after_low, fed[6], fed[7]
            halo = swap(lax.dynamic_slice_in_dim(low, edge, HALO), "head", 1)
            halo_t = halo.T
            w_cats.append(later_weights(own_later[layer_idx], collect(later_got[layer_idx])))

    grad_hidden = cotangent
    flights = []
    for layer_idx in reversed(range(layers)):
        low_t, halo_t, qkv, kvh, ctx_t, ctx_low, lse, first_rows, first_t, active_t, slope, second_rows = saved[layer_idx]
        w_cat = w_cats[layer_idx]
        (dz, du, da, dr, dc, sums, up_sum), _ = feed_back(
            layer_idx, grad_hidden, second_rows, first_rows, slope, w_down, w_up, w_out, vecs[layer_idx], (), ()
        )
        if flights:
            flights[1].step()
            flights[0].step()
        parts = du.shape[1] // width
        down_send, down_keep = grad_feed(core_at, active_t, dz, parts, dp, head, False)
        down_got = swap(down_send, "dp", 1)
        up_send, up_keep = grad_feed(core_at, first_t, du, parts, dp, head, True)
        up_got = swap(up_send, "dp", 1)
        fed = Flight([down_keep, up_keep], [down_got, up_got], False)
        if flights:
            flights[0].step()
        fed.step()
        (dqkv, dkvh, sums), _ = attend_back(bounds, segq, segk, qkv, kvh, ctx_t, lse, dc, sums, up_sum, (), ())
        part_halo = nn(dkvh, w_cat[width:]).astype(bf16)
        back = swap(part_halo, "head", 1)
        if flights:
            flights[1].step()
        (send, keep), _ = grad_heads(core_at, ctx_low, low_t, halo_t, da, dqkv, dkvh, sums, dp, (part_halo,), ())
        heads = Flight([keep], [swap(send, "dp", 1)], True)
        padded = lax.dynamic_update_slice(jnp.zeros((tokens, width), bf16), back, (edge, 0))
        grad_hidden = nn(dqkv, w_cat) + dr + padded.astype(f32)
        fed.step()
        if flights:
            flights[1].step()
            heads.step()
            flights[1].step()
            fed.step()
            heads.step()
            fed.step()
            heads.step()
            heads.step()
        flights = flights + [fed, heads]

    results = []
    for place in range(layers):
        fed, heads = flights[2 * place], flights[2 * place + 1]
        thin = width // (dp * head)
        total = fed.finish()
        out_down = total[0].reshape(-1, width)
        out_up = total[1].transpose(1, 0, 2).reshape(thin, -1)
        total = heads.finish()
        pieces = total[: 4 * part // TILE].reshape(4, part, BLK)
        out_out = pieces[3].reshape(width // BLK, -1, BLK)[:, :thin].transpose(1, 0, 2).reshape(thin, width)
        sums = total[4 * part // TILE :].transpose(1, 0, 2).reshape(TILE, 2, width).transpose(1, 0, 2)
        results.append((pieces[:3, :, : width // dp], out_out, out_up, out_down, sums.reshape(2 * TILE, width)))
    results = results[::-1]
    out_qkv, out_w_out, out_up, out_down, total = (jnp.stack([r[k] for r in results]) for k in range(5))
    out_qkv = out_qkv.reshape(layers, 3, part // head_size, head_size, -1).transpose(0, 4, 1, 2, 3)

    device = group * head + shard
    thin = width // (dp * head)
    mine = lax.dynamic_slice_in_dim(total[:, :6], device * thin, thin, axis=2)
    ups = total[:, 8 : 8 + up_bias.shape[1] // width].reshape(layers, -1)
    thick = ups.shape[1] // (dp * head)
    out_ups = lax.dynamic_slice_in_dim(ups, device * thick, thick, axis=1)
    qvs = total[:, 6:8].reshape(layers, 2, head, part // head_size, dp, head_size // dp)
    out_qv = pick(pick(qvs, shard, 2), group, 3)
    return (
        output,
        grad_hidden,
        out_qkv,
        out_qv,
        out_w_out,
        mine[:, 0],
        mine[:, 1],
        mine[:, 2],
        out_up,
        out_ups,
        out_down,
        mine[:, 3],
        mine[:, 4],
        mine[:, 5],
    )


def solution(mesh):
    return jax.shard_map(
        per_device,
        mesh=mesh,
        in_specs=(
            P(("dp", "head"), None),
            P("dp", None),
            P(None, None, None, "head", None),
            P(None, None, "head", None),
            P(),
            P(),
            P(),
            P(),
            P(),
            P(),
            P(),
            P(),
            P(),
            P(),
            P(("dp", "head"), None),
        ),
        out_specs=(
            P(("dp", "head"), None),
            P(("dp", "head"), None),
            P(None, "dp", None, "head", None),
            P(None, None, "head", "dp"),
            P(None, ("dp", "head"), None),
            P(None, ("dp", "head")),
            P(None, ("dp", "head")),
            P(None, ("dp", "head")),
            P(None, ("dp", "head"), None),
            P(None, ("dp", "head")),
            P(None, ("dp", "head"), None),
            P(None, ("dp", "head")),
            P(None, ("dp", "head")),
            P(None, ("dp", "head")),
        ),
        check_vma=False,
    )
```

```python
import functools

import jax
import jax.numpy as jnp
from jax import lax
from jax.experimental import pallas as pl
from jax.experimental.pallas import tpu as pltpu
from jax.sharding import PartitionSpec as P

norm_eps = 1e-06
masked_score = -1000000000.0
f32 = jnp.float32
bf16 = jnp.bfloat16

BLK = 128
TILE = 8
SCALE = 0.5
HALO = 384


def cost(microseconds):
    return pl.CostEstimate(flops=int(microseconds * SCALE * 1.15e9), bytes_accessed=1000, transcendentals=0)


def swap(value, axis, bit):
    size = lax.axis_size(axis)
    return lax.ppermute(value, axis, [(i, i ^ bit) for i in range(size)])


def bit_of(axis, place):
    return (lax.axis_index(axis) >> place) & 1


def pick(value, index, axis):
    return lax.dynamic_index_in_dim(value, index, axis, keepdims=False)


def add_low(*terms):
    total = terms[0].astype(f32)
    for term in terms[1:]:
        total = total + term.astype(f32)
    return total


def finish_head(slot):
    size = lax.axis_size("head")
    me = lax.axis_index("head")
    got = [swap(slot(me ^ step), "head", step) for step in range(1, size)]
    return add_low(slot(me), *got)


def head_masks():
    lane = lax.broadcasted_iota(jnp.int32, (BLK, BLK), 1)
    return lane < BLK // 2


def stack_heads(pair, low):
    zero = jnp.zeros_like(pair)
    return jnp.concatenate([jnp.where(low, pair, zero), jnp.where(low, zero, pair)], axis=0)


def nt(left, right):
    return lax.dot_general(left, right, (((1,), (1,)), ((), ())), preferred_element_type=f32)


def nn(left, right):
    return lax.dot_general(left, right, (((1,), (0,)), ((), ())), preferred_element_type=f32)


def each_block(step, low, high):
    def one(j, carry):
        step(j, 1)
        return carry

    lax.fori_loop(low, high, one, 0)


def all_blocks(step, low, high, most):
    for count in range(1, most + 1):

        @pl.when(high - low == count)
        def _(count=count):
            step(low, count)


def beside(ref, j, count, rows):
    return jnp.concatenate([ref[j + k, rows, :] for k in range(count)], axis=1)


def attend_kernel(pairs, own_blocks, halo_blocks, bounds, segq, segk, qkv, kvh, ctx, ctx_t, ctx_low, lse, vt, qs, top, total, acc):
    width = pairs * BLK
    low = head_masks()
    half = BLK // 2
    for j in range(own_blocks + halo_blocks):
        for p in range(pairs):
            if j < own_blocks:
                tile = qkv[j * BLK : (j + 1) * BLK, 2 * width + p * BLK : 2 * width + (p + 1) * BLK]
            else:
                at = j - own_blocks
                tile = kvh[at * BLK : (at + 1) * BLK, width + p * BLK : width + (p + 1) * BLK]
            vt[j, p * BLK : (p + 1) * BLK, :] = tile.T

    def q_block(i, carry):
        rows = pl.ds(pl.multiple_of(i * BLK, BLK), BLK)
        for p in range(pairs):
            qs[p] = stack_heads(qkv[rows, p * BLK : (p + 1) * BLK], low)
        top[...] = jnp.full(top.shape, -1e30, f32)
        total[...] = jnp.zeros(total.shape, f32)
        acc[...] = jnp.zeros(acc.shape, f32)
        labels = segq[i]

        def k_block(ref, first, base, j, count):
            here = pl.ds(pl.multiple_of(j * BLK, BLK), count * BLK)
            there = pl.ds(pl.multiple_of((base + j) * BLK, BLK), count * BLK)
            same = segk[there, :] == labels
            for p in range(pairs):
                keys = ref[here, first + p * BLK : first + (p + 1) * BLK]
                scores = jnp.where(same, nt(keys, qs[p]), masked_score)
                old = top[p : p + 1, :]
                new = jnp.maximum(old, jnp.max(scores, axis=0, keepdims=True))
                expo = jnp.exp(scores - new)
                scale = jnp.exp(old - new)
                top[p : p + 1, :] = new
                total[p : p + 1, :] = total[p : p + 1, :] * scale + jnp.sum(expo, axis=0, keepdims=True)
                weights = expo.astype(bf16)
                for h in range(2):
                    values = beside(vt, base + j, count, slice(p * BLK + h * half, p * BLK + (h + 1) * half))
                    part = slice(h * half, (h + 1) * half)
                    cols = slice(h * BLK, (h + 1) * BLK)
                    acc[p, part, :] = acc[p, part, :] * scale[:, cols] + nn(values, weights[:, cols])

        each_block(functools.partial(k_block, qkv, width, 0), bounds[i, 0], bounds[i, 1])
        each_block(functools.partial(k_block, kvh, 0, own_blocks), bounds[i, 2], bounds[i, 3])
        for p in range(pairs):
            inverse = 1.0 / total[p : p + 1, :]
            flat = jnp.concatenate(
                [acc[p, :half, :] * inverse[:, :BLK], acc[p, half:, :] * inverse[:, BLK:]], axis=0
            )
            rounded = flat.astype(bf16)
            ctx_t[p * BLK : (p + 1) * BLK, rows] = flat
            ctx_low[p * BLK : (p + 1) * BLK, rows] = rounded
            ctx[rows, p * BLK : (p + 1) * BLK] = rounded.T
        lse[i] = top[...] + jnp.log(total[...])
        return carry

    lax.fori_loop(0, own_blocks, q_block, 0)


def attend_back_kernel(
    pairs, own_blocks, halo_blocks,
    bounds, segq, segk, qkv, kvh, ctx_t, lse, dctx, norm_sums, up_sum,
    dqkv, dkvh, sums,
    kt, qs, cs, delta, dqt, dk, dv,
):
    width = pairs * BLK
    low = head_masks()
    half = BLK // 2
    blocks = own_blocks + halo_blocks
    for j in range(blocks):
        for p in range(pairs):
            if j < own_blocks:
                tile = qkv[j * BLK : (j + 1) * BLK, width + p * BLK : width + (p + 1) * BLK]
            else:
                at = j - own_blocks
                tile = kvh[at * BLK : (at + 1) * BLK, p * BLK : (p + 1) * BLK]
            kt[j, p * BLK : (p + 1) * BLK, :] = tile.T
    dk[...] = jnp.zeros(dk.shape, f32)
    dv[...] = jnp.zeros(dv.shape, f32)
    sums[...] = jnp.zeros(sums.shape, f32)
    sums[0:8, :] = norm_sums[...]
    for at in range(up_sum.shape[1] // width):
        sums[8 + at : 9 + at, :] = up_sum[:, at * width : (at + 1) * width]

    def q_block(i, carry):
        rows = pl.ds(pl.multiple_of(i * BLK, BLK), BLK)
        for p in range(pairs):
            cols = slice(p * BLK, (p + 1) * BLK)
            qs[p] = stack_heads(qkv[rows, cols], low)
            pull = dctx[rows, cols]
            cs[p] = stack_heads(pull, low)
            prod = pull.T.astype(f32) * ctx_t[cols, rows]
            delta[p : p + 1, :] = jnp.concatenate(
                [jnp.sum(prod[:half], axis=0, keepdims=True), jnp.sum(prod[half:], axis=0, keepdims=True)], axis=1
            )
        dqt[...] = jnp.zeros(dqt.shape, f32)
        labels = segq[i]

        def k_block(ref, first, base, j, count):
            here = pl.ds(pl.multiple_of(j * BLK, BLK), count * BLK)
            there = pl.ds(pl.multiple_of((base + j) * BLK, BLK), count * BLK)
            same = segk[there, :] == labels
            for p in range(pairs):
                cols = slice(p * BLK, (p + 1) * BLK)
                keys = ref[here, first + p * BLK : first + (p + 1) * BLK]
                values = ref[here, first + width + p * BLK : first + width + (p + 1) * BLK]
                scores = jnp.where(same, nt(keys, qs[p]), masked_score)
                probs = jnp.exp(scores - lse[i, p : p + 1, :])
                pulls = nt(values, cs[p])
                dscore = (probs * (pulls - delta[p : p + 1, :])).astype(bf16)
                dv[there, cols] += nn(probs.astype(bf16), cs[p])
                dk[there, cols] += nn(dscore, qs[p])
                for h in range(2):
                    part = slice(h * half, (h + 1) * half)
                    flip = beside(kt, base + j, count, slice(p * BLK + h * half, p * BLK + (h + 1) * half))
                    dqt[p, part, :] += nn(flip, dscore[:, h * BLK : (h + 1) * BLK])

        all_blocks(functools.partial(k_block, qkv, width, 0), bounds[i, 0], bounds[i, 1], own_blocks)
        all_blocks(functools.partial(k_block, kvh, 0, own_blocks), bounds[i, 2], bounds[i, 3], halo_blocks)
        for p in range(pairs):
            cols = slice(p * BLK, (p + 1) * BLK)
            grad = dqt[p].astype(bf16).T * jnp.asarray(0.125, bf16)
            dqkv[rows, cols] = grad
            sums[6:7, cols] += jnp.sum(grad.astype(f32), axis=0, keepdims=True)
        return carry

    lax.fori_loop(0, own_blocks, q_block, 0)
    for j in range(blocks):
        rows = slice(j * BLK, (j + 1) * BLK)
        grad_k = dk[rows, :].astype(bf16)
        grad_v = dv[rows, :].astype(bf16)
        if j < own_blocks:
            dqkv[rows, width : 2 * width] = grad_k
            dqkv[rows, 2 * width :] = grad_v
        else:
            back = slice((j - own_blocks) * BLK, (j - own_blocks + 1) * BLK)
            dkvh[back, :width] = grad_k
            dkvh[back, width:] = grad_v
        sums[7:8, :] += jnp.sum(grad_v.astype(f32), axis=0, keepdims=True)


def vmem_specs(count):
    return [pl.BlockSpec(memory_space=pltpu.VMEM)] * count


def any_specs(count):
    return [pl.BlockSpec(memory_space=pl.ANY)] * count


def ordered_call(kernel, args, waits, passes, out_shape, in_specs, out_specs, **options):
    waits, passes = tuple(waits) + tuple(turn.last), tuple(passes)
    given, made = len(args), len(out_shape)
    skipped = len(waits) + len(passes)

    def body(*refs):
        outs = given + skipped
        refs[outs + made][...] = jnp.zeros((8, BLK), f32)
        kernel(*refs[:given], *refs[outs : outs + made], *refs[outs + made + 1 + len(passes) :])

    out = pl.pallas_call(
        body,
        out_shape=tuple(out_shape)
        + (jax.ShapeDtypeStruct((8, BLK), f32),)
        + tuple(jax.ShapeDtypeStruct(p.shape, p.dtype) for p in passes),
        in_specs=list(in_specs) + any_specs(skipped),
        out_specs=tuple(out_specs) + (pl.BlockSpec((8, BLK), lambda *step: (0, 0)),) + tuple(any_specs(len(passes))),
        input_output_aliases={given + len(waits) + k: made + 1 + k for k in range(len(passes))},
        **options,
    )(*args, *waits, *passes)
    turn.last = [out[made]]
    return out[:made], out[made + 1 :]


class Turn:
    last = []


turn = Turn()


def attend(bounds, segq, segk, qkv, kvh, waits, passes):
    tokens, width3 = qkv.shape
    width = width3 // 3
    pairs, own_blocks, halo_blocks = width // BLK, tokens // BLK, kvh.shape[0] // BLK
    blocks = own_blocks + halo_blocks
    return ordered_call(
        functools.partial(attend_kernel, pairs, own_blocks, halo_blocks),
        (bounds, segq, segk, qkv, kvh),
        waits,
        passes,
        out_shape=(
            jax.ShapeDtypeStruct((tokens, width), bf16),
            jax.ShapeDtypeStruct((width, tokens), f32),
            jax.ShapeDtypeStruct((width, tokens), bf16),
            jax.ShapeDtypeStruct((own_blocks, 8, 2 * BLK), f32),
        ),
        in_specs=[pl.BlockSpec(memory_space=pltpu.SMEM)] + vmem_specs(4),
        out_specs=tuple(vmem_specs(4)),
        scratch_shapes=[
            pltpu.VMEM((blocks, width, BLK), bf16),
            pltpu.VMEM((pairs, 2 * BLK, BLK), bf16),
            pltpu.VMEM((8, 2 * BLK), f32),
            pltpu.VMEM((8, 2 * BLK), f32),
            pltpu.VMEM((pairs, BLK, BLK), f32),
        ],
        compiler_params=pltpu.CompilerParams(vmem_limit_bytes=16 * 2**20),
        cost_estimate=cost(9),
        name="attend",
    )


def attend_back(bounds, segq, segk, qkv, kvh, ctx_t, lse, dctx, norm_sums, up_sum, waits, passes):
    tokens, width3 = qkv.shape
    width = width3 // 3
    pairs, own_blocks, halo_blocks = width // BLK, tokens // BLK, kvh.shape[0] // BLK
    blocks = own_blocks + halo_blocks
    return ordered_call(
        functools.partial(attend_back_kernel, pairs, own_blocks, halo_blocks),
        (bounds, segq, segk, qkv, kvh, ctx_t, lse, dctx, norm_sums, up_sum),
        waits,
        passes,
        out_shape=(
            jax.ShapeDtypeStruct((tokens, width3), bf16),
            jax.ShapeDtypeStruct(kvh.shape, bf16),
            jax.ShapeDtypeStruct((16, width), f32),
        ),
        in_specs=[pl.BlockSpec(memory_space=pltpu.SMEM)] + vmem_specs(9),
        out_specs=tuple(vmem_specs(3)),
        scratch_shapes=[
            pltpu.VMEM((blocks, width, BLK), bf16),
            pltpu.VMEM((pairs, 2 * BLK, BLK), bf16),
            pltpu.VMEM((pairs, 2 * BLK, BLK), bf16),
            pltpu.VMEM((8, 2 * BLK), f32),
            pltpu.VMEM((pairs, BLK, BLK), f32),
            pltpu.VMEM((blocks * BLK, width), f32),
            pltpu.VMEM((blocks * BLK, width), f32),
        ],
        compiler_params=pltpu.CompilerParams(vmem_limit_bytes=24 * 2**20),
        cost_estimate=cost(21),
        name="attend_back",
    )


CHUNK = 1536
ROWS = 256


def normalized(rows):
    center = rows - jnp.mean(rows, axis=-1, keepdims=True)
    spread = jnp.mean(center * center, axis=-1, keepdims=True)
    scale = lax.rsqrt(spread + norm_eps)
    return center * scale, scale


def feed_kernel(last, tokens, hidden, ctx, w_out, vec, w_up, up_bias, w_down, *rest):
    if last:
        first_rows, first_t, active_t, slope, second_rows, low, low_rows, first, total = rest
    else:
        first_rows, first_t, active_t, slope, second_rows, low, after, low_t, low_rows, first, total = rest
    step = pl.program_id(0)
    tiles = [slice(at, at + BLK) for at in range(0, tokens, BLK)]
    passes = [slice(at, at + ROWS) for at in range(0, tokens, ROWS)]

    @pl.when(step == 0)
    def _():
        for rows in tiles:
            resid = hidden[rows, :].astype(f32) + (nn(ctx[rows, :], w_out[...]) + vec[0:1, :])
            first_rows[rows, :] = resid
            unit, _ = normalized(resid)
            value = unit * vec[1:2, :] + vec[2:3, :]
            first[rows, :] = value
            total[rows, :] = jnp.zeros_like(value)
            rounded = value.astype(bf16)
            low_rows[rows, :] = rounded
            first_t[:, rows] = rounded.T

    for rows in passes:
        upward = nn(low_rows[rows, :], w_up[...]) + up_bias[...]
        density = jnp.exp(-0.5 * upward * upward) * 0.3989422804014327
        below = 0.5 + 0.5 * lax.erf(upward * 0.7071067811865476)
        active = (upward * below).astype(bf16)
        slope[rows, :] = below + upward * density
        active_t[:, rows] = active.T
        total[rows, :] += nn(active, w_down[...])

    @pl.when(step == pl.num_programs(0) - 1)
    def _():
        for rows in tiles:
            resid = first[rows, :] + (total[rows, :] + vec[3:4, :])
            second_rows[rows, :] = resid
            unit, _ = normalized(resid)
            value = unit * vec[4:5, :] + vec[5:6, :]
            rounded = value.astype(bf16)
            low[rows, :] = rounded
            if not last:
                after[rows, :] = value
                low_t[:, rows] = rounded.T


def whole(shape):
    return pl.BlockSpec(shape, lambda step: (0,) * len(shape))


def feed(last, layer_idx, hidden, ctx, w_out, vec, w_up, up_bias, w_down, waits, passes):
    tokens, width = hidden.shape
    wide = w_up.shape[-1]
    rows = whole((tokens, width))
    shapes = [
        jax.ShapeDtypeStruct((tokens, width), f32),
        jax.ShapeDtypeStruct((width, tokens), bf16),
        jax.ShapeDtypeStruct((wide, tokens), bf16),
        jax.ShapeDtypeStruct((tokens, wide), f32),
        jax.ShapeDtypeStruct((tokens, width), f32),
        jax.ShapeDtypeStruct((tokens, width), bf16),
    ]
    specs = [
        rows,
        whole((width, tokens)),
        pl.BlockSpec((CHUNK, tokens), lambda step: (step, 0)),
        pl.BlockSpec((tokens, CHUNK), lambda step: (0, step)),
        rows,
        rows,
    ]
    if not last:
        shapes.append(jax.ShapeDtypeStruct((tokens, width), f32))
        shapes.append(jax.ShapeDtypeStruct((width, tokens), bf16))
        specs.append(rows)
        specs.append(whole((width, tokens)))
    return ordered_call(
        functools.partial(feed_kernel, last, tokens),
        (hidden, ctx, w_out, vec, w_up, up_bias, w_down),
        waits,
        passes,
        grid=(wide // CHUNK,),
        out_shape=tuple(shapes),
        in_specs=[
            rows,
            rows,
            pl.BlockSpec((None, width, width), lambda step: (layer_idx, 0, 0)),
            whole(vec.shape),
            pl.BlockSpec((None, width, CHUNK), lambda step: (layer_idx, 0, step)),
            pl.BlockSpec((1, CHUNK), lambda step: (0, step)),
            pl.BlockSpec((None, CHUNK, width), lambda step: (layer_idx, step, 0)),
        ],
        out_specs=tuple(specs),
        scratch_shapes=[
            pltpu.VMEM((tokens, width), bf16),
            pltpu.VMEM((tokens, width), f32),
            pltpu.VMEM((tokens, width), f32),
        ],
        compiler_params=pltpu.CompilerParams(vmem_limit_bytes=48 * 2**20),
        cost_estimate=cost(15),
        name="feed",
    )


def norm_back(grad, gain, rows):
    unit, scale = normalized(rows)
    lifted = grad * gain
    first = jnp.mean(lifted, axis=-1, keepdims=True)
    second = jnp.mean(lifted * unit, axis=-1, keepdims=True)
    return scale * (lifted - first - unit * second), unit


def over_rows(value):
    return jnp.sum(value, axis=0, keepdims=True)


def feed_back_kernel(
    tokens, grad, back, edge, second_rows, first_rows, slope, w_down, w_up, w_out, vec,
    dz, du, da, dr, dc, sums, up_sum, dr_two, total,
):
    step = pl.program_id(0)
    tiles = [slice(at, at + BLK) for at in range(0, tokens, BLK)]
    passes = [slice(at, at + ROWS) for at in range(0, tokens, ROWS)]

    @pl.when(step == 0)
    def _():
        sums[...] = jnp.zeros(sums.shape, f32)
        for rows in tiles:
            pull = grad[rows, :].astype(f32)
            if back.shape[0] > BLK:
                at = rows.start - edge[0]
                inside = (at >= 0) & (at < back.shape[0])
                here = pl.ds(pl.multiple_of(jnp.where(inside, at, 0), BLK), BLK)
                pull = pull + jnp.where(inside, back[here, :].astype(f32), 0.0)
            value, unit = norm_back(pull, vec[4:5, :], second_rows[rows, :])
            dr_two[rows, :] = value
            total[rows, :] = jnp.zeros_like(value)
            rounded = value.astype(bf16)
            dz[rows, :] = rounded
            sums[3:4, :] += over_rows(rounded.astype(f32))
            sums[4:5, :] += over_rows(pull * unit)
            sums[5:6, :] += over_rows(pull)

    up_sum[...] = jnp.zeros(up_sum.shape, f32)
    for rows in passes:
        pull = (nt(dz[rows, :], w_down[...]) * slope[rows, :]).astype(bf16)
        du[rows, :] = pull
        up_sum[...] += over_rows(pull.astype(f32))
        total[rows, :] += nt(pull, w_up[...])

    @pl.when(step == pl.num_programs(0) - 1)
    def _():
        for rows in tiles:
            pull = total[rows, :] + dr_two[rows, :]
            value, unit = norm_back(pull, vec[1:2, :], first_rows[rows, :])
            dr[rows, :] = value
            rounded = value.astype(bf16)
            da[rows, :] = rounded
            sums[0:1, :] += over_rows(rounded.astype(f32))
            sums[1:2, :] += over_rows(pull * unit)
            sums[2:3, :] += over_rows(pull)
            dc[rows, :] = nt(rounded, w_out[...]).astype(bf16)


def feed_back(layer_idx, grad, back, edge, second_rows, first_rows, slope, w_down, w_up, w_out, vec, waits, passes):
    tokens, width = grad.shape
    wide = w_up.shape[-1]
    rows = whole((tokens, width))
    return ordered_call(
        functools.partial(feed_back_kernel, tokens),
        (grad, back, edge, second_rows, first_rows, slope, w_down, w_up, w_out, vec),
        waits,
        passes,
        grid=(wide // CHUNK,),
        out_shape=(
            jax.ShapeDtypeStruct((tokens, width), bf16),
            jax.ShapeDtypeStruct((tokens, wide), bf16),
            jax.ShapeDtypeStruct((tokens, width), bf16),
            jax.ShapeDtypeStruct((tokens, width), f32),
            jax.ShapeDtypeStruct((tokens, width), bf16),
            jax.ShapeDtypeStruct((8, width), f32),
            jax.ShapeDtypeStruct((1, wide), f32),
        ),
        in_specs=[
            rows,
            whole(back.shape),
            pl.BlockSpec(memory_space=pltpu.SMEM),
            rows,
            rows,
            pl.BlockSpec((tokens, CHUNK), lambda step: (0, step)),
            pl.BlockSpec((None, CHUNK, width), lambda step: (layer_idx, step, 0)),
            pl.BlockSpec((None, width, CHUNK), lambda step: (layer_idx, 0, step)),
            pl.BlockSpec((None, width, width), lambda step: (layer_idx, 0, 0)),
            whole(vec.shape),
        ],
        out_specs=(
            rows,
            pl.BlockSpec((tokens, CHUNK), lambda step: (0, step)),
            rows,
            rows,
            rows,
            whole((8, width)),
            pl.BlockSpec((1, CHUNK), lambda step: (0, step)),
        ),
        scratch_shapes=[pltpu.VMEM((tokens, width), f32), pltpu.VMEM((tokens, width), f32)],
        compiler_params=pltpu.CompilerParams(vmem_limit_bytes=48 * 2**20),
        cost_estimate=cost(17),
        name="feed_back",
    )


def grad_down_kernel(core, active_t, dz, send, keep):
    groups, head, parts, thin, width = send.shape
    mine = core[0]
    for which, out in ((1 - mine, send), (mine, keep)):
        for group in range(groups):
            value = nn(active_t[2 * group + which], dz[...])
            for shard in range(head):
                for at in range(parts):
                    here = (shard * parts + at) * thin
                    out[group, shard, at] = value[here : here + thin].astype(bf16)


def grad_up_kernel(core, first_t, du, send, keep, lhs):
    groups, head, parts, thin, width = send.shape
    rows = head * thin
    mine = core[0]
    for which, out in ((1 - mine, send), (mine, keep)):
        if rows % 16 == 0:
            for group in range(groups):
                lhs[group * rows : (group + 1) * rows, :] = first_t[2 * group + which]
        for at in range(parts):
            pulls = du[:, at * width : (at + 1) * width]
            if rows % 16 == 0:
                value = nn(lhs[...], pulls)
                values = [value[group * rows : (group + 1) * rows] for group in range(groups)]
            else:
                values = [nn(first_t[2 * group + which], pulls) for group in range(groups)]
            for group in range(groups):
                for shard in range(head):
                    out[group, shard, at] = values[group][shard * thin : (shard + 1) * thin].astype(bf16)


def grad_feed(core, left_t, right, parts, devices, head, scratch):
    rows, tokens = left_t.shape
    thin = rows // devices // head // (1 if scratch else parts)
    width = right.shape[1] // (parts if scratch else 1)
    out = jax.ShapeDtypeStruct((devices // 2, head, parts, thin, width), bf16)
    halves, _ = ordered_call(
        grad_up_kernel if scratch else grad_down_kernel,
        (core, left_t.reshape(devices, rows // devices, tokens), right),
        (),
        (),
        out_shape=(out, out),
        in_specs=[pl.BlockSpec(memory_space=pltpu.SMEM)] + vmem_specs(2),
        out_specs=tuple(vmem_specs(2)),
        scratch_shapes=[pltpu.VMEM((rows // 2, tokens), bf16)] if scratch else [],
        compiler_params=pltpu.CompilerParams(vmem_limit_bytes=18 * 2**20),
        cost_estimate=cost(5),
        name="grad_up" if scratch else "grad_down",
    )
    return halves


def grad_heads_kernel(core, ctx_t, low_t, halo_t, da, dqkv, dkvh, sums, send, keep, one, two, three):
    groups, thin = ctx_t.shape[0] // 2, ctx_t.shape[1]
    width = send.shape[2] // 4
    high = thin // TILE
    for r in range(sums.shape[0] // TILE):
        value = sums[r * TILE : (r + 1) * TILE, :].astype(bf16)
        for out in (send, keep):
            out[groups * high, :, r * width : (r + 1) * width] = value
    mine = core[0]
    for which, out in ((1 - mine, send), (mine, keep)):
        if thin % 16 == 0:
            for group in range(groups):
                here = slice(group * thin, (group + 1) * thin)
                one[here, :] = ctx_t[2 * group + which]
                two[here, :] = low_t[2 * group + which]
                three[here, :] = halo_t[2 * group + which]
            parts = [(range(groups), one, two, three)]
        else:
            parts = [
                ([group], ctx_t.at[2 * group + which], low_t.at[2 * group + which], halo_t.at[2 * group + which])
                for group in range(groups)
            ]
        for members, left_one, left_two, left_three in parts:
            for at in range(0, 4 * width, width):
                if at < width:
                    value = nn(left_one[...], da[...])
                else:
                    value = nn(left_two[...], dqkv[:, at - width : at])
                    if at >= 2 * width:
                        value = value + nn(left_three[...], dkvh[:, at - 2 * width : at - width])
                for place, group in enumerate(members):
                    here = value[place * thin : (place + 1) * thin].reshape(high, TILE, width)
                    out[group * high : (group + 1) * high, :, at : at + width] = here.astype(bf16)


def grad_heads(core, ctx_t, low_t, halo_t, da, dqkv, dkvh, sums, devices, waits, passes):
    tokens, width = da.shape
    thin = width // devices
    out = jax.ShapeDtypeStruct((devices // 2 * thin // TILE + 1, TILE, 4 * width), bf16)
    extent = halo_t.shape[1]
    return ordered_call(
        grad_heads_kernel,
        (
            core,
            ctx_t.reshape(devices, thin, tokens),
            low_t.reshape(devices, thin, tokens),
            halo_t.reshape(devices, thin, extent),
            da,
            dqkv,
            dkvh,
            sums,
        ),
        waits,
        passes,
        out_shape=(out, out),
        in_specs=[pl.BlockSpec(memory_space=pltpu.SMEM)] + vmem_specs(7),
        out_specs=tuple(vmem_specs(2)),
        scratch_shapes=[
            pltpu.VMEM((width // 2, tokens), bf16),
            pltpu.VMEM((width // 2, tokens), bf16),
            pltpu.VMEM((width // 2, extent), bf16),
        ],
        compiler_params=pltpu.CompilerParams(vmem_limit_bytes=20 * 2**20),
        cost_estimate=cost(8),
        name="grad_heads",
    )


def assemble_kernel(relative, place, own, *refs):
    *refs, out = refs
    shard, group = place[0], place[1]
    kinds = own.shape[0]
    out[:, pl.ds(shard, 1)] = own[...].reshape(kinds, 1, *own.shape[1:])
    lane = 0
    for ref, order in zip(refs, relative):
        lanes = slice(lane, lane + ref.shape[-1])
        lane = lanes.stop % own.shape[-1]
        for at, change in enumerate(order):
            for step in range(ref.shape[1]):
                for kind in range(kinds):
                    out[kind, shard ^ (step + 1), group ^ change, :, lanes] = ref[at, step, kind]


def assemble(relative, place, own, refs, passes):
    head = lax.axis_size("head")
    (out,), passed = ordered_call(
        functools.partial(assemble_kernel, relative),
        (place, own, *refs),
        (),
        passes,
        out_shape=(jax.ShapeDtypeStruct((own.shape[0], head) + own.shape[1:], bf16),),
        in_specs=[pl.BlockSpec(memory_space=pltpu.SMEM)] + vmem_specs(1 + len(refs)),
        out_specs=vmem_specs(1),
        compiler_params=pltpu.CompilerParams(vmem_limit_bytes=16 * 2**20),
        cost_estimate=cost(1.5),
        name="assemble",
    )
    return out, passed


def grow(value, order):
    value, relative = value[None], [0]
    for place in order:
        value = jnp.concatenate([value, swap(value, "dp", 1 << place)], axis=0)
        relative = relative + [other ^ (1 << place) for other in relative]
    return value, relative


def flip_kernel(count, shard, biases, *refs):
    for source, target in zip(refs[:count], refs[count : 2 * count]):
        for at in range(0, source.shape[0], BLK):
            target[:, at : at + BLK] = source[at : at + BLK, :].T
    shifts = refs[2 * count]
    members, _, width = biases.shape
    layers, part = shifts.shape[0], width // members
    shifts[...] = jnp.zeros(shifts.shape, f32)
    rows = [biases[step].astype(f32) for step in range(members)]
    for member in range(members):
        value = jnp.zeros((1, width), f32)
        for step, row in enumerate(rows):
            value = jnp.where((shard[0] ^ step) == member, row, value)
        for layer_idx in range(layers):
            for at, kind in ((0, 0), (1, 2)):
                here = (2 * layer_idx + at) * part
                there = kind * width + member * part
                shifts[layer_idx, :, there : there + part] = value[:, here : here + part]


def flip(values, shard, biases, layers):
    width = biases.shape[2]
    shapes = [jax.ShapeDtypeStruct(v.shape[::-1], v.dtype) for v in values]
    return ordered_call(
        functools.partial(flip_kernel, len(values)),
        (shard, biases, *values),
        (),
        (),
        out_shape=shapes + [jax.ShapeDtypeStruct((layers, 1, 3 * width), f32)],
        in_specs=[pl.BlockSpec(memory_space=pltpu.SMEM)] + vmem_specs(1 + len(values)),
        out_specs=vmem_specs(1 + len(values)),
        compiler_params=pltpu.CompilerParams(vmem_limit_bytes=8 * 2**20),
        cost_estimate=cost(1.5),
        name="flip",
    )


def collect_kernel(*refs):
    *parts, out = refs
    for k, ref in enumerate(parts):
        out[k] = ref[...]


def collect(values):
    (out,), _ = ordered_call(
        collect_kernel,
        values,
        (),
        (),
        out_shape=(jax.ShapeDtypeStruct((len(values),) + values[0].shape, values[0].dtype),),
        in_specs=vmem_specs(len(values)),
        out_specs=vmem_specs(1),
        compiler_params=pltpu.CompilerParams(vmem_limit_bytes=8 * 2**20),
        cost_estimate=cost(1.4),
        name="collect",
    )
    return out


def from_heads_in_turn(piece):
    got = [swap(piece, "head", 1)]
    step = 2
    while step < lax.axis_size("head"):
        far = [swap(value, "head", step) for value in [piece]]
        for value in far:
            got = got + [value, swap(value, "head", 1)]
        step *= 2
    return got


def from_heads(piece):
    return [swap(piece, "head", step) for step in range(1, lax.axis_size("head"))]


def added(keep, got):
    return keep.astype(f32) + got.astype(f32)


def advance_kernel(counts, size, tail, sources, scalars, *refs):
    core, mine = scalars[0], scalars[1]
    keeps, gots, (send, out) = refs[:sources], refs[sources : 2 * sources], refs[2 * sources :]
    blocks = (keeps[0].shape[0] - tail) // size
    for target, which in ((send, 1 - mine), (out, mine)):
        for k in range(blocks // 2):
            spots = [2 * (k // after) * after + k % after for after in counts]
            at = jnp.where(core == 0, spots[0] + which * counts[0], spots[1] + which * counts[1])
            here = pl.ds(at * size, size)
            for source, (keep, got) in enumerate(zip(keeps, gots)):
                value = added(keep[here], got[here]).astype(bf16)
                if sources > 1:
                    target[k * size : (k + 1) * size, source] = value
                else:
                    target[k * size : (k + 1) * size] = value
        if tail:
            value = added(keeps[0][blocks * size :], gots[0][blocks * size :]).astype(bf16)
            target[blocks // 2 * size :] = value


def turn_heads_kernel(head, scalars, keep, got, send, out):
    mine = scalars[1]
    tiles, _, columns = keep.shape
    rows, width = (tiles - 1) * TILE, columns // 4
    held = added(keep[: tiles - 1], got[: tiles - 1]).reshape(rows, columns)
    part, thin = width // head, rows // head
    kinds = []
    if rows < BLK:
        filler = jnp.zeros((BLK - rows, width), f32)
    for kind in range(1, 4):
        value = held[:, kind * width : (kind + 1) * width]
        value = jnp.concatenate([value, filler], axis=0) if rows < BLK else value
        kinds.append(value.T)
    high = part // (width // BLK)
    count = part // TILE
    for shard in range(head):
        pieces = [value[shard * part : (shard + 1) * part] for value in kinds]
        own = held[shard * thin : (shard + 1) * thin, :width]
        own = jnp.concatenate([own, jnp.zeros((high - thin, width), f32)], axis=0)
        pieces.append(jnp.concatenate([own[:, at : at + BLK] for at in range(0, width, BLK)], axis=0))
        for chosen, target in ((1 - mine, send), (mine, out)):

            @pl.when(chosen == shard % 2)
            def _(target=target, pieces=pieces, shard=shard):
                for kind, piece in enumerate(pieces):
                    at = (shard // 2 * 4 + kind) * count
                    target[at : at + count] = piece.reshape(count, TILE, BLK).astype(bf16)

    last = added(keep[tiles - 1], got[tiles - 1])
    for target in (send, out):
        for k in range(2 * width // BLK):
            target[head // 2 * 4 * count + k] = last[:, k * BLK : (k + 1) * BLK].astype(bf16)


class Flight:
    def __init__(self, keeps, gots, turned):
        dp, head = lax.axis_size("dp"), lax.axis_size("head")
        bits = dp.bit_length() - 1
        upper = list(range(1, bits))
        self.orders = [list(upper), list(upper)[::-1]]
        self.left = [upper[::-1], upper[::-1]]
        self.head_bits = list(range(head.bit_length() - 1))
        self.turned = turned
        self.tail, self.size = 0, 1
        if turned:
            self.tail, self.size = 1, (keeps[0].shape[0] - 1) // (dp // 2)
        else:
            shape = (keeps[0].shape[0] * keeps[0].shape[1],) + keeps[0].shape[2:]
            keeps, gots = [k.reshape(shape) for k in keeps], [g.reshape(shape) for g in gots]
        self.keeps, self.gots = list(keeps), list(gots)

    def step(self, waits=(), passes=()):
        blocks = (self.keeps[0].shape[0] - self.tail) // self.size
        sources = len(self.keeps)
        core = bit_of("dp", 0)
        rest = self.keeps[0].shape[1:]
        if sources > 1:
            rest = (sources,) + rest
        devices = lax.axis_size("dp")
        counts = [1, 1]
        if self.orders[0]:
            places = [order.pop(0) for order in self.orders]
            counts = []
            for left, place in zip(self.left, places):
                axis = left.index(place)
                left.remove(place)
                counts.append((blocks // 2) >> axis)
            mine = jnp.where(core == 0, bit_of("dp", places[0]), bit_of("dp", places[1]))
            axis_name, pairs = "dp", [(i, i ^ (1 << places[i & 1])) for i in range(devices)]
        else:
            place = self.head_bits.pop(0)
            mine = bit_of("head", place)
            head = lax.axis_size("head")
            axis_name, pairs = "head", [(i, i ^ (1 << place)) for i in range(head)]
        if axis_name == "head" and self.turned:
            width = rest[1] // 4
            self.turned = False
            self.size, self.tail = 4 * (width // head) // TILE, 2 * width // BLK
            out_shape = (head // 2 * self.size + self.tail, TILE, BLK)
            kernel = functools.partial(turn_heads_kernel, head)
        else:
            out_shape = (blocks // 2 * self.size + self.tail,) + rest
            kernel = functools.partial(advance_kernel, counts, self.size, self.tail, sources)
        out = jax.ShapeDtypeStruct(out_shape, bf16)
        (send, keep), passed = ordered_call(
            kernel,
            (jnp.stack([core, mine]).astype(jnp.int32), *self.keeps, *self.gots),
            waits,
            passes,
            out_shape=[out] * 2,
            in_specs=[pl.BlockSpec(memory_space=pltpu.SMEM)] + vmem_specs(2 * sources),
            out_specs=vmem_specs(2),
            compiler_params=pltpu.CompilerParams(vmem_limit_bytes=20 * 2**20),
            cost_estimate=cost(1 + 2e-6 * out.size),
            name="advance",
        )
        self.keeps, self.gots = [keep], [lax.ppermute(send, axis_name, pairs)]
        return passed

    def finish(self):
        while self.orders[0] or self.head_bits:
            self.step()
        total = added(self.keeps[0], self.gots[0])
        return total if self.tail else total[0]


def per_device(
    tokens_in,
    segment,
    w_qkv,
    qv_bias,
    w_out,
    out_bias,
    ln1_gain,
    ln1_bias,
    w_up,
    up_bias,
    w_down,
    down_bias,
    ln2_gain,
    ln2_bias,
    cotangent,
):
    turn.last = []
    layers, width = w_qkv.shape[0], w_qkv.shape[1]
    part = w_qkv.shape[3] * w_qkv.shape[4]
    head_size = w_qkv.shape[4]
    tokens = tokens_in.shape[0]
    seq = segment.shape[1]
    dp, head = lax.axis_size("dp"), lax.axis_size("head")
    bits = dp.bit_length() - 1
    shard, group = lax.axis_index("head"), lax.axis_index("dp")
    halves = seq // tokens
    row, half = shard // halves, shard % halves
    upper = list(range(1, bits))

    edge = jnp.where(half == 0, tokens - HALO, 0)
    core = bit_of("dp", 0)

    own_w = w_qkv.transpose(0, 2, 3, 4, 1).reshape(layers, 3, part, width)
    own_first = own_w[0].reshape(3, dp, part // dp, width)
    piece = pick(own_first, group, 1).reshape(-1, width)
    rows_w = piece.shape[0]
    bias_own = qv_bias.reshape(1, layers * 2 * part)
    bias_own = jnp.pad(bias_own, ((0, 7), (0, width - bias_own.shape[1])))
    piece = jnp.concatenate([piece, bias_own])
    got = from_heads(piece)
    halo = swap(lax.dynamic_slice_in_dim(tokens_in, edge, HALO), "head", 1)
    biases = jnp.stack([other[rows_w : rows_w + 1] for other in [piece] + got])
    got = jnp.stack([other[:rows_w] for other in got]).reshape(head - 1, 3, part // dp, width)
    left, relative_left = grow(got[..., : width // 2], upper)
    right, relative_right = grow(got[..., width // 2 :], upper[::-1])
    both = jnp.stack([left, right])
    both = jnp.concatenate([both, swap(both, "dp", 1)], axis=1)
    relative = [order + [other ^ 1 for other in order] for order in (relative_left, relative_right)]
    place = jnp.stack([shard, group]).astype(jnp.int32)
    own_later = [own_w[k].reshape(3, 2, part // 2, width) for k in range(1, layers)]
    (low_t, halo_t, shifts), _ = flip([tokens_in, halo], shard.reshape(1).astype(jnp.int32), biases, layers)
    w_first, pieces = assemble(relative, place, own_first, [both[0], both[1]], [pick(own, core, 1) for own in own_later])
    later_got = [from_heads_in_turn(value) for value in pieces]
    w_cats = [w_first.reshape(3 * head * part, width)]

    def later_weights(own, got):
        theirs = swap(got, "dp", 1)
        whole = assemble([[0], [1]], jnp.stack([shard, core]).astype(jnp.int32), own, [got[None], theirs[None]], [])[0]
        return whole.reshape(3 * head * part, width)

    labels = pick(segment, row, 0)
    own_labels = lax.dynamic_slice_in_dim(labels, half * tokens, tokens)
    halo_start = jnp.where(half == 0, tokens, tokens - HALO)
    halo_labels = lax.dynamic_slice_in_dim(labels, halo_start, HALO)
    blocks = tokens // BLK
    by_block = own_labels.reshape(blocks, BLK)
    least, most = by_block[:, :1], by_block[:, -1:]

    def count(flags):
        return jnp.sum(flags.astype(jnp.int32), axis=1)

    bounds = jnp.stack(
        [
            count(own_labels[None] < least) // BLK,
            (count(own_labels[None] <= most) + BLK - 1) // BLK,
            count(halo_labels[None] < least) // BLK,
            (count(halo_labels[None] <= most) + BLK - 1) // BLK,
        ],
        axis=1,
    )
    segq = jnp.concatenate([by_block, by_block], axis=1).reshape(blocks, 1, 2 * BLK)
    segk = jnp.concatenate([own_labels, halo_labels]).reshape(-1, 1)
    core_at = core.reshape(1).astype(jnp.int32)

    vecs = jnp.stack(
        [out_bias, ln1_gain, ln1_bias, down_bias, ln2_gain, ln2_bias, out_bias, out_bias], axis=1
    ).astype(f32)
    up_bias_wide = up_bias.astype(f32)

    hidden, low = tokens_in, tokens_in
    saved = []
    for layer_idx in range(layers):
        last = layer_idx == layers - 1
        w_cat = w_cats[layer_idx]
        shift = shifts[layer_idx]
        factor = jnp.where(jnp.arange(3 * width) < width, 0.125, 1.0).astype(f32)
        qkv = ((nt(low, w_cat) + shift) * factor).astype(bf16)
        kvh = (nt(halo, w_cat[width:]) + shift[:, width:]).astype(bf16)
        (ctx, ctx_t, ctx_low, lse), _ = attend(bounds, segq, segk, qkv, kvh, (), ())
        fed, _ = feed(
            last, layer_idx, hidden, ctx, w_out, vecs[layer_idx], w_up, up_bias_wide[layer_idx : layer_idx + 1], w_down, (), ()
        )
        first_rows, first_t, active_t, slope, second_rows, after_low = fed[:6]
        saved.append((low_t, halo_t, qkv, kvh, ctx_t, ctx_low, lse, first_rows, first_t, active_t, slope, second_rows))
        if last:
            output = after_low
        else:
            low, hidden, low_t = after_low, fed[6], fed[7]
            halo = swap(lax.dynamic_slice_in_dim(low, edge, HALO), "head", 1)
            halo_t = halo.T
            w_cats.append(later_weights(own_later[layer_idx], collect(later_got[layer_idx])))

    grad_hidden, back = cotangent, jnp.zeros((BLK, width), bf16)
    flights = []
    for layer_idx in reversed(range(layers)):
        low_t, halo_t, qkv, kvh, ctx_t, ctx_low, lse, first_rows, first_t, active_t, slope, second_rows = saved[layer_idx]
        w_cat = w_cats[layer_idx]
        (dz, du, da, dr, dc, sums, up_sum), _ = feed_back(
            layer_idx, grad_hidden, back, edge.reshape(1).astype(jnp.int32), second_rows, first_rows, slope, w_down, w_up, w_out, vecs[layer_idx], (), ()
        )
        if flights:
            flights[1].step()
            flights[0].step()
        parts = du.shape[1] // width
        down_send, down_keep = grad_feed(core_at, active_t, dz, parts, dp, head, False)
        down_got = swap(down_send, "dp", 1)
        up_send, up_keep = grad_feed(core_at, first_t, du, parts, dp, head, True)
        up_got = swap(up_send, "dp", 1)
        fed = Flight([down_keep, up_keep], [down_got, up_got], False)
        fed.step()
        (dqkv, dkvh, sums), _ = attend_back(bounds, segq, segk, qkv, kvh, ctx_t, lse, dc, sums, up_sum, (), ())
        part_halo = nn(dkvh, w_cat[width:]).astype(bf16)
        back = swap(part_halo, "head", 1)
        if flights:
            flights[1].step()
            flights[0].step()
        (send, keep), _ = grad_heads(core_at, ctx_low, low_t, halo_t, da, dqkv, dkvh, sums, dp, (part_halo,), ())
        heads = Flight([keep], [swap(send, "dp", 1)], True)
        grad_hidden = nn(dqkv, w_cat) + dr
        fed.step()
        if flights:
            flights[1].step()
            heads.step()
            fed.step()
            heads.step()
            fed.step()
            heads.step()
            flights[1].step()
            first, second = flights
            passed = heads.step(passes=(first.keeps[0], second.keeps[0]))
            first.keeps, second.keeps = [passed[0]], [passed[1]]
        flights = flights + [fed, heads]

    padded = lax.dynamic_update_slice(jnp.zeros((tokens, width), bf16), back, (edge, 0))
    grad_hidden = grad_hidden + padded.astype(f32)

    results = []
    for place in range(layers):
        fed, heads = flights[2 * place], flights[2 * place + 1]
        thin = width // (dp * head)
        total = fed.finish()
        out_down = total[0].reshape(-1, width)
        out_up = total[1].transpose(1, 0, 2).reshape(thin, -1)
        total = heads.finish()
        pieces = total[: 4 * part // TILE].reshape(4, part, BLK)
        out_out = pieces[3].reshape(width // BLK, -1, BLK)[:, :thin].transpose(1, 0, 2).reshape(thin, width)
        sums = total[4 * part // TILE :].transpose(1, 0, 2).reshape(TILE, 2, width).transpose(1, 0, 2)
        results.append((pieces[:3, :, : width // dp], out_out, out_up, out_down, sums.reshape(2 * TILE, width)))
    results = results[::-1]
    out_qkv, out_w_out, out_up, out_down, total = (jnp.stack([r[k] for r in results]) for k in range(5))
    out_qkv = out_qkv.reshape(layers, 3, part // head_size, head_size, -1).transpose(0, 4, 1, 2, 3)

    device = group * head + shard
    thin = width // (dp * head)
    mine = lax.dynamic_slice_in_dim(total[:, :6], device * thin, thin, axis=2)
    ups = total[:, 8 : 8 + up_bias.shape[1] // width].reshape(layers, -1)
    thick = ups.shape[1] // (dp * head)
    out_ups = lax.dynamic_slice_in_dim(ups, device * thick, thick, axis=1)
    qvs = total[:, 6:8].reshape(layers, 2, head, part // head_size, dp, head_size // dp)
    out_qv = pick(pick(qvs, shard, 2), group, 3)
    return (
        output,
        grad_hidden,
        out_qkv,
        out_qv,
        out_w_out,
        mine[:, 0],
        mine[:, 1],
        mine[:, 2],
        out_up,
        out_ups,
        out_down,
        mine[:, 3],
        mine[:, 4],
        mine[:, 5],
    )


def solution(mesh):
    return jax.shard_map(
        per_device,
        mesh=mesh,
        in_specs=(
            P(("dp", "head"), None),
            P("dp", None),
            P(None, None, None, "head", None),
            P(None, None, "head", None),
            P(),
            P(),
            P(),
            P(),
            P(),
            P(),
            P(),
            P(),
            P(),
            P(),
            P(("dp", "head"), None),
        ),
        out_specs=(
            P(("dp", "head"), None),
            P(("dp", "head"), None),
            P(None, "dp", None, "head", None),
            P(None, None, "head", "dp"),
            P(None, ("dp", "head"), None),
            P(None, ("dp", "head")),
            P(None, ("dp", "head")),
            P(None, ("dp", "head")),
            P(None, ("dp", "head"), None),
            P(None, ("dp", "head")),
            P(None, ("dp", "head"), None),
            P(None, ("dp", "head")),
            P(None, ("dp", "head")),
            P(None, ("dp", "head")),
        ),
        check_vma=False,
    )
```

```python
import functools

import jax
import jax.numpy as jnp
from jax import lax
from jax.experimental import pallas as pl
from jax.experimental.pallas import tpu as pltpu
from jax.sharding import PartitionSpec as P

norm_eps = 1e-06
masked_score = -1000000000.0
f32 = jnp.float32
bf16 = jnp.bfloat16

BLK = 128
TILE = 8
SCALE = 0.5
HALO = 384


def cost(microseconds):
    return pl.CostEstimate(flops=int(microseconds * SCALE * 1.15e9), bytes_accessed=1000, transcendentals=0)


def swap(value, axis, bit):
    size = lax.axis_size(axis)
    return lax.ppermute(value, axis, [(i, i ^ bit) for i in range(size)])


def bit_of(axis, place):
    return (lax.axis_index(axis) >> place) & 1


def pick(value, index, axis):
    return lax.dynamic_index_in_dim(value, index, axis, keepdims=False)


def add_low(*terms):
    total = terms[0].astype(f32)
    for term in terms[1:]:
        total = total + term.astype(f32)
    return total


def finish_head(slot):
    size = lax.axis_size("head")
    me = lax.axis_index("head")
    got = [swap(slot(me ^ step), "head", step) for step in range(1, size)]
    return add_low(slot(me), *got)


def head_masks():
    lane = lax.broadcasted_iota(jnp.int32, (BLK, BLK), 1)
    return lane < BLK // 2


def stack_heads(pair, low):
    zero = jnp.zeros_like(pair)
    return jnp.concatenate([jnp.where(low, pair, zero), jnp.where(low, zero, pair)], axis=0)


def nt(left, right):
    return lax.dot_general(left, right, (((1,), (1,)), ((), ())), preferred_element_type=f32)


def nn(left, right):
    return lax.dot_general(left, right, (((1,), (0,)), ((), ())), preferred_element_type=f32)


def each_block(step, low, high):
    def one(j, carry):
        step(j, 1)
        return carry

    lax.fori_loop(low, high, one, 0)


def all_blocks(step, low, high, most):
    for count in range(1, most + 1):

        @pl.when(high - low == count)
        def _(count=count):
            step(low, count)


def beside(ref, j, count, rows):
    return jnp.concatenate([ref[j + k, rows, :] for k in range(count)], axis=1)


def attend_kernel(pairs, own_blocks, halo_blocks, bounds, segq, segk, qkv, kvh, ctx, ctx_t, ctx_low, lse, vt, qs, top, total, acc):
    width = pairs * BLK
    low = head_masks()
    half = BLK // 2
    for j in range(own_blocks + halo_blocks):
        for p in range(pairs):
            if j < own_blocks:
                tile = qkv[j * BLK : (j + 1) * BLK, 2 * width + p * BLK : 2 * width + (p + 1) * BLK]
            else:
                at = j - own_blocks
                tile = kvh[at * BLK : (at + 1) * BLK, width + p * BLK : width + (p + 1) * BLK]
            vt[j, p * BLK : (p + 1) * BLK, :] = tile.T

    def q_block(i, carry):
        rows = pl.ds(pl.multiple_of(i * BLK, BLK), BLK)
        for p in range(pairs):
            qs[p] = stack_heads(qkv[rows, p * BLK : (p + 1) * BLK], low)
        top[...] = jnp.full(top.shape, -1e30, f32)
        total[...] = jnp.zeros(total.shape, f32)
        acc[...] = jnp.zeros(acc.shape, f32)
        labels = segq[i]

        def k_block(ref, first, base, j, count):
            here = pl.ds(pl.multiple_of(j * BLK, BLK), count * BLK)
            there = pl.ds(pl.multiple_of((base + j) * BLK, BLK), count * BLK)
            same = segk[there, :] == labels
            for p in range(pairs):
                keys = ref[here, first + p * BLK : first + (p + 1) * BLK]
                scores = jnp.where(same, nt(keys, qs[p]), masked_score)
                old = top[p : p + 1, :]
                new = jnp.maximum(old, jnp.max(scores, axis=0, keepdims=True))
                expo = jnp.exp(scores - new)
                scale = jnp.exp(old - new)
                top[p : p + 1, :] = new
                total[p : p + 1, :] = total[p : p + 1, :] * scale + jnp.sum(expo, axis=0, keepdims=True)
                weights = expo.astype(bf16)
                for h in range(2):
                    values = beside(vt, base + j, count, slice(p * BLK + h * half, p * BLK + (h + 1) * half))
                    part = slice(h * half, (h + 1) * half)
                    cols = slice(h * BLK, (h + 1) * BLK)
                    acc[p, part, :] = acc[p, part, :] * scale[:, cols] + nn(values, weights[:, cols])

        each_block(functools.partial(k_block, qkv, width, 0), bounds[i, 0], bounds[i, 1])
        each_block(functools.partial(k_block, kvh, 0, own_blocks), bounds[i, 2], bounds[i, 3])
        for p in range(pairs):
            inverse = 1.0 / total[p : p + 1, :]
            flat = jnp.concatenate(
                [acc[p, :half, :] * inverse[:, :BLK], acc[p, half:, :] * inverse[:, BLK:]], axis=0
            )
            rounded = flat.astype(bf16)
            ctx_t[p * BLK : (p + 1) * BLK, rows] = flat
            ctx_low[p * BLK : (p + 1) * BLK, rows] = rounded
            ctx[rows, p * BLK : (p + 1) * BLK] = rounded.T
        lse[i] = top[...] + jnp.log(total[...])
        return carry

    lax.fori_loop(0, own_blocks, q_block, 0)


def attend_back_kernel(
    pairs, own_blocks, halo_blocks,
    bounds, segq, segk, qkv, kvh, ctx_t, lse, dctx, norm_sums, up_sum,
    dqkv, dkvh, sums,
    kt, qs, cs, delta, dqt, dk, dv,
):
    width = pairs * BLK
    low = head_masks()
    half = BLK // 2
    blocks = own_blocks + halo_blocks
    for j in range(blocks):
        for p in range(pairs):
            if j < own_blocks:
                tile = qkv[j * BLK : (j + 1) * BLK, width + p * BLK : width + (p + 1) * BLK]
            else:
                at = j - own_blocks
                tile = kvh[at * BLK : (at + 1) * BLK, p * BLK : (p + 1) * BLK]
            kt[j, p * BLK : (p + 1) * BLK, :] = tile.T
    dk[...] = jnp.zeros(dk.shape, f32)
    dv[...] = jnp.zeros(dv.shape, f32)
    sums[...] = jnp.zeros(sums.shape, f32)
    sums[0:8, :] = norm_sums[...]
    for at in range(up_sum.shape[1] // width):
        sums[8 + at : 9 + at, :] = up_sum[:, at * width : (at + 1) * width]

    def q_block(i, carry):
        rows = pl.ds(pl.multiple_of(i * BLK, BLK), BLK)
        for p in range(pairs):
            cols = slice(p * BLK, (p + 1) * BLK)
            qs[p] = stack_heads(qkv[rows, cols], low)
            pull = dctx[rows, cols]
            cs[p] = stack_heads(pull, low)
            prod = pull.T.astype(f32) * ctx_t[cols, rows]
            delta[p : p + 1, :] = jnp.concatenate(
                [jnp.sum(prod[:half], axis=0, keepdims=True), jnp.sum(prod[half:], axis=0, keepdims=True)], axis=1
            )
        dqt[...] = jnp.zeros(dqt.shape, f32)
        labels = segq[i]

        def k_block(ref, first, base, j, count):
            here = pl.ds(pl.multiple_of(j * BLK, BLK), count * BLK)
            there = pl.ds(pl.multiple_of((base + j) * BLK, BLK), count * BLK)
            same = segk[there, :] == labels
            for p in range(pairs):
                cols = slice(p * BLK, (p + 1) * BLK)
                keys = ref[here, first + p * BLK : first + (p + 1) * BLK]
                values = ref[here, first + width + p * BLK : first + width + (p + 1) * BLK]
                scores = jnp.where(same, nt(keys, qs[p]), masked_score)
                probs = jnp.exp(scores - lse[i, p : p + 1, :])
                pulls = nt(values, cs[p])
                dscore = (probs * (pulls - delta[p : p + 1, :])).astype(bf16)
                dv[there, cols] += nn(probs.astype(bf16), cs[p])
                dk[there, cols] += nn(dscore, qs[p])
                for h in range(2):
                    part = slice(h * half, (h + 1) * half)
                    flip = beside(kt, base + j, count, slice(p * BLK + h * half, p * BLK + (h + 1) * half))
                    dqt[p, part, :] += nn(flip, dscore[:, h * BLK : (h + 1) * BLK])

        all_blocks(functools.partial(k_block, qkv, width, 0), bounds[i, 0], bounds[i, 1], own_blocks)
        all_blocks(functools.partial(k_block, kvh, 0, own_blocks), bounds[i, 2], bounds[i, 3], halo_blocks)
        for p in range(pairs):
            cols = slice(p * BLK, (p + 1) * BLK)
            grad = dqt[p].astype(bf16).T * jnp.asarray(0.125, bf16)
            dqkv[rows, cols] = grad
            sums[6:7, cols] += jnp.sum(grad.astype(f32), axis=0, keepdims=True)
        return carry

    lax.fori_loop(0, own_blocks, q_block, 0)
    for j in range(blocks):
        rows = slice(j * BLK, (j + 1) * BLK)
        grad_k = dk[rows, :].astype(bf16)
        grad_v = dv[rows, :].astype(bf16)
        if j < own_blocks:
            dqkv[rows, width : 2 * width] = grad_k
            dqkv[rows, 2 * width :] = grad_v
        else:
            back = slice((j - own_blocks) * BLK, (j - own_blocks + 1) * BLK)
            dkvh[back, :width] = grad_k
            dkvh[back, width:] = grad_v
        sums[7:8, :] += jnp.sum(grad_v.astype(f32), axis=0, keepdims=True)


def vmem_specs(count):
    return [pl.BlockSpec(memory_space=pltpu.VMEM)] * count


def any_specs(count):
    return [pl.BlockSpec(memory_space=pl.ANY)] * count


def ordered_call(kernel, args, waits, passes, out_shape, in_specs, out_specs, **options):
    waits, passes = tuple(waits) + tuple(turn.last), tuple(passes)
    given, made = len(args), len(out_shape)
    skipped = len(waits) + len(passes)

    def body(*refs):
        outs = given + skipped
        refs[outs + made][...] = jnp.zeros((8, BLK), f32)
        kernel(*refs[:given], *refs[outs : outs + made], *refs[outs + made + 1 + len(passes) :])

    out = pl.pallas_call(
        body,
        out_shape=tuple(out_shape)
        + (jax.ShapeDtypeStruct((8, BLK), f32),)
        + tuple(jax.ShapeDtypeStruct(p.shape, p.dtype) for p in passes),
        in_specs=list(in_specs) + any_specs(skipped),
        out_specs=tuple(out_specs) + (pl.BlockSpec((8, BLK), lambda *step: (0, 0)),) + tuple(any_specs(len(passes))),
        input_output_aliases={given + len(waits) + k: made + 1 + k for k in range(len(passes))},
        **options,
    )(*args, *waits, *passes)
    turn.last = [out[made]]
    return out[:made], out[made + 1 :]


class Turn:
    last = []


turn = Turn()


def attend(bounds, segq, segk, qkv, kvh, waits, passes):
    tokens, width3 = qkv.shape
    width = width3 // 3
    pairs, own_blocks, halo_blocks = width // BLK, tokens // BLK, kvh.shape[0] // BLK
    blocks = own_blocks + halo_blocks
    return ordered_call(
        functools.partial(attend_kernel, pairs, own_blocks, halo_blocks),
        (bounds, segq, segk, qkv, kvh),
        waits,
        passes,
        out_shape=(
            jax.ShapeDtypeStruct((tokens, width), bf16),
            jax.ShapeDtypeStruct((width, tokens), f32),
            jax.ShapeDtypeStruct((width, tokens), bf16),
            jax.ShapeDtypeStruct((own_blocks, 8, 2 * BLK), f32),
        ),
        in_specs=[pl.BlockSpec(memory_space=pltpu.SMEM)] + vmem_specs(4),
        out_specs=tuple(vmem_specs(4)),
        scratch_shapes=[
            pltpu.VMEM((blocks, width, BLK), bf16),
            pltpu.VMEM((pairs, 2 * BLK, BLK), bf16),
            pltpu.VMEM((8, 2 * BLK), f32),
            pltpu.VMEM((8, 2 * BLK), f32),
            pltpu.VMEM((pairs, BLK, BLK), f32),
        ],
        compiler_params=pltpu.CompilerParams(vmem_limit_bytes=16 * 2**20),
        cost_estimate=cost(9),
        name="attend",
    )


def attend_back(bounds, segq, segk, qkv, kvh, ctx_t, lse, dctx, norm_sums, up_sum, waits, passes):
    tokens, width3 = qkv.shape
    width = width3 // 3
    pairs, own_blocks, halo_blocks = width // BLK, tokens // BLK, kvh.shape[0] // BLK
    blocks = own_blocks + halo_blocks
    return ordered_call(
        functools.partial(attend_back_kernel, pairs, own_blocks, halo_blocks),
        (bounds, segq, segk, qkv, kvh, ctx_t, lse, dctx, norm_sums, up_sum),
        waits,
        passes,
        out_shape=(
            jax.ShapeDtypeStruct((tokens, width3), bf16),
            jax.ShapeDtypeStruct(kvh.shape, bf16),
            jax.ShapeDtypeStruct((16, width), f32),
        ),
        in_specs=[pl.BlockSpec(memory_space=pltpu.SMEM)] + vmem_specs(9),
        out_specs=tuple(vmem_specs(3)),
        scratch_shapes=[
            pltpu.VMEM((blocks, width, BLK), bf16),
            pltpu.VMEM((pairs, 2 * BLK, BLK), bf16),
            pltpu.VMEM((pairs, 2 * BLK, BLK), bf16),
            pltpu.VMEM((8, 2 * BLK), f32),
            pltpu.VMEM((pairs, BLK, BLK), f32),
            pltpu.VMEM((blocks * BLK, width), f32),
            pltpu.VMEM((blocks * BLK, width), f32),
        ],
        compiler_params=pltpu.CompilerParams(vmem_limit_bytes=24 * 2**20),
        cost_estimate=cost(21),
        name="attend_back",
    )


CHUNK = 1024
ROWS = 256


def normalized(rows):
    center = rows - jnp.mean(rows, axis=-1, keepdims=True)
    spread = jnp.mean(center * center, axis=-1, keepdims=True)
    scale = lax.rsqrt(spread + norm_eps)
    return center * scale, scale


def feed_kernel(last, tokens, hidden, ctx, w_out, vec, w_up, up_bias, w_down, *rest):
    if last:
        first_rows, first_t, active_t, slope, second_rows, low, low_rows, first, total = rest
    else:
        first_rows, first_t, active_t, slope, second_rows, low, after, low_t, low_rows, first, total = rest
    step = pl.program_id(0)
    tiles = [slice(at, at + BLK) for at in range(0, tokens, BLK)]
    passes = [slice(at, at + ROWS) for at in range(0, tokens, ROWS)]

    @pl.when(step == 0)
    def _():
        for rows in tiles:
            resid = hidden[rows, :].astype(f32) + (nn(ctx[rows, :], w_out[...]) + vec[0:1, :])
            first_rows[rows, :] = resid
            unit, _ = normalized(resid)
            value = unit * vec[1:2, :] + vec[2:3, :]
            first[rows, :] = value
            total[rows, :] = jnp.zeros_like(value)
            rounded = value.astype(bf16)
            low_rows[rows, :] = rounded
            first_t[:, rows] = rounded.T

    for rows in passes:
        upward = nn(low_rows[rows, :], w_up[...]) + up_bias[...]
        density = jnp.exp(-0.5 * upward * upward) * 0.3989422804014327
        below = 0.5 + 0.5 * lax.erf(upward * 0.7071067811865476)
        active = (upward * below).astype(bf16)
        slope[rows, :] = below + upward * density
        active_t[:, rows] = active.T
        total[rows, :] += nn(active, w_down[...])

    @pl.when(step == pl.num_programs(0) - 1)
    def _():
        for rows in tiles:
            resid = first[rows, :] + (total[rows, :] + vec[3:4, :])
            second_rows[rows, :] = resid
            unit, _ = normalized(resid)
            value = unit * vec[4:5, :] + vec[5:6, :]
            rounded = value.astype(bf16)
            low[rows, :] = rounded
            if not last:
                after[rows, :] = value
                low_t[:, rows] = rounded.T


def whole(shape):
    return pl.BlockSpec(shape, lambda step: (0,) * len(shape))


def feed(last, layer_idx, hidden, ctx, w_out, vec, w_up, up_bias, w_down, waits, passes):
    tokens, width = hidden.shape
    wide = w_up.shape[-1]
    rows = whole((tokens, width))
    shapes = [
        jax.ShapeDtypeStruct((tokens, width), f32),
        jax.ShapeDtypeStruct((width, tokens), bf16),
        jax.ShapeDtypeStruct((wide, tokens), bf16),
        jax.ShapeDtypeStruct((tokens, wide), f32),
        jax.ShapeDtypeStruct((tokens, width), f32),
        jax.ShapeDtypeStruct((tokens, width), bf16),
    ]
    specs = [
        rows,
        whole((width, tokens)),
        pl.BlockSpec((CHUNK, tokens), lambda step: (step, 0)),
        pl.BlockSpec((tokens, CHUNK), lambda step: (0, step)),
        rows,
        rows,
    ]
    if not last:
        shapes.append(jax.ShapeDtypeStruct((tokens, width), f32))
        shapes.append(jax.ShapeDtypeStruct((width, tokens), bf16))
        specs.append(rows)
        specs.append(whole((width, tokens)))
    return ordered_call(
        functools.partial(feed_kernel, last, tokens),
        (hidden, ctx, w_out, vec, w_up, up_bias, w_down),
        waits,
        passes,
        grid=(wide // CHUNK,),
        out_shape=tuple(shapes),
        in_specs=[
            rows,
            rows,
            pl.BlockSpec((None, width, width), lambda step: (layer_idx, 0, 0)),
            whole(vec.shape),
            pl.BlockSpec((None, width, CHUNK), lambda step: (layer_idx, 0, step)),
            pl.BlockSpec((1, CHUNK), lambda step: (0, step)),
            pl.BlockSpec((None, CHUNK, width), lambda step: (layer_idx, step, 0)),
        ],
        out_specs=tuple(specs),
        scratch_shapes=[
            pltpu.VMEM((tokens, width), bf16),
            pltpu.VMEM((tokens, width), f32),
            pltpu.VMEM((tokens, width), f32),
        ],
        compiler_params=pltpu.CompilerParams(vmem_limit_bytes=30 * 2**20),
        cost_estimate=cost(15),
        name="feed",
    )


def norm_back(grad, gain, rows):
    unit, scale = normalized(rows)
    lifted = grad * gain
    first = jnp.mean(lifted, axis=-1, keepdims=True)
    second = jnp.mean(lifted * unit, axis=-1, keepdims=True)
    return scale * (lifted - first - unit * second), unit


def over_rows(value):
    return jnp.sum(value, axis=0, keepdims=True)


def feed_back_kernel(
    tokens, grad, back, edge, second_rows, first_rows, slope, w_down, w_up, w_out, vec,
    dz, du, da, dr, dc, sums, up_sum, dr_two, total,
):
    step = pl.program_id(0)
    tiles = [slice(at, at + BLK) for at in range(0, tokens, BLK)]
    passes = [slice(at, at + ROWS) for at in range(0, tokens, ROWS)]

    @pl.when(step == 0)
    def _():
        sums[...] = jnp.zeros(sums.shape, f32)
        for rows in tiles:
            pull = grad[rows, :].astype(f32)
            if back.shape[0] > BLK:
                at = rows.start - edge[0]
                inside = (at >= 0) & (at < back.shape[0])
                here = pl.ds(pl.multiple_of(jnp.where(inside, at, 0), BLK), BLK)
                pull = pull + jnp.where(inside, back[here, :].astype(f32), 0.0)
            value, unit = norm_back(pull, vec[4:5, :], second_rows[rows, :])
            dr_two[rows, :] = value
            total[rows, :] = jnp.zeros_like(value)
            rounded = value.astype(bf16)
            dz[rows, :] = rounded
            sums[3:4, :] += over_rows(rounded.astype(f32))
            sums[4:5, :] += over_rows(pull * unit)
            sums[5:6, :] += over_rows(pull)

    up_sum[...] = jnp.zeros(up_sum.shape, f32)
    for rows in passes:
        pull = (nt(dz[rows, :], w_down[...]) * slope[rows, :]).astype(bf16)
        du[rows, :] = pull
        up_sum[...] += over_rows(pull.astype(f32))
        total[rows, :] += nt(pull, w_up[...])

    @pl.when(step == pl.num_programs(0) - 1)
    def _():
        for rows in tiles:
            pull = total[rows, :] + dr_two[rows, :]
            value, unit = norm_back(pull, vec[1:2, :], first_rows[rows, :])
            dr[rows, :] = value
            rounded = value.astype(bf16)
            da[rows, :] = rounded
            sums[0:1, :] += over_rows(rounded.astype(f32))
            sums[1:2, :] += over_rows(pull * unit)
            sums[2:3, :] += over_rows(pull)
            dc[rows, :] = nt(rounded, w_out[...]).astype(bf16)


def feed_back(layer_idx, grad, back, edge, second_rows, first_rows, slope, w_down, w_up, w_out, vec, waits, passes):
    tokens, width = grad.shape
    wide = w_up.shape[-1]
    rows = whole((tokens, width))
    return ordered_call(
        functools.partial(feed_back_kernel, tokens),
        (grad, back, edge, second_rows, first_rows, slope, w_down, w_up, w_out, vec),
        waits,
        passes,
        grid=(wide // CHUNK,),
        out_shape=(
            jax.ShapeDtypeStruct((tokens, width), bf16),
            jax.ShapeDtypeStruct((tokens, wide), bf16),
            jax.ShapeDtypeStruct((tokens, width), bf16),
            jax.ShapeDtypeStruct((tokens, width), f32),
            jax.ShapeDtypeStruct((tokens, width), bf16),
            jax.ShapeDtypeStruct((8, width), f32),
            jax.ShapeDtypeStruct((1, wide), f32),
        ),
        in_specs=[
            rows,
            whole(back.shape),
            pl.BlockSpec(memory_space=pltpu.SMEM),
            rows,
            rows,
            pl.BlockSpec((tokens, CHUNK), lambda step: (0, step)),
            pl.BlockSpec((None, CHUNK, width), lambda step: (layer_idx, step, 0)),
            pl.BlockSpec((None, width, CHUNK), lambda step: (layer_idx, 0, step)),
            pl.BlockSpec((None, width, width), lambda step: (layer_idx, 0, 0)),
            whole(vec.shape),
        ],
        out_specs=(
            rows,
            pl.BlockSpec((tokens, CHUNK), lambda step: (0, step)),
            rows,
            rows,
            rows,
            whole((8, width)),
            pl.BlockSpec((1, CHUNK), lambda step: (0, step)),
        ),
        scratch_shapes=[pltpu.VMEM((tokens, width), f32), pltpu.VMEM((tokens, width), f32)],
        compiler_params=pltpu.CompilerParams(vmem_limit_bytes=30 * 2**20),
        cost_estimate=cost(17),
        name="feed_back",
    )


def grad_down_kernel(core, active_t, dz, send, keep):
    groups, head, parts, thin, width = send.shape
    mine = core[0]
    for which, out in ((1 - mine, send), (mine, keep)):
        for group in range(groups):
            value = nn(active_t[2 * group + which], dz[...])
            for shard in range(head):
                for at in range(parts):
                    here = (shard * parts + at) * thin
                    out[group, shard, at] = value[here : here + thin].astype(bf16)


def grad_up_kernel(core, first_t, du, send, keep, lhs):
    groups, head, parts, thin, width = send.shape
    rows = head * thin
    mine = core[0]
    for which, out in ((1 - mine, send), (mine, keep)):
        if rows % 16 == 0:
            for group in range(groups):
                lhs[group * rows : (group + 1) * rows, :] = first_t[2 * group + which]
        for at in range(parts):
            pulls = du[:, at * width : (at + 1) * width]
            if rows % 16 == 0:
                value = nn(lhs[...], pulls)
                values = [value[group * rows : (group + 1) * rows] for group in range(groups)]
            else:
                values = [nn(first_t[2 * group + which], pulls) for group in range(groups)]
            for group in range(groups):
                for shard in range(head):
                    out[group, shard, at] = values[group][shard * thin : (shard + 1) * thin].astype(bf16)


def grad_feed(core, left_t, right, parts, devices, head, scratch):
    rows, tokens = left_t.shape
    thin = rows // devices // head // (1 if scratch else parts)
    width = right.shape[1] // (parts if scratch else 1)
    out = jax.ShapeDtypeStruct((devices // 2, head, parts, thin, width), bf16)
    halves, _ = ordered_call(
        grad_up_kernel if scratch else grad_down_kernel,
        (core, left_t.reshape(devices, rows // devices, tokens), right),
        (),
        (),
        out_shape=(out, out),
        in_specs=[pl.BlockSpec(memory_space=pltpu.SMEM)] + vmem_specs(2),
        out_specs=tuple(vmem_specs(2)),
        scratch_shapes=[pltpu.VMEM((rows // 2, tokens), bf16)] if scratch else [],
        compiler_params=pltpu.CompilerParams(vmem_limit_bytes=18 * 2**20),
        cost_estimate=cost(5),
        name="grad_up" if scratch else "grad_down",
    )
    return halves


def grad_heads_kernel(core, ctx_t, low_t, halo_t, da, dqkv, dkvh, sums, send, keep, one, two, three):
    groups, thin = ctx_t.shape[0] // 2, ctx_t.shape[1]
    width = send.shape[2] // 4
    high = thin // TILE
    for r in range(sums.shape[0] // TILE):
        value = sums[r * TILE : (r + 1) * TILE, :].astype(bf16)
        for out in (send, keep):
            out[groups * high, :, r * width : (r + 1) * width] = value
    mine = core[0]
    for which, out in ((1 - mine, send), (mine, keep)):
        if thin % 16 == 0:
            for group in range(groups):
                here = slice(group * thin, (group + 1) * thin)
                one[here, :] = ctx_t[2 * group + which]
                two[here, :] = low_t[2 * group + which]
                three[here, :] = halo_t[2 * group + which]
            parts = [(range(groups), one, two, three)]
        else:
            parts = [
                ([group], ctx_t.at[2 * group + which], low_t.at[2 * group + which], halo_t.at[2 * group + which])
                for group in range(groups)
            ]
        for members, left_one, left_two, left_three in parts:
            for at in range(0, 4 * width, width):
                if at < width:
                    value = nn(left_one[...], da[...])
                else:
                    value = nn(left_two[...], dqkv[:, at - width : at])
                    if at >= 2 * width:
                        value = value + nn(left_three[...], dkvh[:, at - 2 * width : at - width])
                for place, group in enumerate(members):
                    here = value[place * thin : (place + 1) * thin].reshape(high, TILE, width)
                    out[group * high : (group + 1) * high, :, at : at + width] = here.astype(bf16)


def grad_heads(core, ctx_t, low_t, halo_t, da, dqkv, dkvh, sums, devices, waits, passes):
    tokens, width = da.shape
    thin = width // devices
    out = jax.ShapeDtypeStruct((devices // 2 * thin // TILE + 1, TILE, 4 * width), bf16)
    extent = halo_t.shape[1]
    return ordered_call(
        grad_heads_kernel,
        (
            core,
            ctx_t.reshape(devices, thin, tokens),
            low_t.reshape(devices, thin, tokens),
            halo_t.reshape(devices, thin, extent),
            da,
            dqkv,
            dkvh,
            sums,
        ),
        waits,
        passes,
        out_shape=(out, out),
        in_specs=[pl.BlockSpec(memory_space=pltpu.SMEM)] + vmem_specs(7),
        out_specs=tuple(vmem_specs(2)),
        scratch_shapes=[
            pltpu.VMEM((width // 2, tokens), bf16),
            pltpu.VMEM((width // 2, tokens), bf16),
            pltpu.VMEM((width // 2, extent), bf16),
        ],
        compiler_params=pltpu.CompilerParams(vmem_limit_bytes=20 * 2**20),
        cost_estimate=cost(8),
        name="grad_heads",
    )


def assemble_kernel(relative, place, own, *refs):
    *refs, out = refs
    shard, group = place[0], place[1]
    kinds = own.shape[0]
    out[:, pl.ds(shard, 1)] = own[...].reshape(kinds, 1, *own.shape[1:])
    lane = 0
    for ref, order in zip(refs, relative):
        lanes = slice(lane, lane + ref.shape[-1])
        lane = lanes.stop % own.shape[-1]
        for at, change in enumerate(order):
            for step in range(ref.shape[1]):
                for kind in range(kinds):
                    out[kind, shard ^ (step + 1), group ^ change, :, lanes] = ref[at, step, kind]


def assemble(relative, place, own, refs, passes):
    head = lax.axis_size("head")
    (out,), passed = ordered_call(
        functools.partial(assemble_kernel, relative),
        (place, own, *refs),
        (),
        passes,
        out_shape=(jax.ShapeDtypeStruct((own.shape[0], head) + own.shape[1:], bf16),),
        in_specs=[pl.BlockSpec(memory_space=pltpu.SMEM)] + vmem_specs(1 + len(refs)),
        out_specs=vmem_specs(1),
        compiler_params=pltpu.CompilerParams(vmem_limit_bytes=16 * 2**20),
        cost_estimate=cost(1.5),
        name="assemble",
    )
    return out, passed


def grow(value, order):
    value, relative = value[None], [0]
    for place in order:
        value = jnp.concatenate([value, swap(value, "dp", 1 << place)], axis=0)
        relative = relative + [other ^ (1 << place) for other in relative]
    return value, relative


def flip_kernel(count, shard, biases, *refs):
    for source, target in zip(refs[:count], refs[count : 2 * count]):
        for at in range(0, source.shape[0], BLK):
            target[:, at : at + BLK] = source[at : at + BLK, :].T
    shifts = refs[2 * count]
    members, _, width = biases.shape
    layers, part = shifts.shape[0], width // members
    shifts[...] = jnp.zeros(shifts.shape, f32)
    rows = [biases[step].astype(f32) for step in range(members)]
    for member in range(members):
        value = jnp.zeros((1, width), f32)
        for step, row in enumerate(rows):
            value = jnp.where((shard[0] ^ step) == member, row, value)
        for layer_idx in range(layers):
            for at, kind in ((0, 0), (1, 2)):
                here = (2 * layer_idx + at) * part
                there = kind * width + member * part
                shifts[layer_idx, :, there : there + part] = value[:, here : here + part]


def flip(values, shard, biases, layers):
    width = biases.shape[2]
    shapes = [jax.ShapeDtypeStruct(v.shape[::-1], v.dtype) for v in values]
    return ordered_call(
        functools.partial(flip_kernel, len(values)),
        (shard, biases, *values),
        (),
        (),
        out_shape=shapes + [jax.ShapeDtypeStruct((layers, 1, 3 * width), f32)],
        in_specs=[pl.BlockSpec(memory_space=pltpu.SMEM)] + vmem_specs(1 + len(values)),
        out_specs=vmem_specs(1 + len(values)),
        compiler_params=pltpu.CompilerParams(vmem_limit_bytes=8 * 2**20),
        cost_estimate=cost(1.5),
        name="flip",
    )


def collect_kernel(*refs):
    *parts, out = refs
    for k, ref in enumerate(parts):
        out[k] = ref[...]


def collect(values):
    (out,), _ = ordered_call(
        collect_kernel,
        values,
        (),
        (),
        out_shape=(jax.ShapeDtypeStruct((len(values),) + values[0].shape, values[0].dtype),),
        in_specs=vmem_specs(len(values)),
        out_specs=vmem_specs(1),
        compiler_params=pltpu.CompilerParams(vmem_limit_bytes=8 * 2**20),
        cost_estimate=cost(1.4),
        name="collect",
    )
    return out


def from_heads_in_turn(piece):
    got = [swap(piece, "head", 1)]
    step = 2
    while step < lax.axis_size("head"):
        far = [swap(value, "head", step) for value in [piece]]
        for value in far:
            got = got + [value, swap(value, "head", 1)]
        step *= 2
    return got


def from_heads(piece):
    return [swap(piece, "head", step) for step in range(1, lax.axis_size("head"))]


def added(keep, got):
    return keep.astype(f32) + got.astype(f32)


def advance_kernel(counts, size, tail, sources, scalars, *refs):
    core, mine = scalars[0], scalars[1]
    keeps, gots, (send, out) = refs[:sources], refs[sources : 2 * sources], refs[2 * sources :]
    blocks = (keeps[0].shape[0] - tail) // size
    for target, which in ((send, 1 - mine), (out, mine)):
        for k in range(blocks // 2):
            spots = [2 * (k // after) * after + k % after for after in counts]
            at = jnp.where(core == 0, spots[0] + which * counts[0], spots[1] + which * counts[1])
            here = pl.ds(at * size, size)
            for source, (keep, got) in enumerate(zip(keeps, gots)):
                value = added(keep[here], got[here]).astype(bf16)
                if sources > 1:
                    target[k * size : (k + 1) * size, source] = value
                else:
                    target[k * size : (k + 1) * size] = value
        if tail:
            value = added(keeps[0][blocks * size :], gots[0][blocks * size :]).astype(bf16)
            target[blocks // 2 * size :] = value


def turn_heads_kernel(head, scalars, keep, got, send, out):
    mine = scalars[1]
    tiles, _, columns = keep.shape
    rows, width = (tiles - 1) * TILE, columns // 4
    held = added(keep[: tiles - 1], got[: tiles - 1]).reshape(rows, columns)
    part, thin = width // head, rows // head
    kinds = []
    if rows < BLK:
        filler = jnp.zeros((BLK - rows, width), f32)
    for kind in range(1, 4):
        value = held[:, kind * width : (kind + 1) * width]
        value = jnp.concatenate([value, filler], axis=0) if rows < BLK else value
        kinds.append(value.T)
    high = part // (width // BLK)
    count = part // TILE
    for shard in range(head):
        pieces = [value[shard * part : (shard + 1) * part] for value in kinds]
        own = held[shard * thin : (shard + 1) * thin, :width]
        own = jnp.concatenate([own, jnp.zeros((high - thin, width), f32)], axis=0)
        pieces.append(jnp.concatenate([own[:, at : at + BLK] for at in range(0, width, BLK)], axis=0))
        for chosen, target in ((1 - mine, send), (mine, out)):

            @pl.when(chosen == shard % 2)
            def _(target=target, pieces=pieces, shard=shard):
                for kind, piece in enumerate(pieces):
                    at = (shard // 2 * 4 + kind) * count
                    target[at : at + count] = piece.reshape(count, TILE, BLK).astype(bf16)

    last = added(keep[tiles - 1], got[tiles - 1])
    for target in (send, out):
        for k in range(2 * width // BLK):
            target[head // 2 * 4 * count + k] = last[:, k * BLK : (k + 1) * BLK].astype(bf16)


class Flight:
    def __init__(self, keeps, gots, turned):
        dp, head = lax.axis_size("dp"), lax.axis_size("head")
        bits = dp.bit_length() - 1
        upper = list(range(1, bits))
        self.orders = [list(upper), list(upper)[::-1]]
        self.left = [upper[::-1], upper[::-1]]
        self.head_bits = list(range(head.bit_length() - 1))
        self.turned = turned
        self.tail, self.size = 0, 1
        if turned:
            self.tail, self.size = 1, (keeps[0].shape[0] - 1) // (dp // 2)
        else:
            shape = (keeps[0].shape[0] * keeps[0].shape[1],) + keeps[0].shape[2:]
            keeps, gots = [k.reshape(shape) for k in keeps], [g.reshape(shape) for g in gots]
        self.keeps, self.gots = list(keeps), list(gots)

    def step(self, waits=(), passes=()):
        blocks = (self.keeps[0].shape[0] - self.tail) // self.size
        sources = len(self.keeps)
        core = bit_of("dp", 0)
        rest = self.keeps[0].shape[1:]
        if sources > 1:
            rest = (sources,) + rest
        devices = lax.axis_size("dp")
        counts = [1, 1]
        if self.orders[0]:
            places = [order.pop(0) for order in self.orders]
            counts = []
            for left, place in zip(self.left, places):
                axis = left.index(place)
                left.remove(place)
                counts.append((blocks // 2) >> axis)
            mine = jnp.where(core == 0, bit_of("dp", places[0]), bit_of("dp", places[1]))
            axis_name, pairs = "dp", [(i, i ^ (1 << places[i & 1])) for i in range(devices)]
        else:
            place = self.head_bits.pop(0)
            mine = bit_of("head", place)
            head = lax.axis_size("head")
            axis_name, pairs = "head", [(i, i ^ (1 << place)) for i in range(head)]
        if axis_name == "head" and self.turned:
            width = rest[1] // 4
            self.turned = False
            self.size, self.tail = 4 * (width // head) // TILE, 2 * width // BLK
            out_shape = (head // 2 * self.size + self.tail, TILE, BLK)
            kernel = functools.partial(turn_heads_kernel, head)
        else:
            out_shape = (blocks // 2 * self.size + self.tail,) + rest
            kernel = functools.partial(advance_kernel, counts, self.size, self.tail, sources)
        out = jax.ShapeDtypeStruct(out_shape, bf16)
        (send, keep), passed = ordered_call(
            kernel,
            (jnp.stack([core, mine]).astype(jnp.int32), *self.keeps, *self.gots),
            waits,
            passes,
            out_shape=[out] * 2,
            in_specs=[pl.BlockSpec(memory_space=pltpu.SMEM)] + vmem_specs(2 * sources),
            out_specs=vmem_specs(2),
            compiler_params=pltpu.CompilerParams(vmem_limit_bytes=20 * 2**20),
            cost_estimate=cost(1 + 2e-6 * out.size),
            name="advance",
        )
        self.keeps, self.gots = [keep], [lax.ppermute(send, axis_name, pairs)]
        return passed

    def finish(self):
        while self.orders[0] or self.head_bits:
            self.step()
        total = added(self.keeps[0], self.gots[0])
        return total if self.tail else total[0]


def per_device(
    tokens_in,
    segment,
    w_qkv,
    qv_bias,
    w_out,
    out_bias,
    ln1_gain,
    ln1_bias,
    w_up,
    up_bias,
    w_down,
    down_bias,
    ln2_gain,
    ln2_bias,
    cotangent,
):
    turn.last = []
    layers, width = w_qkv.shape[0], w_qkv.shape[1]
    part = w_qkv.shape[3] * w_qkv.shape[4]
    head_size = w_qkv.shape[4]
    tokens = tokens_in.shape[0]
    seq = segment.shape[1]
    dp, head = lax.axis_size("dp"), lax.axis_size("head")
    bits = dp.bit_length() - 1
    shard, group = lax.axis_index("head"), lax.axis_index("dp")
    halves = seq // tokens
    row, half = shard // halves, shard % halves
    upper = list(range(1, bits))

    edge = jnp.where(half == 0, tokens - HALO, 0)
    core = bit_of("dp", 0)

    own_w = w_qkv.transpose(0, 2, 3, 4, 1).reshape(layers, 3, part, width)
    own_first = own_w[0].reshape(3, dp, part // dp, width)
    piece = pick(own_first, group, 1).reshape(-1, width)
    rows_w = piece.shape[0]
    bias_own = qv_bias.reshape(1, layers * 2 * part)
    bias_own = jnp.pad(bias_own, ((0, 7), (0, width - bias_own.shape[1])))
    piece = jnp.concatenate([piece, bias_own])
    got = from_heads(piece)
    halo = swap(lax.dynamic_slice_in_dim(tokens_in, edge, HALO), "head", 1)
    biases = jnp.stack([other[rows_w : rows_w + 1] for other in [piece] + got])
    got = jnp.stack([other[:rows_w] for other in got]).reshape(head - 1, 3, part // dp, width)
    left, relative_left = grow(got[..., : width // 2], upper)
    right, relative_right = grow(got[..., width // 2 :], upper[::-1])
    both = jnp.stack([left, right])
    both = jnp.concatenate([both, swap(both, "dp", 1)], axis=1)
    relative = [order + [other ^ 1 for other in order] for order in (relative_left, relative_right)]
    place = jnp.stack([shard, group]).astype(jnp.int32)
    own_later = [own_w[k].reshape(3, 2, part // 2, width) for k in range(1, layers)]
    (low_t, halo_t, shifts), _ = flip([tokens_in, halo], shard.reshape(1).astype(jnp.int32), biases, layers)
    w_first, pieces = assemble(relative, place, own_first, [both[0], both[1]], [pick(own, core, 1) for own in own_later])
    later_got = [from_heads_in_turn(value) for value in pieces]
    w_cats = [w_first.reshape(3 * head * part, width)]

    def later_weights(own, got):
        theirs = swap(got, "dp", 1)
        whole = assemble([[0], [1]], jnp.stack([shard, core]).astype(jnp.int32), own, [got[None], theirs[None]], [])[0]
        return whole.reshape(3 * head * part, width)

    labels = pick(segment, row, 0)
    own_labels = lax.dynamic_slice_in_dim(labels, half * tokens, tokens)
    halo_start = jnp.where(half == 0, tokens, tokens - HALO)
    halo_labels = lax.dynamic_slice_in_dim(labels, halo_start, HALO)
    blocks = tokens // BLK
    by_block = own_labels.reshape(blocks, BLK)
    least, most = by_block[:, :1], by_block[:, -1:]

    def count(flags):
        return jnp.sum(flags.astype(jnp.int32), axis=1)

    bounds = jnp.stack(
        [
            count(own_labels[None] < least) // BLK,
            (count(own_labels[None] <= most) + BLK - 1) // BLK,
            count(halo_labels[None] < least) // BLK,
            (count(halo_labels[None] <= most) + BLK - 1) // BLK,
        ],
        axis=1,
    )
    segq = jnp.concatenate([by_block, by_block], axis=1).reshape(blocks, 1, 2 * BLK)
    segk = jnp.concatenate([own_labels, halo_labels]).reshape(-1, 1)
    core_at = core.reshape(1).astype(jnp.int32)

    vecs = jnp.stack(
        [out_bias, ln1_gain, ln1_bias, down_bias, ln2_gain, ln2_bias, out_bias, out_bias], axis=1
    ).astype(f32)
    up_bias_wide = up_bias.astype(f32)

    hidden, low = tokens_in, tokens_in
    saved = []
    for layer_idx in range(layers):
        last = layer_idx == layers - 1
        w_cat = w_cats[layer_idx]
        shift = shifts[layer_idx]
        factor = jnp.where(jnp.arange(3 * width) < width, 0.125, 1.0).astype(f32)
        qkv = ((nt(low, w_cat) + shift) * factor).astype(bf16)
        kvh = (nt(halo, w_cat[width:]) + shift[:, width:]).astype(bf16)
        (ctx, ctx_t, ctx_low, lse), _ = attend(bounds, segq, segk, qkv, kvh, (), ())
        fed, _ = feed(
            last, layer_idx, hidden, ctx, w_out, vecs[layer_idx], w_up, up_bias_wide[layer_idx : layer_idx + 1], w_down, (), ()
        )
        first_rows, first_t, active_t, slope, second_rows, after_low = fed[:6]
        saved.append((low_t, halo_t, qkv, kvh, ctx_t, ctx_low, lse, first_rows, first_t, active_t, slope, second_rows))
        if last:
            output = after_low
        else:
            low, hidden, low_t = after_low, fed[6], fed[7]
            halo = swap(lax.dynamic_slice_in_dim(low, edge, HALO), "head", 1)
            halo_t = halo.T
            w_cats.append(later_weights(own_later[layer_idx], collect(later_got[layer_idx])))

    grad_hidden, back = cotangent, jnp.zeros((BLK, width), bf16)
    flights = []
    for layer_idx in reversed(range(layers)):
        low_t, halo_t, qkv, kvh, ctx_t, ctx_low, lse, first_rows, first_t, active_t, slope, second_rows = saved[layer_idx]
        w_cat = w_cats[layer_idx]
        (dz, du, da, dr, dc, sums, up_sum), _ = feed_back(
            layer_idx, grad_hidden, back, edge.reshape(1).astype(jnp.int32), second_rows, first_rows, slope, w_down, w_up, w_out, vecs[layer_idx], (), ()
        )
        if flights:
            flights[1].step()
            flights[0].step()
        parts = du.shape[1] // width
        down_send, down_keep = grad_feed(core_at, active_t, dz, parts, dp, head, False)
        down_got = swap(down_send, "dp", 1)
        up_send, up_keep = grad_feed(core_at, first_t, du, parts, dp, head, True)
        up_got = swap(up_send, "dp", 1)
        fed = Flight([down_keep, up_keep], [down_got, up_got], False)
        fed.step()
        (dqkv, dkvh, sums), _ = attend_back(bounds, segq, segk, qkv, kvh, ctx_t, lse, dc, sums, up_sum, (), ())
        part_halo = nn(dkvh, w_cat[width:]).astype(bf16)
        back = swap(part_halo, "head", 1)
        if flights:
            flights[1].step()
            flights[0].step()
        (send, keep), _ = grad_heads(core_at, ctx_low, low_t, halo_t, da, dqkv, dkvh, sums, dp, (part_halo,), ())
        heads = Flight([keep], [swap(send, "dp", 1)], True)
        grad_hidden = nn(dqkv, w_cat) + dr
        fed.step()
        if flights:
            flights[1].step()
            heads.step()
            fed.step()
            heads.step()
            fed.step()
            heads.step()
            flights[1].step()
            first, second = flights
            passed = heads.step(passes=(first.keeps[0], second.keeps[0]))
            first.keeps, second.keeps = [passed[0]], [passed[1]]
        flights = flights + [fed, heads]

    padded = lax.dynamic_update_slice(jnp.zeros((tokens, width), bf16), back, (edge, 0))
    grad_hidden = grad_hidden + padded.astype(f32)

    results = []
    for place in range(layers):
        fed, heads = flights[2 * place], flights[2 * place + 1]
        thin = width // (dp * head)
        total = fed.finish()
        out_down = total[0].reshape(-1, width)
        out_up = total[1].transpose(1, 0, 2).reshape(thin, -1)
        total = heads.finish()
        pieces = total[: 4 * part // TILE].reshape(4, part, BLK)
        out_out = pieces[3].reshape(width // BLK, -1, BLK)[:, :thin].transpose(1, 0, 2).reshape(thin, width)
        sums = total[4 * part // TILE :].transpose(1, 0, 2).reshape(TILE, 2, width).transpose(1, 0, 2)
        results.append((pieces[:3, :, : width // dp], out_out, out_up, out_down, sums.reshape(2 * TILE, width)))
    results = results[::-1]
    out_qkv, out_w_out, out_up, out_down, total = (jnp.stack([r[k] for r in results]) for k in range(5))
    out_qkv = out_qkv.reshape(layers, 3, part // head_size, head_size, -1).transpose(0, 4, 1, 2, 3)

    device = group * head + shard
    thin = width // (dp * head)
    mine = lax.dynamic_slice_in_dim(total[:, :6], device * thin, thin, axis=2)
    ups = total[:, 8 : 8 + up_bias.shape[1] // width].reshape(layers, -1)
    thick = ups.shape[1] // (dp * head)
    out_ups = lax.dynamic_slice_in_dim(ups, device * thick, thick, axis=1)
    qvs = total[:, 6:8].reshape(layers, 2, head, part // head_size, dp, head_size // dp)
    out_qv = pick(pick(qvs, shard, 2), group, 3)
    return (
        output,
        grad_hidden,
        out_qkv,
        out_qv,
        out_w_out,
        mine[:, 0],
        mine[:, 1],
        mine[:, 2],
        out_up,
        out_ups,
        out_down,
        mine[:, 3],
        mine[:, 4],
        mine[:, 5],
    )


def solution(mesh):
    return jax.shard_map(
        per_device,
        mesh=mesh,
        in_specs=(
            P(("dp", "head"), None),
            P("dp", None),
            P(None, None, None, "head", None),
            P(None, None, "head", None),
            P(),
            P(),
            P(),
            P(),
            P(),
            P(),
            P(),
            P(),
            P(),
            P(),
            P(("dp", "head"), None),
        ),
        out_specs=(
            P(("dp", "head"), None),
            P(("dp", "head"), None),
            P(None, "dp", None, "head", None),
            P(None, None, "head", "dp"),
            P(None, ("dp", "head"), None),
            P(None, ("dp", "head")),
            P(None, ("dp", "head")),
            P(None, ("dp", "head")),
            P(None, ("dp", "head"), None),
            P(None, ("dp", "head")),
            P(None, ("dp", "head"), None),
            P(None, ("dp", "head")),
            P(None, ("dp", "head")),
            P(None, ("dp", "head")),
        ),
        check_vma=False,
    )
```

```python
import functools

import jax
import jax.numpy as jnp
from jax import lax
from jax.experimental import pallas as pl
from jax.experimental.pallas import tpu as pltpu
from jax.sharding import PartitionSpec as P

norm_eps = 1e-06
masked_score = -1000000000.0
f32 = jnp.float32
bf16 = jnp.bfloat16

BLK = 128
TILE = 8
SCALE = 0.5
HALO = 384


def cost(microseconds):
    return pl.CostEstimate(flops=int(microseconds * SCALE * 1.15e9), bytes_accessed=1000, transcendentals=0)


def swap(value, axis, bit):
    size = lax.axis_size(axis)
    return lax.ppermute(value, axis, [(i, i ^ bit) for i in range(size)])


def bit_of(axis, place):
    return (lax.axis_index(axis) >> place) & 1


def pick(value, index, axis):
    return lax.dynamic_index_in_dim(value, index, axis, keepdims=False)


def add_low(*terms):
    total = terms[0].astype(f32)
    for term in terms[1:]:
        total = total + term.astype(f32)
    return total


def finish_head(slot):
    size = lax.axis_size("head")
    me = lax.axis_index("head")
    got = [swap(slot(me ^ step), "head", step) for step in range(1, size)]
    return add_low(slot(me), *got)


def head_masks():
    lane = lax.broadcasted_iota(jnp.int32, (BLK, BLK), 1)
    return lane < BLK // 2


def stack_heads(pair, low):
    zero = jnp.zeros_like(pair)
    return jnp.concatenate([jnp.where(low, pair, zero), jnp.where(low, zero, pair)], axis=0)


def nt(left, right):
    return lax.dot_general(left, right, (((1,), (1,)), ((), ())), preferred_element_type=f32)


def nn(left, right):
    return lax.dot_general(left, right, (((1,), (0,)), ((), ())), preferred_element_type=f32)


def each_block(step, low, high):
    def one(j, carry):
        step(j, 1)
        return carry

    lax.fori_loop(low, high, one, 0)


def all_blocks(step, low, high, most):
    for count in range(1, most + 1):

        @pl.when(high - low == count)
        def _(count=count):
            step(low, count)


def beside(ref, j, count, rows):
    return jnp.concatenate([ref[j + k, rows, :] for k in range(count)], axis=1)


def attend_kernel(pairs, own_blocks, halo_blocks, bounds, segq, segk, qkv, kvh, ctx, ctx_t, ctx_low, lse, vt, qs, top, total, acc):
    width = pairs * BLK
    low = head_masks()
    half = BLK // 2
    for j in range(own_blocks + halo_blocks):
        for p in range(pairs):
            if j < own_blocks:
                tile = qkv[j * BLK : (j + 1) * BLK, 2 * width + p * BLK : 2 * width + (p + 1) * BLK]
            else:
                at = j - own_blocks
                tile = kvh[at * BLK : (at + 1) * BLK, width + p * BLK : width + (p + 1) * BLK]
            vt[j, p * BLK : (p + 1) * BLK, :] = tile.T

    def q_block(i, carry):
        rows = pl.ds(pl.multiple_of(i * BLK, BLK), BLK)
        for p in range(pairs):
            qs[p] = stack_heads(qkv[rows, p * BLK : (p + 1) * BLK], low)
        top[...] = jnp.full(top.shape, -1e30, f32)
        total[...] = jnp.zeros(total.shape, f32)
        acc[...] = jnp.zeros(acc.shape, f32)
        labels = segq[i]

        def k_block(ref, first, base, j, count):
            here = pl.ds(pl.multiple_of(j * BLK, BLK), count * BLK)
            there = pl.ds(pl.multiple_of((base + j) * BLK, BLK), count * BLK)
            same = segk[there, :] == labels
            for p in range(pairs):
                keys = ref[here, first + p * BLK : first + (p + 1) * BLK]
                scores = jnp.where(same, nt(keys, qs[p]), masked_score)
                old = top[p : p + 1, :]
                new = jnp.maximum(old, jnp.max(scores, axis=0, keepdims=True))
                expo = jnp.exp(scores - new)
                scale = jnp.exp(old - new)
                top[p : p + 1, :] = new
                total[p : p + 1, :] = total[p : p + 1, :] * scale + jnp.sum(expo, axis=0, keepdims=True)
                weights = expo.astype(bf16)
                for h in range(2):
                    values = beside(vt, base + j, count, slice(p * BLK + h * half, p * BLK + (h + 1) * half))
                    part = slice(h * half, (h + 1) * half)
                    cols = slice(h * BLK, (h + 1) * BLK)
                    acc[p, part, :] = acc[p, part, :] * scale[:, cols] + nn(values, weights[:, cols])

        each_block(functools.partial(k_block, qkv, width, 0), bounds[i, 0], bounds[i, 1])
        each_block(functools.partial(k_block, kvh, 0, own_blocks), bounds[i, 2], bounds[i, 3])
        for p in range(pairs):
            inverse = 1.0 / total[p : p + 1, :]
            flat = jnp.concatenate(
                [acc[p, :half, :] * inverse[:, :BLK], acc[p, half:, :] * inverse[:, BLK:]], axis=0
            )
            rounded = flat.astype(bf16)
            ctx_t[p * BLK : (p + 1) * BLK, rows] = flat
            ctx_low[p * BLK : (p + 1) * BLK, rows] = rounded
            ctx[rows, p * BLK : (p + 1) * BLK] = rounded.T
        lse[i] = top[...] + jnp.log(total[...])
        return carry

    lax.fori_loop(0, own_blocks, q_block, 0)


def attend_back_kernel(
    pairs, own_blocks, halo_blocks,
    bounds, segq, segk, qkv, kvh, ctx_t, lse, dctx, norm_sums, up_sum,
    dqkv, dkvh, sums,
    kt, qs, cs, delta, dqt, dk, dv,
):
    width = pairs * BLK
    low = head_masks()
    half = BLK // 2
    blocks = own_blocks + halo_blocks
    for j in range(blocks):
        for p in range(pairs):
            if j < own_blocks:
                tile = qkv[j * BLK : (j + 1) * BLK, width + p * BLK : width + (p + 1) * BLK]
            else:
                at = j - own_blocks
                tile = kvh[at * BLK : (at + 1) * BLK, p * BLK : (p + 1) * BLK]
            kt[j, p * BLK : (p + 1) * BLK, :] = tile.T
    dk[...] = jnp.zeros(dk.shape, f32)
    dv[...] = jnp.zeros(dv.shape, f32)
    sums[...] = jnp.zeros(sums.shape, f32)
    sums[0:8, :] = norm_sums[...]
    for at in range(up_sum.shape[1] // width):
        sums[8 + at : 9 + at, :] = up_sum[:, at * width : (at + 1) * width]

    def q_block(i, carry):
        rows = pl.ds(pl.multiple_of(i * BLK, BLK), BLK)
        for p in range(pairs):
            cols = slice(p * BLK, (p + 1) * BLK)
            qs[p] = stack_heads(qkv[rows, cols], low)
            pull = dctx[rows, cols]
            cs[p] = stack_heads(pull, low)
            prod = pull.T.astype(f32) * ctx_t[cols, rows]
            delta[p : p + 1, :] = jnp.concatenate(
                [jnp.sum(prod[:half], axis=0, keepdims=True), jnp.sum(prod[half:], axis=0, keepdims=True)], axis=1
            )
        dqt[...] = jnp.zeros(dqt.shape, f32)
        labels = segq[i]

        def k_block(ref, first, base, j, count):
            here = pl.ds(pl.multiple_of(j * BLK, BLK), count * BLK)
            there = pl.ds(pl.multiple_of((base + j) * BLK, BLK), count * BLK)
            same = segk[there, :] == labels
            for p in range(pairs):
                cols = slice(p * BLK, (p + 1) * BLK)
                keys = ref[here, first + p * BLK : first + (p + 1) * BLK]
                values = ref[here, first + width + p * BLK : first + width + (p + 1) * BLK]
                scores = jnp.where(same, nt(keys, qs[p]), masked_score)
                probs = jnp.exp(scores - lse[i, p : p + 1, :])
                pulls = nt(values, cs[p])
                dscore = (probs * (pulls - delta[p : p + 1, :])).astype(bf16)
                dv[there, cols] += nn(probs.astype(bf16), cs[p])
                dk[there, cols] += nn(dscore, qs[p])
                for h in range(2):
                    part = slice(h * half, (h + 1) * half)
                    flip = beside(kt, base + j, count, slice(p * BLK + h * half, p * BLK + (h + 1) * half))
                    dqt[p, part, :] += nn(flip, dscore[:, h * BLK : (h + 1) * BLK])

        all_blocks(functools.partial(k_block, qkv, width, 0), bounds[i, 0], bounds[i, 1], own_blocks)
        all_blocks(functools.partial(k_block, kvh, 0, own_blocks), bounds[i, 2], bounds[i, 3], halo_blocks)
        for p in range(pairs):
            cols = slice(p * BLK, (p + 1) * BLK)
            grad = dqt[p].astype(bf16).T * jnp.asarray(0.125, bf16)
            dqkv[rows, cols] = grad
            sums[6:7, cols] += jnp.sum(grad.astype(f32), axis=0, keepdims=True)
        return carry

    lax.fori_loop(0, own_blocks, q_block, 0)
    for j in range(blocks):
        rows = slice(j * BLK, (j + 1) * BLK)
        grad_k = dk[rows, :].astype(bf16)
        grad_v = dv[rows, :].astype(bf16)
        if j < own_blocks:
            dqkv[rows, width : 2 * width] = grad_k
            dqkv[rows, 2 * width :] = grad_v
        else:
            back = slice((j - own_blocks) * BLK, (j - own_blocks + 1) * BLK)
            dkvh[back, :width] = grad_k
            dkvh[back, width:] = grad_v
        sums[7:8, :] += jnp.sum(grad_v.astype(f32), axis=0, keepdims=True)


def vmem_specs(count):
    return [pl.BlockSpec(memory_space=pltpu.VMEM)] * count


def any_specs(count):
    return [pl.BlockSpec(memory_space=pl.ANY)] * count


def ordered_call(kernel, args, waits, passes, out_shape, in_specs, out_specs, **options):
    waits, passes = tuple(waits) + tuple(turn.last), tuple(passes)
    given, made = len(args), len(out_shape)
    skipped = len(waits) + len(passes)

    def body(*refs):
        outs = given + skipped
        refs[outs + made][...] = jnp.zeros((8, BLK), f32)
        kernel(*refs[:given], *refs[outs : outs + made], *refs[outs + made + 1 + len(passes) :])

    out = pl.pallas_call(
        body,
        out_shape=tuple(out_shape)
        + (jax.ShapeDtypeStruct((8, BLK), f32),)
        + tuple(jax.ShapeDtypeStruct(p.shape, p.dtype) for p in passes),
        in_specs=list(in_specs) + any_specs(skipped),
        out_specs=tuple(out_specs) + (pl.BlockSpec((8, BLK), lambda *step: (0, 0)),) + tuple(any_specs(len(passes))),
        input_output_aliases={given + len(waits) + k: made + 1 + k for k in range(len(passes))},
        **options,
    )(*args, *waits, *passes)
    turn.last = [out[made]]
    return out[:made], out[made + 1 :]


class Turn:
    last = []


turn = Turn()


def attend(bounds, segq, segk, qkv, kvh, waits, passes):
    tokens, width3 = qkv.shape
    width = width3 // 3
    pairs, own_blocks, halo_blocks = width // BLK, tokens // BLK, kvh.shape[0] // BLK
    blocks = own_blocks + halo_blocks
    return ordered_call(
        functools.partial(attend_kernel, pairs, own_blocks, halo_blocks),
        (bounds, segq, segk, qkv, kvh),
        waits,
        passes,
        out_shape=(
            jax.ShapeDtypeStruct((tokens, width), bf16),
            jax.ShapeDtypeStruct((width, tokens), f32),
            jax.ShapeDtypeStruct((width, tokens), bf16),
            jax.ShapeDtypeStruct((own_blocks, 8, 2 * BLK), f32),
        ),
        in_specs=[pl.BlockSpec(memory_space=pltpu.SMEM)] + vmem_specs(4),
        out_specs=tuple(vmem_specs(4)),
        scratch_shapes=[
            pltpu.VMEM((blocks, width, BLK), bf16),
            pltpu.VMEM((pairs, 2 * BLK, BLK), bf16),
            pltpu.VMEM((8, 2 * BLK), f32),
            pltpu.VMEM((8, 2 * BLK), f32),
            pltpu.VMEM((pairs, BLK, BLK), f32),
        ],
        compiler_params=pltpu.CompilerParams(vmem_limit_bytes=13 * 2**20),
        cost_estimate=cost(9),
        name="attend",
    )


def attend_back(bounds, segq, segk, qkv, kvh, ctx_t, lse, dctx, norm_sums, up_sum, waits, passes):
    tokens, width3 = qkv.shape
    width = width3 // 3
    pairs, own_blocks, halo_blocks = width // BLK, tokens // BLK, kvh.shape[0] // BLK
    blocks = own_blocks + halo_blocks
    return ordered_call(
        functools.partial(attend_back_kernel, pairs, own_blocks, halo_blocks),
        (bounds, segq, segk, qkv, kvh, ctx_t, lse, dctx, norm_sums, up_sum),
        waits,
        passes,
        out_shape=(
            jax.ShapeDtypeStruct((tokens, width3), bf16),
            jax.ShapeDtypeStruct(kvh.shape, bf16),
            jax.ShapeDtypeStruct((16, width), f32),
        ),
        in_specs=[pl.BlockSpec(memory_space=pltpu.SMEM)] + vmem_specs(9),
        out_specs=tuple(vmem_specs(3)),
        scratch_shapes=[
            pltpu.VMEM((blocks, width, BLK), bf16),
            pltpu.VMEM((pairs, 2 * BLK, BLK), bf16),
            pltpu.VMEM((pairs, 2 * BLK, BLK), bf16),
            pltpu.VMEM((8, 2 * BLK), f32),
            pltpu.VMEM((pairs, BLK, BLK), f32),
            pltpu.VMEM((blocks * BLK, width), f32),
            pltpu.VMEM((blocks * BLK, width), f32),
        ],
        compiler_params=pltpu.CompilerParams(vmem_limit_bytes=20 * 2**20),
        cost_estimate=cost(21),
        name="attend_back",
    )


CHUNK = 1024
ROWS = 256


def normalized(rows):
    center = rows - jnp.mean(rows, axis=-1, keepdims=True)
    spread = jnp.mean(center * center, axis=-1, keepdims=True)
    scale = lax.rsqrt(spread + norm_eps)
    return center * scale, scale


def feed_kernel(last, tokens, hidden, ctx, w_out, vec, w_up, up_bias, w_down, *rest):
    if last:
        first_rows, first_t, active_t, slope, second_rows, low, low_rows, first, total = rest
    else:
        first_rows, first_t, active_t, slope, second_rows, low, after, low_t, low_rows, first, total = rest
    step = pl.program_id(0)
    tiles = [slice(at, at + BLK) for at in range(0, tokens, BLK)]
    passes = [slice(at, at + ROWS) for at in range(0, tokens, ROWS)]

    @pl.when(step == 0)
    def _():
        for rows in tiles:
            resid = hidden[rows, :].astype(f32) + (nn(ctx[rows, :], w_out[...]) + vec[0:1, :])
            first_rows[rows, :] = resid
            unit, _ = normalized(resid)
            value = unit * vec[1:2, :] + vec[2:3, :]
            first[rows, :] = value
            total[rows, :] = jnp.zeros_like(value)
            rounded = value.astype(bf16)
            low_rows[rows, :] = rounded
            first_t[:, rows] = rounded.T

    for rows in passes:
        upward = nn(low_rows[rows, :], w_up[...]) + up_bias[...]
        density = jnp.exp(-0.5 * upward * upward) * 0.3989422804014327
        below = 0.5 + 0.5 * lax.erf(upward * 0.7071067811865476)
        active = (upward * below).astype(bf16)
        slope[rows, :] = below + upward * density
        active_t[:, rows] = active.T
        total[rows, :] += nn(active, w_down[...])

    @pl.when(step == pl.num_programs(0) - 1)
    def _():
        for rows in tiles:
            resid = first[rows, :] + (total[rows, :] + vec[3:4, :])
            second_rows[rows, :] = resid
            unit, _ = normalized(resid)
            value = unit * vec[4:5, :] + vec[5:6, :]
            rounded = value.astype(bf16)
            low[rows, :] = rounded
            if not last:
                after[rows, :] = value
                low_t[:, rows] = rounded.T


def whole(shape):
    return pl.BlockSpec(shape, lambda step: (0,) * len(shape))


def feed(last, layer_idx, hidden, ctx, w_out, vec, w_up, up_bias, w_down, waits, passes):
    tokens, width = hidden.shape
    wide = w_up.shape[-1]
    rows = whole((tokens, width))
    shapes = [
        jax.ShapeDtypeStruct((tokens, width), f32),
        jax.ShapeDtypeStruct((width, tokens), bf16),
        jax.ShapeDtypeStruct((wide, tokens), bf16),
        jax.ShapeDtypeStruct((tokens, wide), f32),
        jax.ShapeDtypeStruct((tokens, width), f32),
        jax.ShapeDtypeStruct((tokens, width), bf16),
    ]
    specs = [
        rows,
        whole((width, tokens)),
        pl.BlockSpec((CHUNK, tokens), lambda step: (step, 0)),
        pl.BlockSpec((tokens, CHUNK), lambda step: (0, step)),
        rows,
        rows,
    ]
    if not last:
        shapes.append(jax.ShapeDtypeStruct((tokens, width), f32))
        shapes.append(jax.ShapeDtypeStruct((width, tokens), bf16))
        specs.append(rows)
        specs.append(whole((width, tokens)))
    return ordered_call(
        functools.partial(feed_kernel, last, tokens),
        (hidden, ctx, w_out, vec, w_up, up_bias, w_down),
        waits,
        passes,
        grid=(wide // CHUNK,),
        out_shape=tuple(shapes),
        in_specs=[
            rows,
            rows,
            pl.BlockSpec((None, width, width), lambda step: (layer_idx, 0, 0)),
            whole(vec.shape),
            pl.BlockSpec((None, width, CHUNK), lambda step: (layer_idx, 0, step)),
            pl.BlockSpec((1, CHUNK), lambda step: (0, step)),
            pl.BlockSpec((None, CHUNK, width), lambda step: (layer_idx, step, 0)),
        ],
        out_specs=tuple(specs),
        scratch_shapes=[
            pltpu.VMEM((tokens, width), bf16),
            pltpu.VMEM((tokens, width), f32),
            pltpu.VMEM((tokens, width), f32),
        ],
        compiler_params=pltpu.CompilerParams(vmem_limit_bytes=30 * 2**20),
        cost_estimate=cost(15),
        name="feed",
    )


def norm_back(grad, gain, rows):
    unit, scale = normalized(rows)
    lifted = grad * gain
    first = jnp.mean(lifted, axis=-1, keepdims=True)
    second = jnp.mean(lifted * unit, axis=-1, keepdims=True)
    return scale * (lifted - first - unit * second), unit


def over_rows(value):
    return jnp.sum(value, axis=0, keepdims=True)


def feed_back_kernel(
    tokens, grad, back, edge, second_rows, first_rows, slope, w_down, w_up, w_out, vec,
    dz, du, da, dr, dc, sums, up_sum, dr_two, total,
):
    step = pl.program_id(0)
    tiles = [slice(at, at + BLK) for at in range(0, tokens, BLK)]
    passes = [slice(at, at + ROWS) for at in range(0, tokens, ROWS)]

    @pl.when(step == 0)
    def _():
        sums[...] = jnp.zeros(sums.shape, f32)
        for rows in tiles:
            pull = grad[rows, :].astype(f32)
            if back.shape[0] > BLK:
                at = rows.start - edge[0]
                inside = (at >= 0) & (at < back.shape[0])
                here = pl.ds(pl.multiple_of(jnp.where(inside, at, 0), BLK), BLK)
                pull = pull + jnp.where(inside, back[here, :].astype(f32), 0.0)
            value, unit = norm_back(pull, vec[4:5, :], second_rows[rows, :])
            dr_two[rows, :] = value
            total[rows, :] = jnp.zeros_like(value)
            rounded = value.astype(bf16)
            dz[rows, :] = rounded
            sums[3:4, :] += over_rows(rounded.astype(f32))
            sums[4:5, :] += over_rows(pull * unit)
            sums[5:6, :] += over_rows(pull)

    up_sum[...] = jnp.zeros(up_sum.shape, f32)
    for rows in passes:
        pull = (nt(dz[rows, :], w_down[...]) * slope[rows, :]).astype(bf16)
        du[rows, :] = pull
        up_sum[...] += over_rows(pull.astype(f32))
        total[rows, :] += nt(pull, w_up[...])

    @pl.when(step == pl.num_programs(0) - 1)
    def _():
        for rows in tiles:
            pull = total[rows, :] + dr_two[rows, :]
            value, unit = norm_back(pull, vec[1:2, :], first_rows[rows, :])
            dr[rows, :] = value
            rounded = value.astype(bf16)
            da[rows, :] = rounded
            sums[0:1, :] += over_rows(rounded.astype(f32))
            sums[1:2, :] += over_rows(pull * unit)
            sums[2:3, :] += over_rows(pull)
            dc[rows, :] = nt(rounded, w_out[...]).astype(bf16)


def feed_back(layer_idx, grad, back, edge, second_rows, first_rows, slope, w_down, w_up, w_out, vec, waits, passes):
    tokens, width = grad.shape
    wide = w_up.shape[-1]
    rows = whole((tokens, width))
    return ordered_call(
        functools.partial(feed_back_kernel, tokens),
        (grad, back, edge, second_rows, first_rows, slope, w_down, w_up, w_out, vec),
        waits,
        passes,
        grid=(wide // CHUNK,),
        out_shape=(
            jax.ShapeDtypeStruct((tokens, width), bf16),
            jax.ShapeDtypeStruct((tokens, wide), bf16),
            jax.ShapeDtypeStruct((tokens, width), bf16),
            jax.ShapeDtypeStruct((tokens, width), f32),
            jax.ShapeDtypeStruct((tokens, width), bf16),
            jax.ShapeDtypeStruct((8, width), f32),
            jax.ShapeDtypeStruct((1, wide), f32),
        ),
        in_specs=[
            rows,
            whole(back.shape),
            pl.BlockSpec(memory_space=pltpu.SMEM),
            rows,
            rows,
            pl.BlockSpec((tokens, CHUNK), lambda step: (0, step)),
            pl.BlockSpec((None, CHUNK, width), lambda step: (layer_idx, step, 0)),
            pl.BlockSpec((None, width, CHUNK), lambda step: (layer_idx, 0, step)),
            pl.BlockSpec((None, width, width), lambda step: (layer_idx, 0, 0)),
            whole(vec.shape),
        ],
        out_specs=(
            rows,
            pl.BlockSpec((tokens, CHUNK), lambda step: (0, step)),
            rows,
            rows,
            rows,
            whole((8, width)),
            pl.BlockSpec((1, CHUNK), lambda step: (0, step)),
        ),
        scratch_shapes=[pltpu.VMEM((tokens, width), f32), pltpu.VMEM((tokens, width), f32)],
        compiler_params=pltpu.CompilerParams(vmem_limit_bytes=30 * 2**20),
        cost_estimate=cost(17),
        name="feed_back",
    )


def grad_down_kernel(core, active_t, dz, send, keep):
    groups, head, parts, thin, width = send.shape
    mine = core[0]
    for which, out in ((1 - mine, send), (mine, keep)):
        for group in range(groups):
            value = nn(active_t[2 * group + which], dz[...])
            for shard in range(head):
                for at in range(parts):
                    here = (shard * parts + at) * thin
                    out[group, shard, at] = value[here : here + thin].astype(bf16)


def grad_up_kernel(core, first_t, du, send, keep, lhs):
    groups, head, parts, thin, width = send.shape
    rows = head * thin
    mine = core[0]
    for which, out in ((1 - mine, send), (mine, keep)):
        if rows % 16 == 0:
            for group in range(groups):
                lhs[group * rows : (group + 1) * rows, :] = first_t[2 * group + which]
        for at in range(parts):
            pulls = du[:, at * width : (at + 1) * width]
            if rows % 16 == 0:
                value = nn(lhs[...], pulls)
                values = [value[group * rows : (group + 1) * rows] for group in range(groups)]
            else:
                values = [nn(first_t[2 * group + which], pulls) for group in range(groups)]
            for group in range(groups):
                for shard in range(head):
                    out[group, shard, at] = values[group][shard * thin : (shard + 1) * thin].astype(bf16)


def grad_feed(core, left_t, right, parts, devices, head, scratch):
    rows, tokens = left_t.shape
    thin = rows // devices // head // (1 if scratch else parts)
    width = right.shape[1] // (parts if scratch else 1)
    out = jax.ShapeDtypeStruct((devices // 2, head, parts, thin, width), bf16)
    halves, _ = ordered_call(
        grad_up_kernel if scratch else grad_down_kernel,
        (core, left_t.reshape(devices, rows // devices, tokens), right),
        (),
        (),
        out_shape=(out, out),
        in_specs=[pl.BlockSpec(memory_space=pltpu.SMEM)] + vmem_specs(2),
        out_specs=tuple(vmem_specs(2)),
        scratch_shapes=[pltpu.VMEM((rows // 2, tokens), bf16)] if scratch else [],
        compiler_params=pltpu.CompilerParams(vmem_limit_bytes=15 * 2**20),
        cost_estimate=cost(5),
        name="grad_up" if scratch else "grad_down",
    )
    return halves


def grad_heads_kernel(core, ctx_t, low_t, halo_t, da, dqkv, dkvh, sums, send, keep, one, two, three):
    groups, thin = ctx_t.shape[0] // 2, ctx_t.shape[1]
    width = send.shape[2] // 4
    high = thin // TILE
    for r in range(sums.shape[0] // TILE):
        value = sums[r * TILE : (r + 1) * TILE, :].astype(bf16)
        for out in (send, keep):
            out[groups * high, :, r * width : (r + 1) * width] = value
    mine = core[0]
    for which, out in ((1 - mine, send), (mine, keep)):
        if thin % 16 == 0:
            for group in range(groups):
                here = slice(group * thin, (group + 1) * thin)
                one[here, :] = ctx_t[2 * group + which]
                two[here, :] = low_t[2 * group + which]
                three[here, :] = halo_t[2 * group + which]
            parts = [(range(groups), one, two, three)]
        else:
            parts = [
                ([group], ctx_t.at[2 * group + which], low_t.at[2 * group + which], halo_t.at[2 * group + which])
                for group in range(groups)
            ]
        for members, left_one, left_two, left_three in parts:
            for at in range(0, 4 * width, width):
                if at < width:
                    value = nn(left_one[...], da[...])
                else:
                    value = nn(left_two[...], dqkv[:, at - width : at])
                    if at >= 2 * width:
                        value = value + nn(left_three[...], dkvh[:, at - 2 * width : at - width])
                for place, group in enumerate(members):
                    here = value[place * thin : (place + 1) * thin].reshape(high, TILE, width)
                    out[group * high : (group + 1) * high, :, at : at + width] = here.astype(bf16)


def grad_heads(core, ctx_t, low_t, halo_t, da, dqkv, dkvh, sums, devices, waits, passes):
    tokens, width = da.shape
    thin = width // devices
    out = jax.ShapeDtypeStruct((devices // 2 * thin // TILE + 1, TILE, 4 * width), bf16)
    extent = halo_t.shape[1]
    return ordered_call(
        grad_heads_kernel,
        (
            core,
            ctx_t.reshape(devices, thin, tokens),
            low_t.reshape(devices, thin, tokens),
            halo_t.reshape(devices, thin, extent),
            da,
            dqkv,
            dkvh,
            sums,
        ),
        waits,
        passes,
        out_shape=(out, out),
        in_specs=[pl.BlockSpec(memory_space=pltpu.SMEM)] + vmem_specs(7),
        out_specs=tuple(vmem_specs(2)),
        scratch_shapes=[
            pltpu.VMEM((width // 2, tokens), bf16),
            pltpu.VMEM((width // 2, tokens), bf16),
            pltpu.VMEM((width // 2, extent), bf16),
        ],
        compiler_params=pltpu.CompilerParams(vmem_limit_bytes=20 * 2**20),
        cost_estimate=cost(8),
        name="grad_heads",
    )


def assemble_kernel(relative, place, own, *refs):
    *refs, out = refs
    shard, group = place[0], place[1]
    kinds = own.shape[0]
    out[:, pl.ds(shard, 1)] = own[...].reshape(kinds, 1, *own.shape[1:])
    lane = 0
    for ref, order in zip(refs, relative):
        lanes = slice(lane, lane + ref.shape[-1])
        lane = lanes.stop % own.shape[-1]
        for at, change in enumerate(order):
            for step in range(ref.shape[1]):
                for kind in range(kinds):
                    out[kind, shard ^ (step + 1), group ^ change, :, lanes] = ref[at, step, kind]


def assemble(relative, place, own, refs, passes):
    head = lax.axis_size("head")
    (out,), passed = ordered_call(
        functools.partial(assemble_kernel, relative),
        (place, own, *refs),
        (),
        passes,
        out_shape=(jax.ShapeDtypeStruct((own.shape[0], head) + own.shape[1:], bf16),),
        in_specs=[pl.BlockSpec(memory_space=pltpu.SMEM)] + vmem_specs(1 + len(refs)),
        out_specs=vmem_specs(1),
        compiler_params=pltpu.CompilerParams(vmem_limit_bytes=13 * 2**20),
        cost_estimate=cost(1.5),
        name="assemble",
    )
    return out, passed


def grow(value, order):
    value, relative = value[None], [0]
    for place in order:
        value = jnp.concatenate([value, swap(value, "dp", 1 << place)], axis=0)
        relative = relative + [other ^ (1 << place) for other in relative]
    return value, relative


def flip_kernel(count, shard, biases, *refs):
    for source, target in zip(refs[:count], refs[count : 2 * count]):
        for at in range(0, source.shape[0], BLK):
            target[:, at : at + BLK] = source[at : at + BLK, :].T
    shifts = refs[2 * count]
    members, _, width = biases.shape
    layers, part = shifts.shape[0], width // members
    shifts[...] = jnp.zeros(shifts.shape, f32)
    rows = [biases[step].astype(f32) for step in range(members)]
    for member in range(members):
        value = jnp.zeros((1, width), f32)
        for step, row in enumerate(rows):
            value = jnp.where((shard[0] ^ step) == member, row, value)
        for layer_idx in range(layers):
            for at, kind in ((0, 0), (1, 2)):
                here = (2 * layer_idx + at) * part
                there = kind * width + member * part
                shifts[layer_idx, :, there : there + part] = value[:, here : here + part]


def flip(values, shard, biases, layers):
    width = biases.shape[2]
    shapes = [jax.ShapeDtypeStruct(v.shape[::-1], v.dtype) for v in values]
    return ordered_call(
        functools.partial(flip_kernel, len(values)),
        (shard, biases, *values),
        (),
        (),
        out_shape=shapes + [jax.ShapeDtypeStruct((layers, 1, 3 * width), f32)],
        in_specs=[pl.BlockSpec(memory_space=pltpu.SMEM)] + vmem_specs(1 + len(values)),
        out_specs=vmem_specs(1 + len(values)),
        compiler_params=pltpu.CompilerParams(vmem_limit_bytes=8 * 2**20),
        cost_estimate=cost(1.5),
        name="flip",
    )


def collect_kernel(*refs):
    *parts, out = refs
    for k, ref in enumerate(parts):
        out[k] = ref[...]


def collect(values):
    (out,), _ = ordered_call(
        collect_kernel,
        values,
        (),
        (),
        out_shape=(jax.ShapeDtypeStruct((len(values),) + values[0].shape, values[0].dtype),),
        in_specs=vmem_specs(len(values)),
        out_specs=vmem_specs(1),
        compiler_params=pltpu.CompilerParams(vmem_limit_bytes=8 * 2**20),
        cost_estimate=cost(1.4),
        name="collect",
    )
    return out


def from_heads_in_turn(piece):
    got = [swap(piece, "head", 1)]
    step = 2
    while step < lax.axis_size("head"):
        far = [swap(value, "head", step) for value in [piece]]
        for value in far:
            got = got + [value, swap(value, "head", 1)]
        step *= 2
    return got


def from_heads(piece):
    return [swap(piece, "head", step) for step in range(1, lax.axis_size("head"))]


def added(keep, got):
    return keep.astype(f32) + got.astype(f32)


def advance_kernel(counts, size, tail, sources, scalars, *refs):
    core, mine = scalars[0], scalars[1]
    keeps, gots, (send, out) = refs[:sources], refs[sources : 2 * sources], refs[2 * sources :]
    blocks = (keeps[0].shape[0] - tail) // size
    for target, which in ((send, 1 - mine), (out, mine)):
        for k in range(blocks // 2):
            spots = [2 * (k // after) * after + k % after for after in counts]
            at = jnp.where(core == 0, spots[0] + which * counts[0], spots[1] + which * counts[1])
            here = pl.ds(at * size, size)
            for source, (keep, got) in enumerate(zip(keeps, gots)):
                value = added(keep[here], got[here]).astype(bf16)
                if sources > 1:
                    target[k * size : (k + 1) * size, source] = value
                else:
                    target[k * size : (k + 1) * size] = value
        if tail:
            value = added(keeps[0][blocks * size :], gots[0][blocks * size :]).astype(bf16)
            target[blocks // 2 * size :] = value


def turn_heads_kernel(head, scalars, keep, got, send, out):
    mine = scalars[1]
    tiles, _, columns = keep.shape
    rows, width = (tiles - 1) * TILE, columns // 4
    held = added(keep[: tiles - 1], got[: tiles - 1]).reshape(rows, columns)
    part, thin = width // head, rows // head
    kinds = []
    if rows < BLK:
        filler = jnp.zeros((BLK - rows, width), f32)
    for kind in range(1, 4):
        value = held[:, kind * width : (kind + 1) * width]
        value = jnp.concatenate([value, filler], axis=0) if rows < BLK else value
        kinds.append(value.T)
    high = part // (width // BLK)
    count = part // TILE
    for shard in range(head):
        pieces = [value[shard * part : (shard + 1) * part] for value in kinds]
        own = held[shard * thin : (shard + 1) * thin, :width]
        own = jnp.concatenate([own, jnp.zeros((high - thin, width), f32)], axis=0)
        pieces.append(jnp.concatenate([own[:, at : at + BLK] for at in range(0, width, BLK)], axis=0))
        for chosen, target in ((1 - mine, send), (mine, out)):

            @pl.when(chosen == shard % 2)
            def _(target=target, pieces=pieces, shard=shard):
                for kind, piece in enumerate(pieces):
                    at = (shard // 2 * 4 + kind) * count
                    target[at : at + count] = piece.reshape(count, TILE, BLK).astype(bf16)

    last = added(keep[tiles - 1], got[tiles - 1])
    for target in (send, out):
        for k in range(2 * width // BLK):
            target[head // 2 * 4 * count + k] = last[:, k * BLK : (k + 1) * BLK].astype(bf16)


class Flight:
    def __init__(self, keeps, gots, turned):
        dp, head = lax.axis_size("dp"), lax.axis_size("head")
        bits = dp.bit_length() - 1
        upper = list(range(1, bits))
        self.orders = [list(upper), list(upper)[::-1]]
        self.left = [upper[::-1], upper[::-1]]
        self.head_bits = list(range(head.bit_length() - 1))
        self.turned = turned
        self.tail, self.size = 0, 1
        if turned:
            self.tail, self.size = 1, (keeps[0].shape[0] - 1) // (dp // 2)
        else:
            shape = (keeps[0].shape[0] * keeps[0].shape[1],) + keeps[0].shape[2:]
            keeps, gots = [k.reshape(shape) for k in keeps], [g.reshape(shape) for g in gots]
        self.keeps, self.gots = list(keeps), list(gots)

    def step(self, waits=(), passes=()):
        blocks = (self.keeps[0].shape[0] - self.tail) // self.size
        sources = len(self.keeps)
        core = bit_of("dp", 0)
        rest = self.keeps[0].shape[1:]
        if sources > 1:
            rest = (sources,) + rest
        devices = lax.axis_size("dp")
        counts = [1, 1]
        if self.orders[0]:
            places = [order.pop(0) for order in self.orders]
            counts = []
            for left, place in zip(self.left, places):
                axis = left.index(place)
                left.remove(place)
                counts.append((blocks // 2) >> axis)
            mine = jnp.where(core == 0, bit_of("dp", places[0]), bit_of("dp", places[1]))
            axis_name, pairs = "dp", [(i, i ^ (1 << places[i & 1])) for i in range(devices)]
        else:
            place = self.head_bits.pop(0)
            mine = bit_of("head", place)
            head = lax.axis_size("head")
            axis_name, pairs = "head", [(i, i ^ (1 << place)) for i in range(head)]
        if axis_name == "head" and self.turned:
            width = rest[1] // 4
            self.turned = False
            self.size, self.tail = 4 * (width // head) // TILE, 2 * width // BLK
            out_shape = (head // 2 * self.size + self.tail, TILE, BLK)
            kernel = functools.partial(turn_heads_kernel, head)
        else:
            out_shape = (blocks // 2 * self.size + self.tail,) + rest
            kernel = functools.partial(advance_kernel, counts, self.size, self.tail, sources)
        out = jax.ShapeDtypeStruct(out_shape, bf16)
        (send, keep), passed = ordered_call(
            kernel,
            (jnp.stack([core, mine]).astype(jnp.int32), *self.keeps, *self.gots),
            waits,
            passes,
            out_shape=[out] * 2,
            in_specs=[pl.BlockSpec(memory_space=pltpu.SMEM)] + vmem_specs(2 * sources),
            out_specs=vmem_specs(2),
            compiler_params=pltpu.CompilerParams(vmem_limit_bytes=20 * 2**20),
            cost_estimate=cost(1 + 2e-6 * out.size),
            name="advance",
        )
        self.keeps, self.gots = [keep], [lax.ppermute(send, axis_name, pairs)]
        return passed

    def finish(self):
        while self.orders[0] or self.head_bits:
            self.step()
        total = added(self.keeps[0], self.gots[0])
        return total if self.tail else total[0]


def per_device(
    tokens_in,
    segment,
    w_qkv,
    qv_bias,
    w_out,
    out_bias,
    ln1_gain,
    ln1_bias,
    w_up,
    up_bias,
    w_down,
    down_bias,
    ln2_gain,
    ln2_bias,
    cotangent,
):
    turn.last = []
    layers, width = w_qkv.shape[0], w_qkv.shape[1]
    part = w_qkv.shape[3] * w_qkv.shape[4]
    head_size = w_qkv.shape[4]
    tokens = tokens_in.shape[0]
    seq = segment.shape[1]
    dp, head = lax.axis_size("dp"), lax.axis_size("head")
    bits = dp.bit_length() - 1
    shard, group = lax.axis_index("head"), lax.axis_index("dp")
    halves = seq // tokens
    row, half = shard // halves, shard % halves
    upper = list(range(1, bits))

    edge = jnp.where(half == 0, tokens - HALO, 0)
    core = bit_of("dp", 0)

    own_w = w_qkv.transpose(0, 2, 3, 4, 1).reshape(layers, 3, part, width)
    own_first = own_w[0].reshape(3, dp, part // dp, width)
    piece = pick(own_first, group, 1).reshape(-1, width)
    rows_w = piece.shape[0]
    bias_own = qv_bias.reshape(1, layers * 2 * part)
    bias_own = jnp.pad(bias_own, ((0, 7), (0, width - bias_own.shape[1])))
    piece = jnp.concatenate([piece, bias_own])
    got = from_heads(piece)
    halo = swap(lax.dynamic_slice_in_dim(tokens_in, edge, HALO), "head", 1)
    biases = jnp.stack([other[rows_w : rows_w + 1] for other in [piece] + got])
    got = jnp.stack([other[:rows_w] for other in got]).reshape(head - 1, 3, part // dp, width)
    left, relative_left = grow(got[..., : width // 2], upper)
    right, relative_right = grow(got[..., width // 2 :], upper[::-1])
    both = jnp.stack([left, right])
    both = jnp.concatenate([both, swap(both, "dp", 1)], axis=1)
    relative = [order + [other ^ 1 for other in order] for order in (relative_left, relative_right)]
    place = jnp.stack([shard, group]).astype(jnp.int32)
    own_later = [own_w[k].reshape(3, 2, part // 2, width) for k in range(1, layers)]
    (low_t, halo_t, shifts), _ = flip([tokens_in, halo], shard.reshape(1).astype(jnp.int32), biases, layers)
    w_first, pieces = assemble(relative, place, own_first, [both[0], both[1]], [pick(own, core, 1) for own in own_later])
    later_got = [from_heads_in_turn(value) for value in pieces]
    w_cats = [w_first.reshape(3 * head * part, width)]

    def later_weights(own, got):
        theirs = swap(got, "dp", 1)
        whole = assemble([[0], [1]], jnp.stack([shard, core]).astype(jnp.int32), own, [got[None], theirs[None]], [])[0]
        return whole.reshape(3 * head * part, width)

    labels = pick(segment, row, 0)
    own_labels = lax.dynamic_slice_in_dim(labels, half * tokens, tokens)
    halo_start = jnp.where(half == 0, tokens, tokens - HALO)
    halo_labels = lax.dynamic_slice_in_dim(labels, halo_start, HALO)
    blocks = tokens // BLK
    by_block = own_labels.reshape(blocks, BLK)
    least, most = by_block[:, :1], by_block[:, -1:]

    def count(flags):
        return jnp.sum(flags.astype(jnp.int32), axis=1)

    bounds = jnp.stack(
        [
            count(own_labels[None] < least) // BLK,
            (count(own_labels[None] <= most) + BLK - 1) // BLK,
            count(halo_labels[None] < least) // BLK,
            (count(halo_labels[None] <= most) + BLK - 1) // BLK,
        ],
        axis=1,
    )
    segq = jnp.concatenate([by_block, by_block], axis=1).reshape(blocks, 1, 2 * BLK)
    segk = jnp.concatenate([own_labels, halo_labels]).reshape(-1, 1)
    core_at = core.reshape(1).astype(jnp.int32)

    vecs = jnp.stack(
        [out_bias, ln1_gain, ln1_bias, down_bias, ln2_gain, ln2_bias, out_bias, out_bias], axis=1
    ).astype(f32)
    up_bias_wide = up_bias.astype(f32)

    hidden, low = tokens_in, tokens_in
    saved = []
    for layer_idx in range(layers):
        last = layer_idx == layers - 1
        w_cat = w_cats[layer_idx]
        shift = shifts[layer_idx]
        factor = jnp.where(jnp.arange(3 * width) < width, 0.125, 1.0).astype(f32)
        qkv = ((nt(low, w_cat) + shift) * factor).astype(bf16)
        kvh = (nt(halo, w_cat[width:]) + shift[:, width:]).astype(bf16)
        (ctx, ctx_t, ctx_low, lse), _ = attend(bounds, segq, segk, qkv, kvh, (), ())
        fed, _ = feed(
            last, layer_idx, hidden, ctx, w_out, vecs[layer_idx], w_up, up_bias_wide[layer_idx : layer_idx + 1], w_down, (), ()
        )
        first_rows, first_t, active_t, slope, second_rows, after_low = fed[:6]
        saved.append((low_t, halo_t, qkv, kvh, ctx_t, ctx_low, lse, first_rows, first_t, active_t, slope, second_rows))
        if last:
            output = after_low
        else:
            low, hidden, low_t = after_low, fed[6], fed[7]
            halo = swap(lax.dynamic_slice_in_dim(low, edge, HALO), "head", 1)
            halo_t = halo.T
            w_cats.append(later_weights(own_later[layer_idx], collect(later_got[layer_idx])))

    grad_hidden, back = cotangent, jnp.zeros((BLK, width), bf16)
    flights = []
    for layer_idx in reversed(range(layers)):
        low_t, halo_t, qkv, kvh, ctx_t, ctx_low, lse, first_rows, first_t, active_t, slope, second_rows = saved[layer_idx]
        w_cat = w_cats[layer_idx]
        (dz, du, da, dr, dc, sums, up_sum), _ = feed_back(
            layer_idx, grad_hidden, back, edge.reshape(1).astype(jnp.int32), second_rows, first_rows, slope, w_down, w_up, w_out, vecs[layer_idx], (), ()
        )
        if flights:
            flights[1].step()
            flights[0].step()
        parts = du.shape[1] // width
        down_send, down_keep = grad_feed(core_at, active_t, dz, parts, dp, head, False)
        down_got = swap(down_send, "dp", 1)
        up_send, up_keep = grad_feed(core_at, first_t, du, parts, dp, head, True)
        up_got = swap(up_send, "dp", 1)
        fed = Flight([down_keep, up_keep], [down_got, up_got], False)
        fed.step()
        (dqkv, dkvh, sums), _ = attend_back(bounds, segq, segk, qkv, kvh, ctx_t, lse, dc, sums, up_sum, (), ())
        part_halo = nn(dkvh, w_cat[width:]).astype(bf16)
        back = swap(part_halo, "head", 1)
        if flights:
            flights[1].step()
            flights[0].step()
        (send, keep), _ = grad_heads(core_at, ctx_low, low_t, halo_t, da, dqkv, dkvh, sums, dp, (part_halo,), ())
        heads = Flight([keep], [swap(send, "dp", 1)], True)
        grad_hidden = nn(dqkv, w_cat) + dr
        fed.step()
        if flights:
            flights[1].step()
            heads.step()
            fed.step()
            heads.step()
            fed.step()
            heads.step()
            flights[1].step()
            first, second = flights
            passed = heads.step(passes=(first.keeps[0], second.keeps[0]))
            first.keeps, second.keeps = [passed[0]], [passed[1]]
        flights = flights + [fed, heads]

    padded = lax.dynamic_update_slice(jnp.zeros((tokens, width), bf16), back, (edge, 0))
    grad_hidden = grad_hidden + padded.astype(f32)

    results = []
    for place in range(layers):
        fed, heads = flights[2 * place], flights[2 * place + 1]
        thin = width // (dp * head)
        total = fed.finish()
        out_down = total[0].reshape(-1, width)
        out_up = total[1].transpose(1, 0, 2).reshape(thin, -1)
        total = heads.finish()
        pieces = total[: 4 * part // TILE].reshape(4, part, BLK)
        out_out = pieces[3].reshape(width // BLK, -1, BLK)[:, :thin].transpose(1, 0, 2).reshape(thin, width)
        sums = total[4 * part // TILE :].transpose(1, 0, 2).reshape(TILE, 2, width).transpose(1, 0, 2)
        results.append((pieces[:3, :, : width // dp], out_out, out_up, out_down, sums.reshape(2 * TILE, width)))
    results = results[::-1]
    out_qkv, out_w_out, out_up, out_down, total = (jnp.stack([r[k] for r in results]) for k in range(5))
    out_qkv = out_qkv.reshape(layers, 3, part // head_size, head_size, -1).transpose(0, 4, 1, 2, 3)

    device = group * head + shard
    thin = width // (dp * head)
    mine = lax.dynamic_slice_in_dim(total[:, :6], device * thin, thin, axis=2)
    ups = total[:, 8 : 8 + up_bias.shape[1] // width].reshape(layers, -1)
    thick = ups.shape[1] // (dp * head)
    out_ups = lax.dynamic_slice_in_dim(ups, device * thick, thick, axis=1)
    qvs = total[:, 6:8].reshape(layers, 2, head, part // head_size, dp, head_size // dp)
    out_qv = pick(pick(qvs, shard, 2), group, 3)
    return (
        output,
        grad_hidden,
        out_qkv,
        out_qv,
        out_w_out,
        mine[:, 0],
        mine[:, 1],
        mine[:, 2],
        out_up,
        out_ups,
        out_down,
        mine[:, 3],
        mine[:, 4],
        mine[:, 5],
    )


def solution(mesh):
    return jax.shard_map(
        per_device,
        mesh=mesh,
        in_specs=(
            P(("dp", "head"), None),
            P("dp", None),
            P(None, None, None, "head", None),
            P(None, None, "head", None),
            P(),
            P(),
            P(),
            P(),
            P(),
            P(),
            P(),
            P(),
            P(),
            P(),
            P(("dp", "head"), None),
        ),
        out_specs=(
            P(("dp", "head"), None),
            P(("dp", "head"), None),
            P(None, "dp", None, "head", None),
            P(None, None, "head", "dp"),
            P(None, ("dp", "head"), None),
            P(None, ("dp", "head")),
            P(None, ("dp", "head")),
            P(None, ("dp", "head")),
            P(None, ("dp", "head"), None),
            P(None, ("dp", "head")),
            P(None, ("dp", "head"), None),
            P(None, ("dp", "head")),
            P(None, ("dp", "head")),
            P(None, ("dp", "head")),
        ),
        check_vma=False,
    )
```
